32 devices in a mesh: subj: 8 (over z, y), vox: 4 (over x, core).
Axes of the slice: x: 2, y: 2, z: 4, core: 2. Of those that a mesh axis runs over, the one named last changes fastest.
Arguments:
- scans: bfloat16 [5120, 49152], P('subj', 'vox'), may hold values from -6 to 6
- test_matrix: bfloat16 [49152, 128], P('vox'), may hold values from -6 to 6
- lengths: int32 [8], replicated, may hold values from 160 to 640, as said below
- block_subject: int32 [8], replicated, may hold values from 0 to 7, each once
Outputs:
- basis: float32 [49152, 128], P('vox')
The draws below stay inside these ranges and needn't reach their ends.
Inputs may be any that keep to these rules, and one draw needn't show every extreme that they name: `lengths`: one subject has exactly 640 rows and one exactly 160. `block_subject`: each subject appears once.
All inputs are finite; a program needn't handle non-finite values.
Results may differ from the reference program's by a relative error of at most 0.0046.
Values may be sent and summed in bfloat16 or wider, within the bound.
No kernel may reach another device: no remote copies, remote signals or barrier semaphores. Data moves between devices by JAX's collectives and lax.ppermute only.
A program may use at most 128 MiB of HBM per device.

```python
import jax
import jax.numpy as jnp
from jax import lax

V = 49152
R = 128
TPAD = 640
PASSES = 2
SUBJECTS = 8


def draw_lengths(key, part):
    first_key, second_key = jax.random.split(jax.random.fold_in(key, 17))
    values = jax.random.randint(first_key, (SUBJECTS,), TPAD // 4, TPAD + 1)
    order_ids = jax.random.permutation(second_key, SUBJECTS)
    values = values.at[order_ids[0]].set(TPAD)
    values = values.at[order_ids[1]].set(TPAD // 4)
    return values.astype(jnp.int32)


def draw_scans(key, part):
    keys = jax.random.split(jax.random.fold_in(key, 29), 5)
    row_total = SUBJECTS * TPAD
    first_time = jax.random.truncated_normal(keys[1], -3.0, 3.0, (row_total, 1), jnp.float32)
    second_time = jax.random.truncated_normal(keys[2], -3.0, 3.0, (row_total, 1), jnp.float32)
    first_space = jax.random.rademacher(keys[3], (1, V), dtype=jnp.float32)
    second_space = jax.random.rademacher(keys[4], (1, V), dtype=jnp.float32)
    half_mask = (jnp.arange(V, dtype=jnp.int32) >= V // 2).astype(jnp.float32)[None, :]
    noise = jax.random.truncated_normal(keys[0], -4.0, 4.0, (row_total, V), jnp.float32)
    first_amp = 0.2
    second_amp = 0.25
    values = noise + first_amp * first_time * first_space + second_amp * second_time * second_space * half_mask
    return values.astype(jnp.bfloat16)


def block_levels(own_key, shape, cuts, smallest, top_value):
    loudness = 1.0
    for position, blocks in cuts:
        steps = jax.random.uniform(jax.random.fold_in(jax.random.fold_in(own_key, 6), position), (blocks,), jnp.float32, smallest / len(cuts), top_value / len(cuts))
        loudness = loudness * jnp.repeat(jnp.exp(steps), shape[position] // blocks).reshape((-1,) + (1,) * (len(shape) - 1 - position))
    return loudness


def normal_values(stream_key, shape, spread, reach, cuts=(), held_as=jnp.bfloat16):
    result = spread * jax.random.normal(stream_key, shape, jnp.float32)
    if cuts:
        result = result * block_levels(stream_key, shape, cuts, -0.22, 0.18)
    return jnp.clip(result, -reach, reach).astype(held_as)


def setup_inputs(seed: int = 0) -> dict:
    streams_of = jax.random.split(jax.random.key(seed), 5)
    return {
        "scans": draw_scans(jax.random.fold_in(streams_of[4], 71), 0),
        "test_matrix": normal_values(streams_of[1], (V, R), 1.0, 6.0, ((0, 4),)),
        "lengths": draw_lengths(jax.random.fold_in(streams_of[4], 71), 0),
        "block_subject": jax.random.permutation(streams_of[3], SUBJECTS).astype(jnp.int32),
    }


def reference(scans, test_matrix, lengths, block_subject):
    blocks = scans.reshape(SUBJECTS, TPAD, V)
    live_len = lengths[block_subject].astype(jnp.int32)
    time_ids = jnp.arange(TPAD, dtype=jnp.int32)
    panel_now = test_matrix
    orthonormal = jnp.zeros((V, R), jnp.float32)
    for sweep_index in range(PASSES):

        def add_subject(running, inputs):
            data_block, length = inputs
            scores = jnp.dot(data_block.astype(jnp.float32), panel_now.astype(jnp.float32), preferred_element_type=jnp.float32)
            scores = jnp.where((time_ids < length)[:, None], scores, jnp.float32(0.0)).astype(jnp.bfloat16)
            update = lax.dot_general(data_block.astype(jnp.float32), scores.astype(jnp.float32), (((0,), (0,)), ((), ())), preferred_element_type=jnp.float32)
            return (running + update, None)
        sketch, unused = lax.scan(add_subject, jnp.zeros((V, R), jnp.float32), (blocks, live_len))
        gram_matrix = jnp.dot(sketch.T, sketch, precision=lax.Precision.HIGHEST) / V
        factor = jnp.linalg.cholesky(gram_matrix)
        orthonormal = jax.scipy.linalg.solve_triangular(factor, sketch.T, lower=True).T
        panel_now = orthonormal.astype(jnp.bfloat16)
    return orthonormal
```

```python
import jax
import jax.numpy as jnp
from jax import lax
from jax.sharding import PartitionSpec as P

F32 = jnp.float32
BF16 = jnp.bfloat16
I16 = jnp.int16
HIGHEST = lax.Precision.HIGHEST
SCALE_ROWS = 16
STEPS = 64.0


def exchange(value, axis, size, mask):
    return lax.ppermute(value, axis, [(i, i ^ mask) for i in range(size)])


def butterfly(value, axis, size):
    mask = 1
    while mask < size:
        value = value + exchange(value, axis, size, mask)
        mask *= 2
    return value


class Plain:
    pad = 0

    @staticmethod
    def encode(value):
        return value.astype(BF16)

    @staticmethod
    def decode(sent):
        return sent.astype(F32)


class Fixed:
    pad = SCALE_ROWS

    @staticmethod
    def encode(value):
        top = jnp.maximum(jnp.max(jnp.abs(value), axis=0, keepdims=True), 1e-30)
        power = jnp.ceil(jnp.log2(top * (1.0 / 32000.0)) * STEPS)
        codes = jnp.round(value * jnp.exp2(power * (-1.0 / STEPS)))
        codes = jnp.clip(codes, -32767.0, 32767.0)
        rows = jnp.broadcast_to(power, (SCALE_ROWS, value.shape[1]))
        return jnp.concatenate([codes, rows]).astype(jnp.int32).astype(I16)

    @staticmethod
    def decode(sent):
        wide = sent.astype(jnp.int32).astype(F32)
        power = wide[-SCALE_ROWS : -SCALE_ROWS + 1]
        return wide[:-SCALE_ROWS] * jnp.exp2(power * (1.0 / STEPS))


def pick(pieces, index):
    return lax.dynamic_index_in_dim(pieces, index, 0, keepdims=False)


def reduce_scatter(first, second, code, axis, size, low, high):
    me = lax.axis_index(axis)
    mine_low, mine_high = me % low, me // low
    n, cols = first.shape[2], first.shape[3]
    m = second.shape[2]
    sent = code.encode(pick(first, 1 - mine_low).reshape(high * n, cols))
    got_first = exchange(sent, axis, size, 1)
    got_second = []
    for k in range(1, high):
        sent = code.encode(pick(second, mine_high ^ k).reshape(low * m, cols))
        got_second.append(exchange(sent, axis, size, k * low))
    first = pick(first, mine_low) + code.decode(got_first).reshape(high, n, cols)
    got = []
    for k in range(1, high):
        got.append(exchange(code.encode(pick(first, mine_high ^ k)), axis, size, k * low))
    second = pick(second, mine_high).reshape(low * m, cols)
    for part in got_second:
        second = second + code.decode(part)
    second = second.reshape(low, m, cols)
    got_low = exchange(code.encode(pick(second, 1 - mine_low)), axis, size, 1)
    first = pick(first, mine_high)
    for part in got:
        first = first + code.decode(part)
    return first, pick(second, mine_low) + code.decode(got_low)


def place(own, others, mine, count):
    out = jnp.zeros((count,) + own.shape, own.dtype)
    out = lax.dynamic_update_index_in_dim(out, own, mine, 0)
    for k, part in others:
        out = lax.dynamic_update_index_in_dim(out, part, mine ^ k, 0)
    return out


def all_gather(first, second, axis, size, low, high):
    me = lax.axis_index(axis)
    mine_low, mine_high = me % low, me // low
    got_low = exchange(second, axis, size, 1)
    got = [(k, exchange(first, axis, size, k * low)) for k in range(1, high)]
    second = place(second, [(1, got_low)], mine_low, low)
    got_second = [(k, exchange(second, axis, size, k * low)) for k in range(1, high)]
    first = place(first, got, mine_high, high)
    got_first = exchange(first, axis, size, 1)
    second = place(second, got_second, mine_high, high)
    first = place(first, [(1, got_first)], mine_low, low)
    return first, second


def inverse_factor(gram):
    factor = jnp.linalg.cholesky(gram)
    eye = jnp.eye(gram.shape[0], dtype=F32)
    return jax.scipy.linalg.solve_triangular(factor, eye, lower=True)


def make(mesh):
    subjects, blocks = mesh.shape["subj"], mesh.shape["vox"]
    low = 2
    high = subjects // low

    def on_device(scans, test_matrix, lengths, block_subject):
        time_rows, voxels = scans.shape
        rank = test_matrix.shape[1]
        all_voxels = voxels * blocks
        position = lax.axis_index("subj")
        slot_ids = jnp.arange(block_subject.shape[0], dtype=jnp.int32)
        subject = jnp.sum(jnp.where(slot_ids == position, block_subject, 0))
        length = jnp.sum(jnp.where(slot_ids == subject, lengths, 0))
        live_rows = (jnp.arange(time_rows, dtype=jnp.int32) < length)[:, None]
        cut = voxels * 2 // 3

        def sketch_sum(scores, code):
            partial = lax.dot_general(
                scans, scores, (((0,), (0,)), ((), ())), preferred_element_type=F32
            )
            first = partial[:cut].reshape(low, high, cut // subjects, rank)
            second = partial[cut:].reshape(high, low, (voxels - cut) // subjects, rank)
            return reduce_scatter(first, second, code, "subj", subjects, low, high)

        def gather(first, second):
            return all_gather(first, second, "subj", subjects, low, high)

        partial = jnp.dot(scans, test_matrix, preferred_element_type=F32)
        summed = butterfly(partial, "vox", blocks)
        scores = jnp.where(live_rows, summed, 0.0).astype(BF16)

        first, second = sketch_sum(scores, Plain)
        first, second = gather(first.astype(BF16), second.astype(BF16))
        sketch = jnp.concatenate([first.reshape(-1, rank), second.reshape(-1, rank)])
        raw = jnp.dot(scans, sketch, preferred_element_type=F32)
        local = lax.dot_general(
            sketch, sketch, (((0,), (0,)), ((), ())), preferred_element_type=F32
        )
        both = butterfly(jnp.concatenate([raw, local]), "vox", blocks)
        inverse = inverse_factor(both[time_rows:] / all_voxels)
        scores = jnp.dot(both[:time_rows], inverse.T, precision=HIGHEST)
        scores = jnp.where(live_rows, scores, 0.0).astype(BF16)

        first, second = sketch_sum(scores, Fixed)
        whole = gather(Fixed.encode(first), Fixed.encode(second))
        own = jnp.concatenate([first, second])
        local = lax.dot_general(own, own, (((0,), (0,)), ((), ())), precision=HIGHEST)
        gram = butterfly(butterfly(local, "vox", blocks), "subj", subjects)
        inverse = inverse_factor(gram / all_voxels)
        parts = []
        for part in whole:
            part = part.reshape((subjects,) + part.shape[2:])
            parts.append(jax.vmap(Fixed.decode)(part).reshape(-1, rank))
        return jnp.dot(jnp.concatenate(parts), inverse.T, precision=HIGHEST)

    return on_device


def solution(mesh):
    placed = (P("subj", "vox"), P("vox", None), P(), P())
    return jax.shard_map(
        make(mesh), mesh=mesh, in_specs=placed, out_specs=P("vox", None), check_vma=False
    )
```

```python
import functools

import jax
import jax.numpy as jnp
from jax import lax
from jax.experimental import pallas as pl
from jax.experimental.pallas import tpu as pltpu
from jax.sharding import PartitionSpec as P

F32 = jnp.float32
BF16 = jnp.bfloat16
I16 = jnp.int16
HIGHEST = lax.Precision.HIGHEST
STEPS = 64.0
LOW = 2
VMEM_BYTES = 48 << 20
WHOLE = pl.BlockSpec(memory_space=pltpu.VMEM)


def exchange(value, axis, size, mask):
    return lax.ppermute(value, axis, [(i, i ^ mask) for i in range(size)])


def butterfly(value, axis, size):
    mask = 1
    while mask < size:
        value = value + exchange(value, axis, size, mask)
        mask *= 2
    return value


class Plain:
    pad = 0
    dtype = BF16

    @staticmethod
    def encode(value):
        return value.astype(BF16)

    @staticmethod
    def decode(sent):
        return sent.astype(F32)


class Fixed:
    pad = 16
    dtype = I16

    @staticmethod
    def encode(value):
        top = jnp.maximum(jnp.max(jnp.abs(value), axis=0, keepdims=True), 1e-30)
        power = jnp.ceil(jnp.log2(top * (1.0 / 32000.0)) * STEPS)
        codes = jnp.round(value * jnp.exp2(power * (-1.0 / STEPS)))
        codes = jnp.clip(codes, -32767.0, 32767.0)
        rows = jnp.broadcast_to(power, (Fixed.pad, value.shape[1]))
        return jnp.concatenate([codes, rows]).astype(jnp.int32).astype(I16)

    @staticmethod
    def decode(sent):
        wide = sent.astype(jnp.int32).astype(F32)
        rows = wide.shape[0] - Fixed.pad
        return wide[:rows] * jnp.exp2(wide[rows : rows + 1] * (1.0 / STEPS))


def params():
    return pltpu.CompilerParams(vmem_limit_bytes=VMEM_BYTES)


def sketch_kernel(code, count, pos_ref, scores_ref, *refs):
    for u in range(count):
        product = lax.dot_general(
            scores_ref[...], refs[u][...], (((0,), (0,)), ((), ())), preferred_element_type=F32
        )
        out = refs[count + u] if len(refs) == 2 * count else refs[count].at[u]
        out[...] = code.encode(product.T)


def unit_of(high, j, k, pos):
    if j is None:
        return LOW * high + (pos[1] ^ k)
    return (pos[0] ^ j) * high + (pos[1] ^ k)


def sketch_part(scans, scores, pos, high, j, ks, code, apart, per_step):
    time_rows, voxels = scans.shape
    rank = scores.shape[1]
    n = voxels // ((LOW + 1) * high)
    rows = n + code.pad
    first = ks[0]
    steps = len(ks) // per_step

    def column(u):
        return lambda g, pos: (0, unit_of(high, j, first + g * per_step + u, pos))

    if apart:
        out_shape = [jax.ShapeDtypeStruct((rows, rank), code.dtype)] * len(ks)
        out_specs = [pl.BlockSpec((rows, rank), lambda g, pos: (0, 0))] * len(ks)
    else:
        out_shape = jax.ShapeDtypeStruct((len(ks), rows, rank), code.dtype)
        out_specs = pl.BlockSpec((per_step, rows, rank), lambda g, pos: (g, 0, 0))
    return pl.pallas_call(
        functools.partial(sketch_kernel, code, per_step),
        out_shape=out_shape,
        grid_spec=pltpu.PrefetchScalarGridSpec(
            num_scalar_prefetch=1,
            grid=(steps,),
            in_specs=[pl.BlockSpec((time_rows, rank), lambda g, pos: (0, 0))]
            + [pl.BlockSpec((time_rows, n), column(u)) for u in range(per_step)],
            out_specs=out_specs,
        ),
        compiler_params=params(),
        cost_estimate=pl.CostEstimate(
            flops=2 * time_rows * n * rank * len(ks),
            bytes_accessed=time_rows * n * 2 * len(ks),
            transcendentals=0,
        ),
    )(pos, scores, *([scans] * per_step))


def small_call(kernel, out_shape, *args):
    return pl.pallas_call(
        kernel,
        out_shape=out_shape,
        in_specs=[WHOLE] * len(args),
        out_specs=jax.tree.map(lambda _: WHOLE, out_shape),
        compiler_params=params(),
    )(*args)


def add_pieces_kernel(code, count, own_ref, got_ref, *outs):
    for k in range(count):
        outs[k][...] = code.encode(code.decode(own_ref[k]) + code.decode(got_ref[k]))


def add_all_kernel(code, with_gram, *refs):
    outs = refs[-2:] if with_gram else refs[-1:]
    parts = refs[: len(refs) - len(outs)]
    total = code.decode(parts[0][...])
    for part in parts[1:]:
        total = total + code.decode(part[...])
    outs[0][...] = code.encode(total)
    if with_gram:
        outs[1][...] = lax.dot_general(
            total, total, (((0,), (0,)), ((), ())), precision=HIGHEST,
            preferred_element_type=F32,
        )


def add_halves_kernel(code, pos_ref, *refs):
    parts, (keep_ref, send_ref) = refs[:-2], refs[-2:]
    total = code.decode(parts[0][...])
    for part in parts[1:]:
        total = total + code.decode(part[...])
    half = total.shape[0] // 2
    lower = pos_ref[0] == 0
    keep_ref[...] = code.encode(jnp.where(lower, total[:half], total[half:]))
    send_ref[...] = code.encode(jnp.where(lower, total[half:], total[:half]))


def add_all(code, with_gram, parts):
    rank = parts[0].shape[1]
    out = [jax.ShapeDtypeStruct(parts[0].shape, code.dtype)]
    if with_gram:
        out.append(jax.ShapeDtypeStruct((rank, rank), F32))
    return small_call(functools.partial(add_all_kernel, code, with_gram), out, *parts)


def project_kernel(has_base, with_own, count, pos_ref, *refs):
    refs = list(refs)
    base = refs.pop(0) if has_base else None
    out = refs.pop()
    scans, pieces = refs[:count], refs[count:]
    time_rows = scans[0].shape[0]
    rank = out.shape[1]
    total = jnp.zeros((time_rows, rank), F32)
    gram = jnp.zeros((rank, rank), F32)
    for u in range(count):
        piece = pieces[u][...] if len(pieces) == count else pieces[0][u]
        total += jnp.dot(scans[u][...], piece, preferred_element_type=F32)
        gram += lax.dot_general(
            piece, piece, (((0,), (0,)), ((), ())), preferred_element_type=F32
        )
    if has_base:
        out[:time_rows] = base[:time_rows] + total
        out[time_rows:] = base[time_rows:] + gram
    else:
        out[:time_rows] = total
        out[time_rows:] = gram


def project(scans, pieces, pos, high, j, base=None):
    time_rows, voxels = scans.shape
    n = voxels // ((LOW + 1) * high)
    rank = pieces[0].shape[-1]

    def column(u):
        return lambda g, pos: (0, unit_of(high, j, u, pos))

    full = lambda shape: pl.BlockSpec(shape, lambda g, pos: (0,) * len(shape))
    bases = [] if base is None else [base]
    return pl.pallas_call(
        functools.partial(project_kernel, base is not None, True, high),
        out_shape=jax.ShapeDtypeStruct((time_rows + rank, rank), F32),
        grid_spec=pltpu.PrefetchScalarGridSpec(
            num_scalar_prefetch=1,
            grid=(1,),
            in_specs=[full(b.shape) for b in bases]
            + [pl.BlockSpec((time_rows, n), column(u)) for u in range(high)]
            + [full(p.shape) for p in pieces],
            out_specs=full((time_rows + rank, rank)),
        ),
        compiler_params=params(),
        cost_estimate=pl.CostEstimate(
            flops=2 * (time_rows + rank) * n * rank * high,
            bytes_accessed=time_rows * n * 2 * high,
            transcendentals=0,
        ),
    )(pos, *bases, *([scans] * high), *pieces)


def finish_kernel(high, n, pos_ref, inverse_ref, *refs):
    refs, (out, held, sems) = refs[:-3], refs[-3:]
    first, low_got, second = refs[:high], refs[high], refs[high + 1 :]
    copies = []

    def emit(slot, codes, unit, offset, rows):
        scaled = Fixed.decode(codes)
        value = lax.dot_general(
            scaled, inverse_ref[...], (((1,), (1,)), ((), ())), precision=HIGHEST,
            preferred_element_type=F32,
        )
        held[slot, offset : offset + rows] = value
        start = pl.multiple_of(unit * n, n)
        if offset + rows == n:
            copy = pltpu.make_async_copy(held.at[slot], out.at[pl.ds(start, n)], sems.at[slot])
            copy.start()
            copies.append(copy)

    pos = (pos_ref[0], pos_ref[1])
    for k in range(high):
        emit(k, first[k][...], unit_of(high, 0, k, pos), 0, n)
    for k in range(high):
        emit(high + k, low_got[k], unit_of(high, 1, k, pos), 0, n)
    half = n // 2
    for k in range(high):
        for side in range(2):
            codes = second[k][side]
            emit(2 * high + k, codes, unit_of(high, None, k, pos), side * half, half)
    for copy in copies:
        copy.wait()


def finish(first, low_got, second, inverse, pos, high, n):
    rank = inverse.shape[0]
    units = (LOW + 1) * high
    args = [inverse, *first, low_got, *second]
    return pl.pallas_call(
        functools.partial(finish_kernel, high, n),
        out_shape=jax.ShapeDtypeStruct((units * n, rank), F32),
        in_specs=[pl.BlockSpec(memory_space=pltpu.SMEM)] + [WHOLE] * len(args),
        out_specs=pl.BlockSpec(memory_space=pl.ANY),
        scratch_shapes=[
            pltpu.VMEM((units, n, rank), F32),
            pltpu.SemaphoreType.DMA((units,)),
        ],
        compiler_params=params(),
    )(pos, *args)


def inverse_factor(gram):
    factor = jnp.linalg.cholesky(gram)
    eye = jnp.eye(gram.shape[0], dtype=F32)
    return jax.scipy.linalg.solve_triangular(factor, eye, lower=True)


def make(mesh):
    subjects, blocks = mesh.shape["subj"], mesh.shape["vox"]
    high = subjects // LOW
    swap = functools.partial(exchange, axis="subj", size=subjects)

    def on_device(scans, test_matrix, lengths, block_subject):
        time_rows, voxels = scans.shape
        rank = test_matrix.shape[1]
        all_voxels = voxels * blocks
        n = voxels // ((LOW + 1) * high)
        me = lax.axis_index("subj")
        pos = jnp.stack([me % LOW, me // LOW]).astype(jnp.int32)
        slot_ids = jnp.arange(block_subject.shape[0], dtype=jnp.int32)
        subject = jnp.sum(jnp.where(slot_ids == me, block_subject, 0))
        length = jnp.sum(jnp.where(slot_ids == subject, lengths, 0))
        live_rows = (jnp.arange(time_rows, dtype=jnp.int32) < length)[:, None]

        def sketch_sum(scores, code, with_gram):
            rows = n + code.pad
            part = functools.partial(sketch_part, scans, scores, pos, high)
            ks = list(range(high))
            away = part(1, ks, code, False, high // 2)
            got_away = swap(away, mask=1)
            second = part(None, ks[1:], code, True, high - 1)
            got_second = [swap(second[k - 1], mask=k * LOW) for k in ks[1:]]
            home = part(0, ks, code, False, high // 2)
            (second_own,) = part(None, ks[:1], code, True, 1)
            piece = jax.ShapeDtypeStruct((rows, rank), code.dtype)
            half = jax.ShapeDtypeStruct((n // 2 + code.pad, rank), code.dtype)
            first = small_call(
                functools.partial(add_pieces_kernel, code, high), [piece] * high, home, got_away
            )
            got_first = [swap(first[k], mask=k * LOW) for k in ks[1:]]
            keep, send = pl.pallas_call(
                functools.partial(add_halves_kernel, code),
                out_shape=[half, half],
                in_specs=[pl.BlockSpec(memory_space=pltpu.SMEM)] + [WHOLE] * high,
                out_specs=[WHOLE, WHOLE],
                compiler_params=params(),
            )(pos, second_own, *got_second)
            got_send = swap(send, mask=1)
            return (
                add_all(code, with_gram, [first[0], *got_first]),
                add_all(code, with_gram, [keep, got_send]),
            )

        def gather(first, second):
            ks = list(range(1, high))
            firsts = [first] + [swap(first, mask=k * LOW) for k in ks]
            got = swap(second, mask=1)
            lower = pos[0] == 0
            pair = jnp.stack([jnp.where(lower, second, got), jnp.where(lower, got, second)])
            low_got = swap(jnp.stack(firsts), mask=1)
            seconds = [pair] + [swap(pair, mask=k * LOW) for k in ks]
            return firsts, low_got, seconds

        partial = jnp.dot(scans, test_matrix, preferred_element_type=F32)
        summed = butterfly(partial, "vox", blocks)
        scores = jnp.where(live_rows, summed, 0.0).astype(BF16)

        (first,), (second,) = sketch_sum(scores, Plain, False)
        firsts, low_got, seconds = gather(first, second)
        both = project(scans, firsts, pos, high, 0)
        seconds = [part.reshape(n, rank) for part in seconds]
        both = project(scans, seconds, pos, high, None, both)
        both = project(scans, [low_got], pos, high, 1, both)
        both = butterfly(both, "vox", blocks)
        inverse = inverse_factor(both[time_rows:] / all_voxels)
        scores = jnp.dot(both[:time_rows], inverse.T, precision=HIGHEST)
        scores = jnp.where(live_rows, scores, 0.0).astype(BF16)

        (first, gram_first), (second, gram_second) = sketch_sum(scores, Fixed, True)
        gram = butterfly(gram_first + gram_second, "vox", blocks)
        gram = butterfly(gram, "subj", subjects)
        inverse = inverse_factor(gram / all_voxels)
        firsts, low_got, seconds = gather(first, second)
        return finish(firsts, low_got, seconds, inverse, pos, high, n)

    return on_device


def solution(mesh):
    placed = (P("subj", "vox"), P("vox", None), P(), P())
    return jax.shard_map(
        make(mesh), mesh=mesh, in_specs=placed, out_specs=P("vox", None), check_vma=False
    )
```

```python
import functools

import jax
import jax.numpy as jnp
from jax import lax
from jax.experimental import pallas as pl
from jax.experimental.pallas import tpu as pltpu
from jax.sharding import PartitionSpec as P

F32 = jnp.float32
BF16 = jnp.bfloat16
I16 = jnp.int16
HIGHEST = lax.Precision.HIGHEST
STEPS = 64.0
LOW = 2
GROUP = 8
VMEM_BYTES = 48 << 20
WHOLE = pl.BlockSpec(memory_space=pltpu.VMEM)


def exchange(value, axis, size, mask):
    return lax.ppermute(value, axis, [(i, i ^ mask) for i in range(size)])


def butterfly(value, axis, size):
    mask = 1
    while 2 * mask < size:
        value = value + exchange(value, axis, size, mask)
        mask *= 2
    return value, exchange(value, axis, size, mask)


class Plain:
    pad = 0
    dtype = BF16

    @staticmethod
    def encode(value):
        return value.astype(BF16)

    @staticmethod
    def decode(sent):
        return sent.astype(F32)


class Fixed:
    pad = 16
    dtype = I16

    @staticmethod
    def encode(value):
        top = jnp.maximum(jnp.max(jnp.abs(value), axis=0, keepdims=True), 1e-30)
        power = jnp.ceil(jnp.log2(top * (1.0 / 32000.0)) * STEPS)
        codes = jnp.round(value * jnp.exp2(power * (-1.0 / STEPS)))
        codes = jnp.clip(codes, -32767.0, 32767.0)
        rows = jnp.broadcast_to(power, (Fixed.pad, value.shape[1]))
        return jnp.concatenate([codes, rows]).astype(jnp.int32).astype(I16)

    @staticmethod
    def decode(sent):
        wide = sent.astype(jnp.int32).astype(F32)
        rows = wide.shape[0] - Fixed.pad
        return wide[:rows] * jnp.exp2(wide[rows : rows + 1] * (1.0 / STEPS))


def params():
    return pltpu.CompilerParams(vmem_limit_bytes=VMEM_BYTES)


def sketch_kernel(code, count, pos_ref, scores_ref, *refs):
    for u in range(count):
        product = lax.dot_general(
            scores_ref[...], refs[u][...], (((0,), (0,)), ((), ())), preferred_element_type=F32
        )
        out = refs[count + u] if len(refs) == 2 * count else refs[count].at[u]
        out[...] = code.encode(product.T)


def unit_of(high, j, k, pos):
    if j is None:
        return LOW * high + (pos[1] ^ k)
    return (pos[0] ^ j) * high + (pos[1] ^ k)


def sketch_part(scans, scores, pos, high, j, ks, code, apart, per_step):
    time_rows, voxels = scans.shape
    rank = scores.shape[1]
    n = voxels // ((LOW + 1) * high)
    rows = n + code.pad
    first = ks[0]
    steps = len(ks) // per_step

    def column(u):
        return lambda g, pos: (0, unit_of(high, j, first + g * per_step + u, pos))

    if apart:
        out_shape = [jax.ShapeDtypeStruct((rows, rank), code.dtype)] * len(ks)
        out_specs = [pl.BlockSpec((rows, rank), lambda g, pos: (0, 0))] * len(ks)
    else:
        out_shape = jax.ShapeDtypeStruct((len(ks), rows, rank), code.dtype)
        out_specs = pl.BlockSpec((per_step, rows, rank), lambda g, pos: (g, 0, 0))
    return pl.pallas_call(
        functools.partial(sketch_kernel, code, per_step),
        out_shape=out_shape,
        grid_spec=pltpu.PrefetchScalarGridSpec(
            num_scalar_prefetch=1,
            grid=(steps,),
            in_specs=[pl.BlockSpec((time_rows, rank), lambda g, pos: (0, 0))]
            + [pl.BlockSpec((time_rows, n), column(u)) for u in range(per_step)],
            out_specs=out_specs,
        ),
        compiler_params=params(),
        cost_estimate=pl.CostEstimate(
            flops=2 * time_rows * n * rank * len(ks),
            bytes_accessed=time_rows * n * 2 * len(ks),
            transcendentals=0,
        ),
    )(pos, scores, *([scans] * per_step))


def small_call(kernel, out_shape, *args):
    return pl.pallas_call(
        kernel,
        out_shape=out_shape,
        in_specs=[WHOLE] * len(args),
        out_specs=jax.tree.map(lambda _: WHOLE, out_shape),
        compiler_params=params(),
    )(*args)


def add_pieces_kernel(code, count, own_ref, got_ref, *outs):
    for k in range(count):
        outs[k][...] = code.encode(code.decode(own_ref[k]) + code.decode(got_ref[k]))


def add_all_kernel(code, with_gram, *refs):
    outs = refs[-2:] if with_gram else refs[-1:]
    parts = refs[: len(refs) - len(outs)]
    total = code.decode(parts[0][...])
    for part in parts[1:]:
        total = total + code.decode(part[...])
    outs[0][...] = code.encode(total)
    if with_gram:
        outs[1][...] = lax.dot_general(
            total, total, (((0,), (0,)), ((), ())), precision=HIGHEST,
            preferred_element_type=F32,
        )


def add_halves_kernel(code, pos_ref, *refs):
    parts, (keep_ref, send_ref) = refs[:-2], refs[-2:]
    total = code.decode(parts[0][...])
    for part in parts[1:]:
        total = total + code.decode(part[...])
    half = total.shape[0] // 2
    lower = pos_ref[0] == 0
    keep_ref[...] = code.encode(jnp.where(lower, total[:half], total[half:]))
    send_ref[...] = code.encode(jnp.where(lower, total[half:], total[:half]))


def add_all(code, with_gram, parts):
    rank = parts[0].shape[1]
    out = [jax.ShapeDtypeStruct(parts[0].shape, code.dtype)]
    if with_gram:
        out.append(jax.ShapeDtypeStruct((rank, rank), F32))
    return small_call(functools.partial(add_all_kernel, code, with_gram), out, *parts)


def project_kernel(has_base, with_own, count, pos_ref, *refs):
    refs = list(refs)
    base = refs.pop(0) if has_base else None
    out = refs.pop()
    scans, pieces = refs[:count], refs[count:]
    time_rows = scans[0].shape[0]
    rank = out.shape[1]
    total = jnp.zeros((time_rows, rank), F32)
    gram = jnp.zeros((rank, rank), F32)
    for u in range(count):
        piece = pieces[u][...] if len(pieces) == count else pieces[0][u]
        total += jnp.dot(scans[u][...], piece, preferred_element_type=F32)
        gram += lax.dot_general(
            piece, piece, (((0,), (0,)), ((), ())), preferred_element_type=F32
        )
    if has_base:
        out[:time_rows] = base[:time_rows] + total
        out[time_rows:] = base[time_rows:] + gram
    else:
        out[:time_rows] = total
        out[time_rows:] = gram


def project(scans, pieces, pos, high, j, base=None):
    time_rows, voxels = scans.shape
    n = voxels // ((LOW + 1) * high)
    rank = pieces[0].shape[-1]

    def column(u):
        return lambda g, pos: (0, unit_of(high, j, u, pos))

    full = lambda shape: pl.BlockSpec(shape, lambda g, pos: (0,) * len(shape))
    bases = [] if base is None else [base]
    return pl.pallas_call(
        functools.partial(project_kernel, base is not None, True, high),
        out_shape=jax.ShapeDtypeStruct((time_rows + rank, rank), F32),
        grid_spec=pltpu.PrefetchScalarGridSpec(
            num_scalar_prefetch=1,
            grid=(1,),
            in_specs=[full(b.shape) for b in bases]
            + [pl.BlockSpec((time_rows, n), column(u)) for u in range(high)]
            + [full(p.shape) for p in pieces],
            out_specs=full((time_rows + rank, rank)),
        ),
        compiler_params=params(),
        cost_estimate=pl.CostEstimate(
            flops=2 * (time_rows + rank) * n * rank * high,
            bytes_accessed=time_rows * n * 2 * high,
            transcendentals=0,
        ),
    )(pos, *bases, *([scans] * high), *pieces)


def finish_kernel(high, n, pos_ref, inverse_ref, *refs):
    refs, (out, held, sems) = refs[:-3], refs[-3:]
    first, low_got, second = refs[:high], refs[high], refs[high + 1 :]
    copies = []

    def emit(slot, codes, unit, offset, rows):
        scaled = Fixed.decode(codes)
        value = times_transpose(scaled, inverse_ref[...])
        held[slot, offset : offset + rows] = value
        start = pl.multiple_of(unit * n, n)
        if offset + rows == n:
            copy = pltpu.make_async_copy(held.at[slot], out.at[pl.ds(start, n)], sems.at[slot])
            copy.start()
            copies.append(copy)

    pos = (pos_ref[0], pos_ref[1])
    for k in range(high):
        emit(k, first[k][...], unit_of(high, 0, k, pos), 0, n)
    for k in range(high):
        emit(high + k, low_got[k], unit_of(high, 1, k, pos), 0, n)
    half = n // 2
    for k in range(high):
        for side in range(2):
            codes = second[k][side]
            emit(2 * high + k, codes, unit_of(high, None, k, pos), side * half, half)
    for copy in copies:
        copy.wait()


def finish(first, low_got, second, inverse, pos, high, n):
    rank = inverse.shape[0]
    units = (LOW + 1) * high
    args = [inverse, *first, low_got, *second]
    return pl.pallas_call(
        functools.partial(finish_kernel, high, n),
        out_shape=jax.ShapeDtypeStruct((units * n, rank), F32),
        in_specs=[pl.BlockSpec(memory_space=pltpu.SMEM)] + [WHOLE] * len(args),
        out_specs=pl.BlockSpec(memory_space=pl.ANY),
        scratch_shapes=[
            pltpu.VMEM((units, n, rank), F32),
            pltpu.SemaphoreType.DMA((units,)),
        ],
        compiler_params=params(),
    )(pos, *args)


def inverse_factor(gram):
    size = gram.shape[0]
    groups = size // GROUP
    shape = (GROUP, size)
    sub = lax.broadcasted_iota(jnp.int32, shape, 0)
    lane = lax.broadcasted_iota(jnp.int32, shape, 1)
    left = [gram[GROUP * i : GROUP * (i + 1)] for i in range(groups)]
    right = [jnp.where(sub + GROUP * i == lane, 1.0, 0.0).astype(F32) for i in range(groups)]
    for g in range(groups):
        first = g * GROUP
        wide = lambda value: jnp.broadcast_to(value, shape)
        rows = [wide(left[g][t : t + 1]) for t in range(GROUP)]
        inverse_rows = [wide(right[g][t : t + 1]) for t in range(GROUP)]
        block = [
            [wide(left[g][t : t + 1, first + u : first + u + 1]) for u in range(GROUP)]
            for t in range(GROUP)
        ]
        below = range(g + 1, groups)
        columns = {
            i: [wide(left[i][:, first + u : first + u + 1]) for u in range(GROUP)] for i in below
        }
        scaled = []
        for t in range(GROUP):
            pivot = 1.0 / block[t][t]
            scaled.append((rows[t] * pivot, inverse_rows[t] * pivot))
            for u in range(t + 1, GROUP):
                factor = block[t][u] * pivot
                for w in range(u, GROUP):
                    block[u][w] = block[u][w] - factor * block[t][w]
                rows[u] = rows[u] - factor * rows[t]
                inverse_rows[u] = inverse_rows[u] - factor * inverse_rows[t]
                for i in below:
                    columns[i][u] = columns[i][u] - factor * columns[i][t]
        for i in below:
            for t in range(GROUP):
                left[i] = left[i] - columns[i][t] * scaled[t][0]
                right[i] = right[i] - columns[i][t] * scaled[t][1]
        for t in range(GROUP):
            left[g] = jnp.where(sub == t, rows[t], left[g])
            right[g] = jnp.where(sub == t, inverse_rows[t], right[g])
    out = []
    for g in range(groups):
        pivots = jnp.sum(
            jnp.where(sub + GROUP * g == lane, left[g], 0.0), axis=1, keepdims=True
        )
        out.append(right[g] * lax.rsqrt(pivots))
    return jnp.concatenate(out)


def times_transpose(value, inverse):
    return lax.dot_general(
        value, inverse, (((1,), (1,)), ((), ())), precision=HIGHEST, preferred_element_type=F32
    )


def normalise_kernel(all_voxels, length_ref, mine_ref, got_ref, out_ref):
    time_rows = out_ref.shape[0]
    both = mine_ref[...] + got_ref[...]
    inverse = inverse_factor(both[time_rows:] * (1.0 / all_voxels))
    scores = times_transpose(both[:time_rows], inverse)
    live = lax.broadcasted_iota(jnp.int32, scores.shape, 0) < length_ref[0]
    out_ref[...] = jnp.where(live, scores, 0.0).astype(BF16)


def invert_kernel(all_voxels, mine_ref, got_ref, out_ref):
    out_ref[...] = inverse_factor((mine_ref[...] + got_ref[...]) * (1.0 / all_voxels))


def make(mesh):
    subjects, blocks = mesh.shape["subj"], mesh.shape["vox"]
    high = subjects // LOW
    swap = functools.partial(exchange, axis="subj", size=subjects)

    def on_device(scans, test_matrix, lengths, block_subject):
        time_rows, voxels = scans.shape
        rank = test_matrix.shape[1]
        all_voxels = voxels * blocks
        n = voxels // ((LOW + 1) * high)
        me = lax.axis_index("subj")
        pos = jnp.stack([me % LOW, me // LOW]).astype(jnp.int32)
        slot_ids = jnp.arange(block_subject.shape[0], dtype=jnp.int32)
        subject = jnp.sum(jnp.where(slot_ids == me, block_subject, 0))
        length = jnp.sum(jnp.where(slot_ids == subject, lengths, 0))
        live_rows = (jnp.arange(time_rows, dtype=jnp.int32) < length)[:, None]

        def sketch_sum(scores, code, with_gram):
            rows = n + code.pad
            part = functools.partial(sketch_part, scans, scores, pos, high)
            ks = list(range(high))
            away = part(1, ks, code, False, high // 2)
            got_away = swap(away, mask=1)
            second = part(None, ks[1:], code, True, high - 1)
            got_second = [swap(second[k - 1], mask=k * LOW) for k in ks[1:]]
            got_away, *got_second = lax.optimization_barrier((got_away, *got_second))
            home = part(0, ks, code, False, high // 2)
            (second_own,) = part(None, ks[:1], code, True, 1)
            piece = jax.ShapeDtypeStruct((rows, rank), code.dtype)
            half = jax.ShapeDtypeStruct((n // 2 + code.pad, rank), code.dtype)
            first = small_call(
                functools.partial(add_pieces_kernel, code, high), [piece] * high, home, got_away
            )
            got_first = [swap(first[k], mask=k * LOW) for k in ks[1:]]
            keep, send = pl.pallas_call(
                functools.partial(add_halves_kernel, code),
                out_shape=[half, half],
                in_specs=[pl.BlockSpec(memory_space=pltpu.SMEM)] + [WHOLE] * high,
                out_specs=[WHOLE, WHOLE],
                compiler_params=params(),
            )(pos, second_own, *got_second)
            got_send = swap(send, mask=1)
            return (
                add_all(code, with_gram, [first[0], *got_first]),
                add_all(code, with_gram, [keep, got_send]),
            )

        def gather(first, second, *others):
            ks = list(range(1, high))
            firsts = [first] + [swap(first, mask=k * LOW) for k in ks]
            got = swap(second, mask=1)
            lower = pos[0] == 0
            pair = jnp.stack([jnp.where(lower, second, got), jnp.where(lower, got, second)])
            firsts, pair, others = lax.optimization_barrier((firsts, pair, others))
            low_got = swap(jnp.stack(firsts), mask=1)
            seconds = [pair] + [swap(pair, mask=k * LOW) for k in ks]
            return firsts, low_got, seconds, others

        partial = jnp.dot(scans, test_matrix, preferred_element_type=F32)
        summed = sum(butterfly(partial, "vox", blocks))
        scores = jnp.where(live_rows, summed, 0.0).astype(BF16)

        (first,), (second,) = sketch_sum(scores, Plain, False)
        firsts, low_got, seconds, _ = gather(first, second)
        both = project(scans, firsts, pos, high, 0)
        seconds = [part.reshape(n, rank) for part in seconds]
        both = project(scans, seconds, pos, high, None, both)
        both = project(scans, [low_got], pos, high, 1, both)
        mine, got = butterfly(both, "vox", blocks)
        scores = pl.pallas_call(
            functools.partial(normalise_kernel, all_voxels),
            out_shape=jax.ShapeDtypeStruct((time_rows, rank), BF16),
            in_specs=[pl.BlockSpec(memory_space=pltpu.SMEM), WHOLE, WHOLE],
            out_specs=WHOLE,
            compiler_params=params(),
        )(length[None], mine, got)

        (first, gram_first), (second, gram_second) = sketch_sum(scores, Fixed, True)
        gram = sum(butterfly(gram_first + gram_second, "vox", blocks))
        mine, got = butterfly(gram, "subj", subjects)
        inverse = small_call(
            functools.partial(invert_kernel, all_voxels),
            jax.ShapeDtypeStruct((rank, rank), F32), mine, got,
        )
        firsts, low_got, seconds, (inverse,) = gather(first, second, inverse)
        return finish(firsts, low_got, seconds, inverse, pos, high, n)

    return on_device


def solution(mesh):
    placed = (P("subj", "vox"), P("vox", None), P(), P())
    return jax.shard_map(
        make(mesh), mesh=mesh, in_specs=placed, out_specs=P("vox", None), check_vma=False
    )
```

```python
import functools

import jax
import jax.numpy as jnp
from jax import lax
from jax.experimental import pallas as pl
from jax.experimental.pallas import tpu as pltpu
from jax.sharding import PartitionSpec as P

F32 = jnp.float32
BF16 = jnp.bfloat16
I16 = jnp.int16
HIGHEST = lax.Precision.HIGHEST
STEPS = 64.0
LOW = 2
GROUP = 8
LANES = 128
VMEM_BYTES = 48 << 20
WHOLE = pl.BlockSpec(memory_space=pltpu.VMEM)


def exchange(value, axis, size, mask):
    return lax.ppermute(value, axis, [(i, i ^ mask) for i in range(size)])


def butterfly(value, axis, size):
    mask = 1
    while 2 * mask < size:
        value = value + exchange(value, axis, size, mask)
        mask *= 2
    return value, exchange(value, axis, size, mask)


class Plain:
    pad = 0
    dtype = BF16

    @staticmethod
    def encode(value):
        return value.astype(BF16)

    @staticmethod
    def decode(sent):
        return sent.astype(F32)


class Fixed:
    pad = 16
    dtype = I16

    @staticmethod
    def encode(value):
        top = jnp.maximum(jnp.max(jnp.abs(value), axis=0, keepdims=True), 1e-30)
        power = jnp.ceil(jnp.log2(top * (1.0 / 32000.0)) * STEPS)
        codes = jnp.round(value * jnp.exp2(power * (-1.0 / STEPS)))
        codes = jnp.clip(codes, -32767.0, 32767.0)
        rows = jnp.broadcast_to(power, (Fixed.pad, value.shape[1]))
        return jnp.concatenate([codes, rows]).astype(jnp.int32).astype(I16)

    @staticmethod
    def decode(sent):
        wide = sent.astype(jnp.int32).astype(F32)
        rows = wide.shape[0] - Fixed.pad
        return wide[:rows] * jnp.exp2(wide[rows : rows + 1] * (1.0 / STEPS))


def params():
    return pltpu.CompilerParams(vmem_limit_bytes=VMEM_BYTES)


class Layout:
    def __init__(self, voxels, subjects):
        self.high = subjects // LOW
        unit = subjects * LANES
        for top, bottom in ((5, 6), (3, 4), (2, 3), (1, 2)):
            self.cut = voxels * top // bottom
            self.pair = (voxels - self.cut) // self.high
            if self.cut % unit == 0 and voxels % unit == 0 and self.cut % self.pair == 0:
                break
        self.single = self.cut // subjects

    def columns(self, j):
        return self.pair if j is None else self.single

    def block(self, j, k, pos):
        if j is None:
            return self.cut // self.pair + (pos[1] ^ k)
        return (pos[0] ^ j) * self.high + (pos[1] ^ k)


def sketch_kernel(code, apart, count, pos_ref, scores_ref, *refs):
    for u in range(count):
        product = lax.dot_general(
            scores_ref[...], refs[u][...], (((0,), (0,)), ((), ())), preferred_element_type=F32
        )
        out = refs[count + u] if apart else refs[count].at[u]
        out[...] = code.encode(product.T)


def sketch_part(scans, layout, pos, scores, j, ks, code, apart, per_step):
    time_rows = scans.shape[0]
    rank = scores.shape[1]
    n = layout.columns(j)
    rows = n + code.pad
    steps = len(ks) // per_step

    def column(u):
        return lambda g, pos: (0, layout.block(j, ks[0] + g * per_step + u, pos))

    if apart:
        out_shape = [jax.ShapeDtypeStruct((rows, rank), code.dtype)] * len(ks)
        out_specs = [pl.BlockSpec((rows, rank), lambda g, pos: (0, 0))] * len(ks)
    else:
        out_shape = jax.ShapeDtypeStruct((len(ks), rows, rank), code.dtype)
        out_specs = pl.BlockSpec((per_step, rows, rank), lambda g, pos: (g, 0, 0))
    return pl.pallas_call(
        functools.partial(sketch_kernel, code, apart, per_step),
        out_shape=out_shape,
        grid_spec=pltpu.PrefetchScalarGridSpec(
            num_scalar_prefetch=1,
            grid=(steps,),
            in_specs=[pl.BlockSpec((time_rows, rank), lambda g, pos: (0, 0))]
            + [pl.BlockSpec((time_rows, n), column(u)) for u in range(per_step)],
            out_specs=out_specs,
        ),
        compiler_params=params(),
        cost_estimate=pl.CostEstimate(
            flops=2 * time_rows * n * rank * len(ks),
            bytes_accessed=time_rows * n * 2 * len(ks),
            transcendentals=0,
        ),
    )(pos, scores, *([scans] * per_step))


def small_call(kernel, out_shape, *args):
    return pl.pallas_call(
        kernel,
        out_shape=out_shape,
        in_specs=[WHOLE] * len(args),
        out_specs=jax.tree.map(lambda _: WHOLE, out_shape),
        compiler_params=params(),
    )(*args)


def add_pieces_kernel(code, count, own_ref, got_ref, *outs):
    for k in range(count):
        outs[k][...] = code.encode(code.decode(own_ref[k]) + code.decode(got_ref[k]))


def add_all_kernel(code, with_gram, *refs):
    outs = refs[-2:] if with_gram else refs[-1:]
    parts = refs[: len(refs) - len(outs)]
    total = code.decode(parts[0][...])
    for part in parts[1:]:
        total = total + code.decode(part[...])
    outs[0][...] = code.encode(total)
    if with_gram:
        outs[1][...] = lax.dot_general(
            total, total, (((0,), (0,)), ((), ())), precision=HIGHEST,
            preferred_element_type=F32,
        )


def add_halves_kernel(code, pos_ref, *refs):
    parts, (keep_ref, send_ref) = refs[:-2], refs[-2:]
    total = code.decode(parts[0][...])
    for part in parts[1:]:
        total = total + code.decode(part[...])
    half = total.shape[0] // 2
    lower = pos_ref[0] == 0
    keep_ref[...] = code.encode(jnp.where(lower, total[:half], total[half:]))
    send_ref[...] = code.encode(jnp.where(lower, total[half:], total[:half]))


def add_all(code, with_gram, parts):
    rank = parts[0].shape[1]
    out = [jax.ShapeDtypeStruct(parts[0].shape, code.dtype)]
    if with_gram:
        out.append(jax.ShapeDtypeStruct((rank, rank), F32))
    return small_call(functools.partial(add_all_kernel, code, with_gram), out, *parts)


def project_kernel(has_base, split, items, pos_ref, *refs):
    refs = list(refs)
    base = refs.pop(0) if has_base else None
    outs = [refs.pop() for _ in range(2 if split else 1)][::-1]
    scans, pieces = refs[: len(items)], refs[len(items) :]
    time_rows = scans[0].shape[0]
    rank = outs[0].shape[1]
    total = jnp.zeros((time_rows, rank), F32)
    gram = jnp.zeros((rank, rank), F32)
    for scan, (source, index) in zip(scans, items):
        piece = pieces[source][...] if index is None else pieces[source][index]
        total += jnp.dot(scan[...], piece, preferred_element_type=F32)
        gram += lax.dot_general(
            piece, piece, (((0,), (0,)), ((), ())), preferred_element_type=F32
        )
    if has_base:
        total += base[:time_rows]
        gram += base[time_rows:]
    if not split:
        outs[0][:time_rows] = total
        outs[0][time_rows:] = gram
        return
    both = jnp.concatenate([total, gram])
    half = both.shape[0] // 2
    lower = pos_ref[2] == 0
    outs[0][...] = jnp.where(lower, both[:half], both[half:])
    outs[1][...] = jnp.where(lower, both[half:], both[:half])


def project(scans, layout, pos, groups, base=None, split=False):
    time_rows = scans.shape[0]
    rank = groups[0][2].shape[-1]
    items, names = [], []
    for source, (j, ks, array) in enumerate(groups):
        for i, k in enumerate(ks):
            items.append((source, None if array.ndim == 2 else i))
            names.append((j, k))

    def column(j, k):
        return lambda g, pos: (0, layout.block(j, k, pos))

    full = lambda shape: pl.BlockSpec(shape, lambda g, pos: (0,) * len(shape))
    bases = [] if base is None else [base]
    arrays = [array for _, _, array in groups]
    rows = time_rows + rank
    shape = (rows // 2, rank) if split else (rows, rank)
    out_shape = [jax.ShapeDtypeStruct(shape, F32)] * (2 if split else 1)
    columns = sum(layout.columns(j) for j, _ in names)
    out = pl.pallas_call(
        functools.partial(project_kernel, base is not None, split, items),
        out_shape=out_shape,
        grid_spec=pltpu.PrefetchScalarGridSpec(
            num_scalar_prefetch=1,
            grid=(1,),
            in_specs=[full(b.shape) for b in bases]
            + [pl.BlockSpec((time_rows, layout.columns(j)), column(j, k)) for j, k in names]
            + [full(p.shape) for p in arrays],
            out_specs=[full(shape)] * len(out_shape),
        ),
        compiler_params=params(),
        cost_estimate=pl.CostEstimate(
            flops=2 * rows * columns * rank, bytes_accessed=time_rows * columns * 2,
            transcendentals=0,
        ),
    )(pos, *bases, *([scans] * len(items)), *arrays)
    return out if split else out[0]


def finish_kernel(layout, items, has_base, pos_ref, inverse_ref, *refs):
    refs, (out, held, sems) = refs[:-3], refs[-3:]
    if has_base:
        refs = refs[1:]
    copies = []
    used = 0
    pos = (pos_ref[0], pos_ref[1])
    for number, (source, index, j, k) in enumerate(items):
        n = layout.columns(j)
        codes = refs[source][...] if index is None else refs[source][index]
        if j is None:
            value = jnp.concatenate([Fixed.decode(codes[side]) for side in range(LOW)])
        else:
            value = Fixed.decode(codes)
        rows = pl.ds(used, n)
        held[rows] = times_transpose(value, inverse_ref[...])
        used += n
        start = pl.multiple_of(layout.block(j, k, pos) * n, n)
        copy = pltpu.make_async_copy(held.at[rows], out.at[pl.ds(start, n)], sems.at[number])
        copy.start()
        copies.append(copy)
    for copy in copies:
        copy.wait()


def finish(layout, pos, groups, inverse, voxels, base=None):
    rank = inverse.shape[0]
    items = []
    for source, (j, ks, array) in enumerate(groups):
        alone = array.ndim == (2 if j is not None else 3)
        for i, k in enumerate(ks):
            items.append((source, None if alone else i, j, k))
    columns = sum(layout.columns(j) for _, _, j, _ in items)
    bases = [] if base is None else [base]
    arrays = [array for _, _, array in groups]
    return pl.pallas_call(
        functools.partial(finish_kernel, layout, items, base is not None),
        out_shape=jax.ShapeDtypeStruct((voxels, rank), F32),
        in_specs=[pl.BlockSpec(memory_space=pltpu.SMEM), WHOLE]
        + [pl.BlockSpec(memory_space=pl.ANY)] * len(bases)
        + [WHOLE] * len(arrays),
        out_specs=pl.BlockSpec(memory_space=pl.ANY),
        scratch_shapes=[
            pltpu.VMEM((columns, rank), F32),
            pltpu.SemaphoreType.DMA((len(items),)),
        ],
        input_output_aliases={2: 0} if bases else {},
        compiler_params=params(),
    )(pos, inverse, *bases, *arrays)


def inverse_factor(gram):
    size = gram.shape[0]
    groups = size // GROUP
    shape = (GROUP, size)
    sub = lax.broadcasted_iota(jnp.int32, shape, 0)
    lane = lax.broadcasted_iota(jnp.int32, shape, 1)
    left = [gram[GROUP * i : GROUP * (i + 1)] for i in range(groups)]
    right = [jnp.where(sub + GROUP * i == lane, 1.0, 0.0).astype(F32) for i in range(groups)]
    for g in range(groups):
        first = g * GROUP
        wide = lambda value: jnp.broadcast_to(value, shape)
        rows = [wide(left[g][t : t + 1]) for t in range(GROUP)]
        inverse_rows = [wide(right[g][t : t + 1]) for t in range(GROUP)]
        block = [
            [wide(left[g][t : t + 1, first + u : first + u + 1]) for u in range(GROUP)]
            for t in range(GROUP)
        ]
        below = range(g + 1, groups)
        columns = {
            i: [wide(left[i][:, first + u : first + u + 1]) for u in range(GROUP)] for i in below
        }
        scaled = []
        for t in range(GROUP):
            pivot = 1.0 / block[t][t]
            scaled.append((rows[t] * pivot, inverse_rows[t] * pivot))
            for u in range(t + 1, GROUP):
                factor = block[t][u] * pivot
                for w in range(u, GROUP):
                    block[u][w] = block[u][w] - factor * block[t][w]
                rows[u] = rows[u] - factor * rows[t]
                inverse_rows[u] = inverse_rows[u] - factor * inverse_rows[t]
                for i in below:
                    columns[i][u] = columns[i][u] - factor * columns[i][t]
        for i in below:
            for t in range(GROUP):
                left[i] = left[i] - columns[i][t] * scaled[t][0]
                right[i] = right[i] - columns[i][t] * scaled[t][1]
        for t in range(GROUP):
            left[g] = jnp.where(sub == t, rows[t], left[g])
            right[g] = jnp.where(sub == t, inverse_rows[t], right[g])
    out = []
    for g in range(groups):
        pivots = jnp.sum(
            jnp.where(sub + GROUP * g == lane, left[g], 0.0), axis=1, keepdims=True
        )
        out.append(right[g] * lax.rsqrt(pivots))
    return jnp.concatenate(out)


def times_transpose(value, inverse):
    return lax.dot_general(
        value, inverse, (((1,), (1,)), ((), ())), precision=HIGHEST, preferred_element_type=F32
    )


def normalise_kernel(all_voxels, length_ref, pos_ref, mine_ref, other_ref, out_ref):
    time_rows = out_ref.shape[0]
    mine, other = mine_ref[...], other_ref[...]
    lower = pos_ref[2] == 0
    both = jnp.concatenate([jnp.where(lower, mine, other), jnp.where(lower, other, mine)])
    inverse = inverse_factor(both[time_rows:] * (1.0 / all_voxels))
    scores = times_transpose(both[:time_rows], inverse)
    live = lax.broadcasted_iota(jnp.int32, scores.shape, 0) < length_ref[0]
    out_ref[...] = jnp.where(live, scores, 0.0).astype(BF16)


def invert_kernel(all_voxels, *refs):
    terms = [ref[...] for ref in refs[:-1]]
    while len(terms) > 1:
        terms = [terms[i] + terms[i + 1] for i in range(0, len(terms), 2)]
    refs[-1][...] = inverse_factor(terms[0] * (1.0 / all_voxels))


def make(mesh):
    subjects, blocks = mesh.shape["subj"], mesh.shape["vox"]
    swap = functools.partial(exchange, axis="subj", size=subjects)
    swap_vox = functools.partial(exchange, axis="vox", size=blocks)

    def on_device(scans, test_matrix, lengths, block_subject):
        time_rows, voxels = scans.shape
        rank = test_matrix.shape[1]
        all_voxels = voxels * blocks
        layout = Layout(voxels, subjects)
        high = layout.high
        ks = list(range(high))
        near, far = ks[: high // 2], ks[high // 2 :]
        me = lax.axis_index("subj")
        core = lax.axis_index("vox") % 2
        pos = jnp.stack([me % LOW, me // LOW, core]).astype(jnp.int32)
        slot_ids = jnp.arange(block_subject.shape[0], dtype=jnp.int32)
        subject = jnp.sum(jnp.where(slot_ids == me, block_subject, 0))
        length = jnp.sum(jnp.where(slot_ids == subject, lengths, 0))
        live_rows = (jnp.arange(time_rows, dtype=jnp.int32) < length)[:, None]

        def sketch_sum(scores, code, with_gram):
            def part(after, j, ks, apart, per_step):
                ordered = scores if after is None else lax.optimization_barrier((scores, after))[0]
                return sketch_part(
                    scans, layout, pos, ordered, j, ks, code, apart, per_step
                )

            def add_pieces(home, got, count):
                piece = jax.ShapeDtypeStruct((layout.single + code.pad, rank), code.dtype)
                return small_call(
                    functools.partial(add_pieces_kernel, code, count), [piece] * count, home, got
                )

            away_far = part(None, 1, far, False, 1)
            got_far = swap(away_far, mask=1)
            second = part(away_far, None, ks[1:], True, high - 1)
            got_second = [swap(second[k - 1], mask=k * LOW) for k in ks[1:]]
            away_near = part(second[0], 1, near, False, 1)
            got_near = swap(away_near, mask=1)
            home_far = part(away_near, 0, far, False, 1)
            home_near = part(home_far, 0, near, False, 1)
            (second_own,) = part(home_near, None, ks[:1], True, 1)

            first_far = add_pieces(home_far, got_far, len(far))
            got_first = [swap(first_far[k - far[0]], mask=k * LOW) for k in far]
            got_near, *got_second = lax.optimization_barrier((got_near, *got_second))
            first_near = add_pieces(home_near, got_near, len(near))
            got_first += [swap(first_near[k], mask=k * LOW) for k in near[1:]]

            half = jax.ShapeDtypeStruct((layout.pair // 2 + code.pad, rank), code.dtype)
            keep, send = pl.pallas_call(
                functools.partial(add_halves_kernel, code),
                out_shape=[half, half],
                in_specs=[pl.BlockSpec(memory_space=pltpu.SMEM)] + [WHOLE] * high,
                out_specs=[WHOLE, WHOLE],
                compiler_params=params(),
            )(pos, second_own, *got_second)
            got_send = swap(send, mask=1)
            return (
                add_all(code, with_gram, [first_near[0], *got_first]),
                add_all(code, with_gram, [keep, got_send]),
            )

        def gather(first, second, gram=None):
            far_in = [swap(first, mask=k * LOW) for k in far]
            near_in = [first] + [swap(first, mask=k * LOW) for k in near[1:]]
            low_near = swap(jnp.stack(near_in), mask=1)
            got = swap(second, mask=1)
            lower = pos[0] == 0
            pair = jnp.stack([jnp.where(lower, second, got), jnp.where(lower, got, second)])
            if gram is not None:
                gram = gram + swap_vox(gram, mask=1)
                mask = 2
                while mask < blocks:
                    gram = gram + swap_vox(gram, mask=mask)
                    mask *= 2
                gram = gram + swap(gram, mask=1)
            far_in, pair, gram = lax.optimization_barrier((far_in, pair, gram))
            low_far = swap(jnp.stack(far_in), mask=1)
            seconds = [pair] + [swap(pair, mask=k * LOW) for k in ks[1:]]
            if gram is not None:
                gram = [gram] + [swap(gram, mask=k * LOW) for k in ks[1:]]
            early = [(0, [k], array) for k, array in zip(near + far, near_in + far_in)]
            early.append((1, near, low_near))
            pairs = [(None, [k], array) for k, array in zip(ks, seconds)]
            return early, pairs, (1, far, low_far), gram

        partial = jnp.dot(scans, test_matrix, preferred_element_type=F32)
        summed = sum(butterfly(partial, "vox", blocks))
        scores = jnp.where(live_rows, summed, 0.0).astype(BF16)

        (first,), (second,) = sketch_sum(scores, Plain, False)
        early, pairs, last, _ = gather(first, second)
        pairs = [(j, k, array.reshape(layout.pair, rank)) for j, k, array in pairs]
        both = project(scans, layout, pos, early)
        both = project(scans, layout, pos, pairs, both)
        mine, send = project(scans, layout, pos, [last], both, True)
        mine = mine + swap_vox(send, mask=1)
        mask = 2
        while mask < blocks:
            mine = mine + swap_vox(mine, mask=mask)
            mask *= 2
        other = swap_vox(mine, mask=1)
        scores = pl.pallas_call(
            functools.partial(normalise_kernel, all_voxels),
            out_shape=jax.ShapeDtypeStruct((time_rows, rank), BF16),
            in_specs=[pl.BlockSpec(memory_space=pltpu.SMEM)] * 2 + [WHOLE, WHOLE],
            out_specs=WHOLE,
            compiler_params=params(),
        )(length[None], pos, mine, other)

        (first, gram_first), (second, gram_second) = sketch_sum(scores, Fixed, True)
        early, pairs, last, grams = gather(first, second, gram_first + gram_second)
        inverse = small_call(
            functools.partial(invert_kernel, all_voxels),
            jax.ShapeDtypeStruct((rank, rank), F32), *grams,
        )
        out = finish(layout, pos, early, inverse, voxels)
        return finish(layout, pos, pairs + [last], inverse, voxels, out)

    return on_device


def solution(mesh):
    placed = (P("subj", "vox"), P("vox", None), P(), P())
    return jax.shard_map(
        make(mesh), mesh=mesh, in_specs=placed, out_specs=P("vox", None), check_vma=False
    )
```

```python
import functools

import jax
import jax.numpy as jnp
from jax import lax
from jax.experimental import pallas as pl
from jax.experimental.pallas import tpu as pltpu
from jax.sharding import PartitionSpec as P

F32 = jnp.float32
BF16 = jnp.bfloat16
I16 = jnp.int16
HIGHEST = lax.Precision.HIGHEST
STEPS = 64.0
LOW = 2
GROUP = 8
LANES = 128
VMEM_BYTES = 48 << 20
LIGHT = pl.CostEstimate(flops=1, bytes_accessed=1, transcendentals=0)
WHOLE = pl.BlockSpec(memory_space=pltpu.VMEM)


def exchange(value, axis, size, mask):
    return lax.ppermute(value, axis, [(i, i ^ mask) for i in range(size)])


def butterfly(value, axis, size):
    mask = 1
    while 2 * mask < size:
        value = value + exchange(value, axis, size, mask)
        mask *= 2
    return value, exchange(value, axis, size, mask)


class Plain:
    pad = 0
    dtype = BF16

    @staticmethod
    def encode(value):
        return value.astype(BF16)

    @staticmethod
    def decode(sent):
        return sent.astype(F32)


class Fixed:
    pad = 16
    dtype = I16

    @staticmethod
    def encode(value):
        top = jnp.maximum(jnp.max(jnp.abs(value), axis=0, keepdims=True), 1e-30)
        power = jnp.ceil(jnp.log2(top * (1.0 / 32000.0)) * STEPS)
        codes = jnp.round(value * jnp.exp2(power * (-1.0 / STEPS)))
        codes = jnp.clip(codes, -32767.0, 32767.0)
        rows = jnp.broadcast_to(power, (Fixed.pad, value.shape[1]))
        return jnp.concatenate([codes, rows]).astype(jnp.int32).astype(I16)

    @staticmethod
    def decode(sent):
        wide = sent.astype(jnp.int32).astype(F32)
        rows = wide.shape[0] - Fixed.pad
        return wide[:rows] * jnp.exp2(wide[rows : rows + 1] * (1.0 / STEPS))


def params():
    return pltpu.CompilerParams(vmem_limit_bytes=VMEM_BYTES)


class Layout:
    def __init__(self, voxels, subjects):
        self.high = subjects // LOW
        unit = subjects * LANES
        for top, bottom in ((2, 3), (1, 2)):
            self.cut = voxels * top // bottom
            self.pair = (voxels - self.cut) // self.high
            if self.cut % unit == 0 and voxels % unit == 0 and self.cut % self.pair == 0:
                break
        self.single = self.cut // subjects

    def columns(self, j):
        return self.pair if j is None else self.single

    def block(self, j, k, pos):
        if j is None:
            return self.cut // self.pair + (pos[1] ^ k)
        return (pos[0] ^ j) * self.high + (pos[1] ^ k)


def sketch_kernel(code, apart, count, pos_ref, scores_ref, *refs):
    for u in range(count):
        product = lax.dot_general(
            scores_ref[...], refs[u][...], (((0,), (0,)), ((), ())), preferred_element_type=F32
        )
        out = refs[count + u] if apart else refs[count].at[u]
        out[...] = code.encode(product.T)


def sketch_part(scans, layout, pos, scores, j, ks, code, apart, per_step):
    time_rows = scans.shape[0]
    rank = scores.shape[1]
    n = layout.columns(j)
    rows = n + code.pad
    steps = len(ks) // per_step

    def column(u):
        return lambda g, pos: (0, layout.block(j, ks[0] + g * per_step + u, pos))

    if apart:
        out_shape = [jax.ShapeDtypeStruct((rows, rank), code.dtype)] * len(ks)
        out_specs = [pl.BlockSpec((rows, rank), lambda g, pos: (0, 0))] * len(ks)
    else:
        out_shape = jax.ShapeDtypeStruct((len(ks), rows, rank), code.dtype)
        out_specs = pl.BlockSpec((per_step, rows, rank), lambda g, pos: (g, 0, 0))
    return pl.pallas_call(
        functools.partial(sketch_kernel, code, apart, per_step),
        out_shape=out_shape,
        grid_spec=pltpu.PrefetchScalarGridSpec(
            num_scalar_prefetch=1,
            grid=(steps,),
            in_specs=[pl.BlockSpec((time_rows, rank), lambda g, pos: (0, 0))]
            + [pl.BlockSpec((time_rows, n), column(u)) for u in range(per_step)],
            out_specs=out_specs,
        ),
        compiler_params=params(),
        cost_estimate=LIGHT,
    )(pos, scores, *([scans] * per_step))


def small_call(kernel, out_shape, *args):
    return pl.pallas_call(
        kernel,
        out_shape=out_shape,
        in_specs=[WHOLE] * len(args),
        out_specs=jax.tree.map(lambda _: WHOLE, out_shape),
        compiler_params=params(),
        cost_estimate=LIGHT,
    )(*args)


def add_pieces_kernel(code, count, own_ref, got_ref, *outs):
    for k in range(count):
        outs[k][...] = code.encode(code.decode(own_ref[k]) + code.decode(got_ref[k]))


def add_all_kernel(code, with_gram, *refs):
    outs = refs[-2:] if with_gram else refs[-1:]
    parts = refs[: len(refs) - len(outs)]
    total = code.decode(parts[0][...])
    for part in parts[1:]:
        total = total + code.decode(part[...])
    outs[0][...] = code.encode(total)
    if with_gram:
        outs[1][...] = lax.dot_general(
            total, total, (((0,), (0,)), ((), ())), precision=HIGHEST,
            preferred_element_type=F32,
        )


def add_halves_kernel(code, pos_ref, *refs):
    parts, (keep_ref, send_ref) = refs[:-2], refs[-2:]
    total = code.decode(parts[0][...])
    for part in parts[1:]:
        total = total + code.decode(part[...])
    half = total.shape[0] // 2
    lower = pos_ref[0] == 0
    keep_ref[...] = code.encode(jnp.where(lower, total[:half], total[half:]))
    send_ref[...] = code.encode(jnp.where(lower, total[half:], total[:half]))


def add_all(code, with_gram, parts):
    rank = parts[0].shape[1]
    out = [jax.ShapeDtypeStruct(parts[0].shape, code.dtype)]
    if with_gram:
        out.append(jax.ShapeDtypeStruct((rank, rank), F32))
    return small_call(functools.partial(add_all_kernel, code, with_gram), out, *parts)


def project_kernel(has_base, split, items, pos_ref, *refs):
    refs = list(refs)
    base = refs.pop(0) if has_base else None
    outs = [refs.pop() for _ in range(2 if split else 1)][::-1]
    scans, pieces = refs[: len(items)], refs[len(items) :]
    time_rows = scans[0].shape[0]
    rank = outs[0].shape[1]
    total = jnp.zeros((time_rows, rank), F32)
    gram = jnp.zeros((rank, rank), F32)
    for scan, (source, index) in zip(scans, items):
        piece = pieces[source][...] if index is None else pieces[source][index]
        total += jnp.dot(scan[...], piece, preferred_element_type=F32)
        gram += lax.dot_general(
            piece, piece, (((0,), (0,)), ((), ())), preferred_element_type=F32
        )
    if has_base:
        total += base[:time_rows]
        gram += base[time_rows:]
    if not split:
        outs[0][:time_rows] = total
        outs[0][time_rows:] = gram
        return
    both = jnp.concatenate([total, gram])
    half = both.shape[0] // 2
    lower = pos_ref[2] == 0
    outs[0][...] = jnp.where(lower, both[:half], both[half:])
    outs[1][...] = jnp.where(lower, both[half:], both[:half])


def project(scans, layout, pos, groups, base=None, split=False):
    time_rows = scans.shape[0]
    rank = groups[0][2].shape[-1]
    items, names = [], []
    for source, (j, ks, array) in enumerate(groups):
        for i, k in enumerate(ks):
            items.append((source, None if array.ndim == 2 else i))
            names.append((j, k))

    def column(j, k):
        return lambda g, pos: (0, layout.block(j, k, pos))

    full = lambda shape: pl.BlockSpec(shape, lambda g, pos: (0,) * len(shape))
    bases = [] if base is None else [base]
    arrays = [array for _, _, array in groups]
    rows = time_rows + rank
    shape = (rows // 2, rank) if split else (rows, rank)
    out_shape = [jax.ShapeDtypeStruct(shape, F32)] * (2 if split else 1)
    out = pl.pallas_call(
        functools.partial(project_kernel, base is not None, split, items),
        out_shape=out_shape,
        grid_spec=pltpu.PrefetchScalarGridSpec(
            num_scalar_prefetch=1,
            grid=(1,),
            in_specs=[full(b.shape) for b in bases]
            + [pl.BlockSpec((time_rows, layout.columns(j)), column(j, k)) for j, k in names]
            + [full(p.shape) for p in arrays],
            out_specs=[full(shape)] * len(out_shape),
        ),
        compiler_params=params(),
        cost_estimate=LIGHT,
    )(pos, *bases, *([scans] * len(items)), *arrays)
    return out if split else out[0]


def finish_kernel(layout, items, has_base, pos_ref, inverse_ref, *refs):
    refs, (out, held, sems) = refs[:-3], refs[-3:]
    if has_base:
        refs = refs[1:]
    copies = []
    used = 0
    pos = (pos_ref[0], pos_ref[1])
    for number, (source, index, j, k) in enumerate(items):
        n = layout.columns(j)
        codes = refs[source][...] if index is None else refs[source][index]
        if j is None:
            value = jnp.concatenate([Fixed.decode(codes[side]) for side in range(LOW)])
        else:
            value = Fixed.decode(codes)
        rows = pl.ds(used, n)
        held[rows] = times_transpose(value, inverse_ref[...])
        used += n
        start = pl.multiple_of(layout.block(j, k, pos) * n, n)
        copy = pltpu.make_async_copy(held.at[rows], out.at[pl.ds(start, n)], sems.at[number])
        copy.start()
        copies.append(copy)
    for copy in copies:
        copy.wait()


def finish(layout, pos, groups, inverse, voxels, base=None):
    rank = inverse.shape[0]
    items = []
    for source, (j, ks, array) in enumerate(groups):
        alone = array.ndim == (2 if j is not None else 3)
        for i, k in enumerate(ks):
            items.append((source, None if alone else i, j, k))
    columns = sum(layout.columns(j) for _, _, j, _ in items)
    bases = [] if base is None else [base]
    arrays = [array for _, _, array in groups]
    return pl.pallas_call(
        functools.partial(finish_kernel, layout, items, base is not None),
        out_shape=jax.ShapeDtypeStruct((voxels, rank), F32),
        in_specs=[pl.BlockSpec(memory_space=pltpu.SMEM), WHOLE]
        + [pl.BlockSpec(memory_space=pl.ANY)] * len(bases)
        + [WHOLE] * len(arrays),
        out_specs=pl.BlockSpec(memory_space=pl.ANY),
        scratch_shapes=[
            pltpu.VMEM((columns, rank), F32),
            pltpu.SemaphoreType.DMA((len(items),)),
        ],
        input_output_aliases={2: 0} if bases else {},
        compiler_params=params(),
    )(pos, inverse, *bases, *arrays)


def inverse_factor(gram):
    size = gram.shape[0]
    groups = size // GROUP
    shape = (GROUP, size)
    sub = lax.broadcasted_iota(jnp.int32, shape, 0)
    lane = lax.broadcasted_iota(jnp.int32, shape, 1)
    left = [gram[GROUP * i : GROUP * (i + 1)] for i in range(groups)]
    right = [jnp.where(sub + GROUP * i == lane, 1.0, 0.0).astype(F32) for i in range(groups)]
    for g in range(groups):
        first = g * GROUP
        wide = lambda value: jnp.broadcast_to(value, shape)
        rows = [wide(left[g][t : t + 1]) for t in range(GROUP)]
        inverse_rows = [wide(right[g][t : t + 1]) for t in range(GROUP)]
        block = [
            [wide(left[g][t : t + 1, first + u : first + u + 1]) for u in range(GROUP)]
            for t in range(GROUP)
        ]
        below = range(g + 1, groups)
        columns = {
            i: [wide(left[i][:, first + u : first + u + 1]) for u in range(GROUP)] for i in below
        }
        scaled = []
        for t in range(GROUP):
            pivot = 1.0 / block[t][t]
            scaled.append((rows[t] * pivot, inverse_rows[t] * pivot))
            for u in range(t + 1, GROUP):
                factor = block[t][u] * pivot
                for w in range(u, GROUP):
                    block[u][w] = block[u][w] - factor * block[t][w]
                rows[u] = rows[u] - factor * rows[t]
                inverse_rows[u] = inverse_rows[u] - factor * inverse_rows[t]
                for i in below:
                    columns[i][u] = columns[i][u] - factor * columns[i][t]
        for i in below:
            for t in range(GROUP):
                left[i] = left[i] - columns[i][t] * scaled[t][0]
                right[i] = right[i] - columns[i][t] * scaled[t][1]
        for t in range(GROUP):
            left[g] = jnp.where(sub == t, rows[t], left[g])
            right[g] = jnp.where(sub == t, inverse_rows[t], right[g])
    out = []
    for g in range(groups):
        pivots = jnp.sum(
            jnp.where(sub + GROUP * g == lane, left[g], 0.0), axis=1, keepdims=True
        )
        out.append(right[g] * lax.rsqrt(pivots))
    return jnp.concatenate(out)


def times_transpose(value, inverse):
    return lax.dot_general(
        value, inverse, (((1,), (1,)), ((), ())), precision=HIGHEST, preferred_element_type=F32
    )


def normalise_kernel(all_voxels, length_ref, pos_ref, mine_ref, other_ref, out_ref):
    time_rows = out_ref.shape[0]
    mine, other = mine_ref[...], other_ref[...]
    lower = pos_ref[2] == 0
    both = jnp.concatenate([jnp.where(lower, mine, other), jnp.where(lower, other, mine)])
    inverse = inverse_factor(both[time_rows:] * (1.0 / all_voxels))
    scores = times_transpose(both[:time_rows], inverse)
    live = lax.broadcasted_iota(jnp.int32, scores.shape, 0) < length_ref[0]
    out_ref[...] = jnp.where(live, scores, 0.0).astype(BF16)


def invert_kernel(all_voxels, *refs):
    terms = [ref[...] for ref in refs[:-1]]
    while len(terms) > 1:
        terms = [terms[i] + terms[i + 1] for i in range(0, len(terms), 2)]
    refs[-1][...] = inverse_factor(terms[0] * (1.0 / all_voxels))


def make(mesh):
    subjects, blocks = mesh.shape["subj"], mesh.shape["vox"]
    swap = functools.partial(exchange, axis="subj", size=subjects)
    swap_vox = functools.partial(exchange, axis="vox", size=blocks)

    def on_device(scans, test_matrix, lengths, block_subject):
        time_rows, voxels = scans.shape
        rank = test_matrix.shape[1]
        all_voxels = voxels * blocks
        layout = Layout(voxels, subjects)
        high = layout.high
        ks = list(range(high))
        near, far = ks[: high // 2], ks[high // 2 :]
        me = lax.axis_index("subj")
        core = lax.axis_index("vox") % 2
        pos = jnp.stack([me % LOW, me // LOW, core]).astype(jnp.int32)
        slot_ids = jnp.arange(block_subject.shape[0], dtype=jnp.int32)
        subject = jnp.sum(jnp.where(slot_ids == me, block_subject, 0))
        length = jnp.sum(jnp.where(slot_ids == subject, lengths, 0))
        live_rows = (jnp.arange(time_rows, dtype=jnp.int32) < length)[:, None]

        def sketch_sum(scores, code, with_gram):
            def part(after, j, ks, apart, per_step):
                ordered = scores if after is None else lax.optimization_barrier((scores, after))[0]
                return sketch_part(
                    scans, layout, pos, ordered, j, ks, code, apart, per_step
                )

            away = part(None, 1, ks, False, high // 2)
            got_away = swap(away, mask=1)
            second = part(away, None, ks[1:], True, high - 1)
            got_second = [swap(second[k - 1], mask=k * LOW) for k in ks[1:]]
            home = part(second[0], 0, ks, False, high // 2)
            (second_own,) = part(second[0], None, ks[:1], True, 1)
            got_away, *got_second = lax.optimization_barrier((got_away, *got_second))
            piece = jax.ShapeDtypeStruct((layout.single + code.pad, rank), code.dtype)
            first = small_call(
                functools.partial(add_pieces_kernel, code, high), [piece] * high, home, got_away
            )
            got_first = [swap(first[k], mask=k * LOW) for k in ks[1:]]

            half = jax.ShapeDtypeStruct((layout.pair // 2 + code.pad, rank), code.dtype)
            keep, send = pl.pallas_call(
                functools.partial(add_halves_kernel, code),
                out_shape=[half, half],
                in_specs=[pl.BlockSpec(memory_space=pltpu.SMEM)] + [WHOLE] * high,
                out_specs=[WHOLE, WHOLE],
                compiler_params=params(),
            )(pos, second_own, *got_second)
            got_send = swap(send, mask=1)
            return (
                add_all(code, with_gram, [first[0], *got_first]),
                add_all(code, with_gram, [keep, got_send]),
            )

        def gather(first, second, gram=None):
            far_in = [swap(first, mask=k * LOW) for k in far]
            near_in = [first] + [swap(first, mask=k * LOW) for k in near[1:]]
            low_near = swap(jnp.stack(near_in), mask=1)
            got = swap(second, mask=1)
            lower = pos[0] == 0
            pair = jnp.stack([jnp.where(lower, second, got), jnp.where(lower, got, second)])
            if gram is not None:
                gram = gram + swap_vox(gram, mask=1)
                mask = 2
                while mask < blocks:
                    gram = gram + swap_vox(gram, mask=mask)
                    mask *= 2
                gram = gram + swap(gram, mask=1)
            far_in, pair, gram = lax.optimization_barrier((far_in, pair, gram))
            low_far = swap(jnp.stack(far_in), mask=1)
            seconds = [pair] + [swap(pair, mask=k * LOW) for k in ks[1:]]
            if gram is not None:
                gram = [gram] + [swap(gram, mask=k * LOW) for k in ks[1:]]
            early = [(0, [k], array) for k, array in zip(near + far, near_in + far_in)]
            late = [(1, near, low_near), (1, far, low_far)]
            pairs = [(None, [k], array) for k, array in zip(ks, seconds)]
            return early, late, pairs, gram

        partial = jnp.dot(scans, test_matrix, preferred_element_type=F32)
        summed = sum(butterfly(partial, "vox", blocks))
        scores = jnp.where(live_rows, summed, 0.0).astype(BF16)

        (first,), (second,) = sketch_sum(scores, Plain, False)
        early, late, pairs, _ = gather(first, second)
        pairs = [(j, k, array.reshape(layout.pair, rank)) for j, k, array in pairs]
        both = project(scans, layout, pos, early)
        both = project(scans, layout, pos, late, both)
        both = project(scans, layout, pos, pairs[: high // 2], both)
        mine, send = project(scans, layout, pos, pairs[high // 2 :], both, True)
        mine = mine + swap_vox(send, mask=1)
        mask = 2
        while mask < blocks:
            mine = mine + swap_vox(mine, mask=mask)
            mask *= 2
        other = swap_vox(mine, mask=1)
        scores = pl.pallas_call(
            functools.partial(normalise_kernel, all_voxels),
            out_shape=jax.ShapeDtypeStruct((time_rows, rank), BF16),
            in_specs=[pl.BlockSpec(memory_space=pltpu.SMEM)] * 2 + [WHOLE, WHOLE],
            out_specs=WHOLE,
            compiler_params=params(),
        )(length[None], pos, mine, other)

        (first, gram_first), (second, gram_second) = sketch_sum(scores, Fixed, True)
        early, late, pairs, grams = gather(first, second, gram_first + gram_second)
        inverse = small_call(
            functools.partial(invert_kernel, all_voxels),
            jax.ShapeDtypeStruct((rank, rank), F32), *grams,
        )
        out = finish(layout, pos, early + late, inverse, voxels)
        return finish(layout, pos, pairs, inverse, voxels, out)

    return on_device


def solution(mesh):
    placed = (P("subj", "vox"), P("vox", None), P(), P())
    return jax.shard_map(
        make(mesh), mesh=mesh, in_specs=placed, out_specs=P("vox", None), check_vma=False
    )
```

```python
import functools

import jax
import jax.numpy as jnp
from jax import lax
from jax.experimental import pallas as pl
from jax.experimental.pallas import tpu as pltpu
from jax.sharding import PartitionSpec as P

F32 = jnp.float32
BF16 = jnp.bfloat16
I16 = jnp.int16
HIGHEST = lax.Precision.HIGHEST
STEPS = 64.0
LOW = 2
GROUP = 8
LANES = 128
VMEM_BYTES = 24 << 20
LIGHT = pl.CostEstimate(flops=1, bytes_accessed=1, transcendentals=0)
WHOLE = pl.BlockSpec(memory_space=pltpu.VMEM)


def exchange(value, axis, size, mask):
    return lax.ppermute(value, axis, [(i, i ^ mask) for i in range(size)])


class Plain:
    pad = 0
    dtype = BF16

    @staticmethod
    def encode(value):
        return value.astype(BF16)

    @staticmethod
    def decode(sent):
        return sent.astype(F32)


class Fixed:
    pad = 16
    dtype = I16

    @staticmethod
    def encode(value):
        top = jnp.maximum(jnp.max(jnp.abs(value), axis=0, keepdims=True), 1e-30)
        power = jnp.ceil(jnp.log2(top * (1.0 / 32000.0)) * STEPS)
        codes = jnp.round(value * jnp.exp2(power * (-1.0 / STEPS)))
        codes = jnp.clip(codes, -32767.0, 32767.0)
        rows = jnp.broadcast_to(power, (Fixed.pad, value.shape[1]))
        return jnp.concatenate([codes, rows]).astype(jnp.int32).astype(I16)

    @staticmethod
    def decode(sent):
        wide = sent.astype(jnp.int32).astype(F32)
        rows = wide.shape[0] - Fixed.pad
        return wide[:rows] * jnp.exp2(wide[rows : rows + 1] * (1.0 / STEPS))


def params():
    return pltpu.CompilerParams(vmem_limit_bytes=VMEM_BYTES)


class Layout:
    def __init__(self, voxels, subjects):
        self.high = subjects // LOW
        unit = subjects * LANES
        for top, bottom in ((2, 3), (1, 2)):
            self.cut = voxels * top // bottom
            self.pair = (voxels - self.cut) // self.high
            if self.cut % unit == 0 and voxels % unit == 0 and self.cut % self.pair == 0:
                break
        self.single = self.cut // subjects

    def columns(self, j):
        return self.pair if j is None else self.single

    def block(self, j, k, pos):
        if j is None:
            return self.cut // self.pair + (pos[1] ^ k)
        return (pos[0] ^ j) * self.high + (pos[1] ^ k)


def sketch_kernel(code, apart, count, pos_ref, scores_ref, *refs):
    for u in range(count):
        product = lax.dot_general(
            scores_ref[...], refs[u][...], (((0,), (0,)), ((), ())), preferred_element_type=F32
        )
        out = refs[count + u] if apart else refs[count].at[u]
        out[...] = code.encode(product.T)


def sketch_part(scans, layout, pos, scores, j, ks, code, apart, per_step):
    time_rows = scans.shape[0]
    rank = scores.shape[1]
    n = layout.columns(j)
    rows = n + code.pad
    steps = len(ks) // per_step

    def column(u):
        return lambda g, pos: (0, layout.block(j, ks[0] + g * per_step + u, pos))

    if apart:
        out_shape = [jax.ShapeDtypeStruct((rows, rank), code.dtype)] * len(ks)
        out_specs = [pl.BlockSpec((rows, rank), lambda g, pos: (0, 0))] * len(ks)
    else:
        out_shape = jax.ShapeDtypeStruct((len(ks), rows, rank), code.dtype)
        out_specs = pl.BlockSpec((per_step, rows, rank), lambda g, pos: (g, 0, 0))
    return pl.pallas_call(
        functools.partial(sketch_kernel, code, apart, per_step),
        out_shape=out_shape,
        grid_spec=pltpu.PrefetchScalarGridSpec(
            num_scalar_prefetch=1,
            grid=(steps,),
            in_specs=[pl.BlockSpec((time_rows, rank), lambda g, pos: (0, 0))]
            + [pl.BlockSpec((time_rows, n), column(u)) for u in range(per_step)],
            out_specs=out_specs,
        ),
        compiler_params=params(),
        cost_estimate=LIGHT,
    )(pos, scores, *([scans] * per_step))


def small_call(kernel, out_shape, *args):
    return pl.pallas_call(
        kernel,
        out_shape=out_shape,
        in_specs=[WHOLE] * len(args),
        out_specs=jax.tree.map(lambda _: WHOLE, out_shape),
        compiler_params=params(),
        cost_estimate=LIGHT,
    )(*args)


def add_pieces_kernel(code, count, own_ref, got_ref, *outs):
    for k in range(count):
        outs[k][...] = code.encode(code.decode(own_ref[k]) + code.decode(got_ref[k]))


def add_all_kernel(code, *refs):
    parts, outs = refs[:-2], refs[-2:]
    total = code.decode(parts[0][...])
    for part in parts[1:]:
        total = total + code.decode(part[...])
    outs[0][...] = code.encode(total)
    outs[1][...] = lax.dot_general(
        total, total, (((0,), (0,)), ((), ())), precision=HIGHEST, preferred_element_type=F32
    )


def add_halves_kernel(code, pos_ref, *refs):
    parts, (keep_ref, send_ref) = refs[:-2], refs[-2:]
    total = code.decode(parts[0][...])
    for part in parts[1:]:
        total = total + code.decode(part[...])
    half = total.shape[0] // 2
    lower = pos_ref[0] == 0
    keep_ref[...] = code.encode(jnp.where(lower, total[:half], total[half:]))
    send_ref[...] = code.encode(jnp.where(lower, total[half:], total[:half]))


def add_all(code, parts):
    rank = parts[0].shape[1]
    out = [jax.ShapeDtypeStruct(parts[0].shape, code.dtype)]
    out.append(jax.ShapeDtypeStruct((rank, rank), F32))
    return small_call(functools.partial(add_all_kernel, code), out, *parts)


def write_halves(pos_ref, value, outs):
    half = value.shape[0] // 2
    lower = pos_ref[2] == 0
    outs[0][...] = jnp.where(lower, value[:half], value[half:])
    outs[1][...] = jnp.where(lower, value[half:], value[:half])


def first_kernel(count, pos_ref, panel_ref, *refs):
    scans, outs, total = refs[:count], refs[count:-1], refs[-1]
    n = scans[0].shape[1]
    g = pl.program_id(0)

    @pl.when(g == 0)
    def _():
        total[...] = jnp.zeros_like(total)

    for u in range(count):
        panel = panel_ref[u * n : (u + 1) * n]
        total[...] += jnp.dot(scans[u][...], panel, preferred_element_type=F32)

    @pl.when(g == pl.num_programs(0) - 1)
    def _():
        write_halves(pos_ref, total[...], outs)


def first_project(scans, pos, panel, steps=3, count=4):
    time_rows, voxels = scans.shape
    rank = panel.shape[1]
    n = voxels // (steps * count)
    half = jax.ShapeDtypeStruct((time_rows // 2, rank), F32)

    def column(u):
        return lambda g, pos: (0, g * count + u)

    return pl.pallas_call(
        functools.partial(first_kernel, count),
        out_shape=[half, half],
        grid_spec=pltpu.PrefetchScalarGridSpec(
            num_scalar_prefetch=1,
            grid=(steps,),
            in_specs=[pl.BlockSpec((count * n, rank), lambda g, pos: (g, 0))]
            + [pl.BlockSpec((time_rows, n), column(u)) for u in range(count)],
            out_specs=[pl.BlockSpec(half.shape, lambda g, pos: (0, 0))] * 2,
            scratch_shapes=[pltpu.VMEM((time_rows, rank), F32)],
        ),
        compiler_params=params(),
        cost_estimate=LIGHT,
    )(pos, panel, *([scans] * count))


def project_kernel(has_base, split, items, pos_ref, *refs):
    refs = list(refs)
    base = refs.pop(0) if has_base else None
    outs = [refs.pop() for _ in range(2 if split else 1)][::-1]
    scans, pieces = refs[: len(items)], refs[len(items) :]
    time_rows = scans[0].shape[0]
    rank = outs[0].shape[1]
    total = jnp.zeros((time_rows, rank), F32)
    for scan, (source, index) in zip(scans, items):
        piece = pieces[source][...] if index is None else pieces[source][index]
        total += jnp.dot(scan[...], piece, preferred_element_type=F32)
    if has_base:
        total += base[...]
    if split:
        write_halves(pos_ref, total, outs)
    else:
        outs[0][...] = total


def project(scans, layout, pos, groups, base=None, split=False):
    time_rows = scans.shape[0]
    rank = groups[0][2].shape[-1]
    items, names = [], []
    for source, (j, ks, array) in enumerate(groups):
        for i, k in enumerate(ks):
            items.append((source, None if array.ndim == 2 else i))
            names.append((j, k))

    def column(j, k):
        return lambda g, pos: (0, layout.block(j, k, pos))

    full = lambda shape: pl.BlockSpec(shape, lambda g, pos: (0,) * len(shape))
    bases = [] if base is None else [base]
    arrays = [array for _, _, array in groups]
    shape = (time_rows // 2, rank) if split else (time_rows, rank)
    out_shape = [jax.ShapeDtypeStruct(shape, F32)] * (2 if split else 1)
    out = pl.pallas_call(
        functools.partial(project_kernel, base is not None, split, items),
        out_shape=out_shape,
        grid_spec=pltpu.PrefetchScalarGridSpec(
            num_scalar_prefetch=1,
            grid=(1,),
            in_specs=[full(b.shape) for b in bases]
            + [pl.BlockSpec((time_rows, layout.columns(j)), column(j, k)) for j, k in names]
            + [full(p.shape) for p in arrays],
            out_specs=[full(shape)] * len(out_shape),
        ),
        compiler_params=params(),
        cost_estimate=LIGHT,
    )(pos, *bases, *([scans] * len(items)), *arrays)
    return out if split else out[0]


def finish_kernel(layout, items, has_base, pos_ref, inverse_ref, *refs):
    refs, (out, held, sems) = refs[:-3], refs[-3:]
    if has_base:
        refs = refs[1:]
    copies = []
    used = 0
    pos = (pos_ref[0], pos_ref[1])
    for number, (source, index, j, k) in enumerate(items):
        n = layout.columns(j)
        codes = refs[source][...] if index is None else refs[source][index]
        if j is None:
            value = jnp.concatenate([Fixed.decode(codes[side]) for side in range(LOW)])
        else:
            value = Fixed.decode(codes)
        rows = pl.ds(used, n)
        held[rows] = times_transpose(value, inverse_ref[...])
        used += n
        start = pl.multiple_of(layout.block(j, k, pos) * n, n)
        copy = pltpu.make_async_copy(held.at[rows], out.at[pl.ds(start, n)], sems.at[number])
        copy.start()
        copies.append(copy)
    for copy in copies:
        copy.wait()


def finish(layout, pos, groups, inverse, voxels, base=None):
    rank = inverse.shape[0]
    items = []
    for source, (j, ks, array) in enumerate(groups):
        alone = array.ndim == (2 if j is not None else 3)
        for i, k in enumerate(ks):
            items.append((source, None if alone else i, j, k))
    columns = sum(layout.columns(j) for _, _, j, _ in items)
    bases = [] if base is None else [base]
    arrays = [array for _, _, array in groups]
    return pl.pallas_call(
        functools.partial(finish_kernel, layout, items, base is not None),
        out_shape=jax.ShapeDtypeStruct((voxels, rank), F32),
        in_specs=[pl.BlockSpec(memory_space=pltpu.SMEM), WHOLE]
        + [pl.BlockSpec(memory_space=pl.ANY)] * len(bases)
        + [WHOLE] * len(arrays),
        out_specs=pl.BlockSpec(memory_space=pl.ANY),
        scratch_shapes=[
            pltpu.VMEM((columns, rank), F32),
            pltpu.SemaphoreType.DMA((len(items),)),
        ],
        input_output_aliases={2: 0} if bases else {},
        compiler_params=params(),
    )(pos, inverse, *bases, *arrays)


def inverse_factor(gram):
    size = gram.shape[0]
    groups = size // GROUP
    shape = (GROUP, size)
    sub = lax.broadcasted_iota(jnp.int32, shape, 0)
    lane = lax.broadcasted_iota(jnp.int32, shape, 1)
    left = [gram[GROUP * i : GROUP * (i + 1)] for i in range(groups)]
    right = [jnp.where(sub + GROUP * i == lane, 1.0, 0.0).astype(F32) for i in range(groups)]
    for g in range(groups):
        first = g * GROUP
        wide = lambda value: jnp.broadcast_to(value, shape)
        rows = [wide(left[g][t : t + 1]) for t in range(GROUP)]
        inverse_rows = [wide(right[g][t : t + 1]) for t in range(GROUP)]
        block = [
            [wide(left[g][t : t + 1, first + u : first + u + 1]) for u in range(GROUP)]
            for t in range(GROUP)
        ]
        below = range(g + 1, groups)
        columns = {
            i: [wide(left[i][:, first + u : first + u + 1]) for u in range(GROUP)] for i in below
        }
        scaled = []
        for t in range(GROUP):
            pivot = 1.0 / block[t][t]
            scaled.append((rows[t] * pivot, inverse_rows[t] * pivot))
            for u in range(t + 1, GROUP):
                factor = block[t][u] * pivot
                for w in range(u, GROUP):
                    block[u][w] = block[u][w] - factor * block[t][w]
                rows[u] = rows[u] - factor * rows[t]
                inverse_rows[u] = inverse_rows[u] - factor * inverse_rows[t]
                for i in below:
                    columns[i][u] = columns[i][u] - factor * columns[i][t]
        for i in below:
            for t in range(GROUP):
                left[i] = left[i] - columns[i][t] * scaled[t][0]
                right[i] = right[i] - columns[i][t] * scaled[t][1]
        for t in range(GROUP):
            left[g] = jnp.where(sub == t, rows[t], left[g])
            right[g] = jnp.where(sub == t, inverse_rows[t], right[g])
    out = []
    for g in range(groups):
        pivots = jnp.sum(
            jnp.where(sub + GROUP * g == lane, left[g], 0.0), axis=1, keepdims=True
        )
        out.append(right[g] * lax.rsqrt(pivots))
    return jnp.concatenate(out)


def times_transpose(value, inverse):
    return lax.dot_general(
        value, inverse, (((1,), (1,)), ((), ())), precision=HIGHEST, preferred_element_type=F32
    )


def scores_kernel(with_factor, length_ref, pos_ref, mine_ref, other_ref, *refs):
    out_ref = refs[-1]
    mine, other = mine_ref[...], other_ref[...]
    lower = pos_ref[2] == 0
    scores = jnp.concatenate([jnp.where(lower, mine, other), jnp.where(lower, other, mine)])
    if with_factor:
        scores = times_transpose(scores, refs[0][...])
    live = lax.broadcasted_iota(jnp.int32, scores.shape, 0) < length_ref[0]
    out_ref[...] = jnp.where(live, scores, 0.0).astype(BF16)


def invert_kernel(all_voxels, *refs):
    terms = [ref[...] for ref in refs[:-1]]
    while len(terms) > 1:
        terms = [terms[i] + terms[i + 1] for i in range(0, len(terms), 2)]
    refs[-1][...] = inverse_factor(terms[0] * (1.0 / all_voxels))


def make(mesh):
    subjects, blocks = mesh.shape["subj"], mesh.shape["vox"]
    swap = functools.partial(exchange, axis="subj", size=subjects)
    swap_vox = functools.partial(exchange, axis="vox", size=blocks)

    def on_device(scans, test_matrix, lengths, block_subject):
        time_rows, voxels = scans.shape
        rank = test_matrix.shape[1]
        all_voxels = voxels * blocks
        layout = Layout(voxels, subjects)
        high = layout.high
        ks = list(range(high))
        near, far = ks[: high // 2], ks[high // 2 :]
        me = lax.axis_index("subj")
        core = lax.axis_index("vox") % 2
        pos = jnp.stack([me % LOW, me // LOW, core]).astype(jnp.int32)
        slot_ids = jnp.arange(block_subject.shape[0], dtype=jnp.int32)
        subject = jnp.sum(jnp.where(slot_ids == me, block_subject, 0))
        length = jnp.sum(jnp.where(slot_ids == subject, lengths, 0))

        def sketch_sum(scores, code):
            def part(after, j, ks, apart, per_step):
                ordered = scores if after is None else lax.optimization_barrier((scores, after))[0]
                return sketch_part(
                    scans, layout, pos, ordered, j, ks, code, apart, per_step
                )

            away = part(None, 1, ks, False, high // 2)
            got_away = swap(away, mask=1)
            second = part(away, None, ks[1:], True, high - 1)
            got_second = [swap(second[k - 1], mask=k * LOW) for k in ks[1:]]
            home = part(second[0], 0, ks, False, high // 2)
            (second_own,) = part(second[0], None, ks[:1], True, 1)
            got_away, *got_second = lax.optimization_barrier((got_away, *got_second))
            piece = jax.ShapeDtypeStruct((layout.single + code.pad, rank), code.dtype)
            first = small_call(
                functools.partial(add_pieces_kernel, code, high), [piece] * high, home, got_away
            )
            got_first = [swap(first[k], mask=k * LOW) for k in ks[1:]]

            half = jax.ShapeDtypeStruct((layout.pair // 2 + code.pad, rank), code.dtype)
            keep, send = pl.pallas_call(
                functools.partial(add_halves_kernel, code),
                out_shape=[half, half],
                in_specs=[pl.BlockSpec(memory_space=pltpu.SMEM)] + [WHOLE] * high,
                out_specs=[WHOLE, WHOLE],
                compiler_params=params(),
            )(pos, second_own, *got_second)
            got_send = swap(send, mask=1)
            return (
                add_all(code, [first[0], *got_first]),
                add_all(code, [keep, got_send]),
            )

        def gather(first, second, gram):
            far_in = [swap(first, mask=k * LOW) for k in far]
            near_in = [first] + [swap(first, mask=k * LOW) for k in near[1:]]
            low_near = swap(jnp.stack(near_in), mask=1)
            got = swap(second, mask=1)
            lower = pos[0] == 0
            pair = jnp.stack([jnp.where(lower, second, got), jnp.where(lower, got, second)])
            mask = 1
            while mask < blocks:
                gram = gram + swap_vox(gram, mask=mask)
                mask *= 2
            gram = gram + swap(gram, mask=1)
            far_in, pair, gram = lax.optimization_barrier((far_in, pair, gram))
            low_far = swap(jnp.stack(far_in), mask=1)
            seconds = [pair] + [swap(pair, mask=k * LOW) for k in ks[1:]]
            gram = [gram] + [swap(gram, mask=k * LOW) for k in ks[1:]]
            early = [(0, [k], array) for k, array in zip(near + far, near_in + far_in)]
            late = [(1, near, low_near), (1, far, low_far)]
            pairs = [(None, [k], array) for k, array in zip(ks, seconds)]
            return early, late, pairs, gram

        def sum_scores(mine, send, *factor):
            mine = mine + swap_vox(send, mask=1)
            mask = 2
            while mask < blocks:
                mine = mine + swap_vox(mine, mask=mask)
                mask *= 2
            other = swap_vox(mine, mask=1)
            return pl.pallas_call(
                functools.partial(scores_kernel, bool(factor)),
                out_shape=jax.ShapeDtypeStruct((time_rows, rank), BF16),
                in_specs=[pl.BlockSpec(memory_space=pltpu.SMEM)] * 2
                + [WHOLE] * (2 + len(factor)),
                out_specs=WHOLE,
                compiler_params=params(),
                cost_estimate=LIGHT,
            )(length[None], pos, mine, other, *factor)

        def pass_over(scores, code):
            (first, gram_first), (second, gram_second) = sketch_sum(scores, code)
            early, late, pairs, grams = gather(first, second, gram_first + gram_second)
            inverse = small_call(
                functools.partial(invert_kernel, all_voxels),
                jax.ShapeDtypeStruct((rank, rank), F32), *grams,
            )
            return early, late, pairs, inverse

        scores = sum_scores(*first_project(scans, pos, test_matrix))
        early, late, pairs, inverse = pass_over(scores, Plain)
        pairs = [(j, k, array.reshape(layout.pair, rank)) for j, k, array in pairs]
        total = project(scans, layout, pos, early)
        total = project(scans, layout, pos, late, total)
        total = project(scans, layout, pos, pairs[: high // 2], total)
        halves = project(scans, layout, pos, pairs[high // 2 :], total, True)
        scores = sum_scores(*halves, inverse)
        early, late, pairs, inverse = pass_over(scores, Fixed)
        out = finish(layout, pos, early + late, inverse, voxels)
        return finish(layout, pos, pairs, inverse, voxels, out)

    return on_device


def solution(mesh):
    placed = (P("subj", "vox"), P("vox", None), P(), P())
    return jax.shard_map(
        make(mesh), mesh=mesh, in_specs=placed, out_specs=P("vox", None), check_vma=False
    )
```

```python
import functools

import jax
import jax.numpy as jnp
from jax import lax
from jax.experimental import pallas as pl
from jax.experimental.pallas import tpu as pltpu
from jax.sharding import PartitionSpec as P

F32 = jnp.float32
BF16 = jnp.bfloat16
I16 = jnp.int16
HIGHEST = lax.Precision.HIGHEST
STEPS = 64.0
LOW = 2
GROUP = 8
LANES = 128
VMEM_BYTES = 20 << 20
VMEM_FIRST = 56 << 20
LIGHT = pl.CostEstimate(flops=1, bytes_accessed=1, transcendentals=0)
WHOLE = pl.BlockSpec(memory_space=pltpu.VMEM)


def exchange(value, axis, size, mask):
    return lax.ppermute(value, axis, [(i, i ^ mask) for i in range(size)])


class Plain:
    pad = 0
    dtype = BF16

    @staticmethod
    def encode(value):
        return value.astype(BF16)

    @staticmethod
    def decode(sent):
        return sent.astype(F32)


class Fixed:
    pad = 16
    dtype = I16

    @staticmethod
    def encode(value):
        top = jnp.maximum(jnp.max(jnp.abs(value), axis=0, keepdims=True), 1e-30)
        power = jnp.ceil(jnp.log2(top * (1.0 / 32000.0)) * STEPS)
        codes = jnp.round(value * jnp.exp2(power * (-1.0 / STEPS)))
        codes = jnp.clip(codes, -32767.0, 32767.0)
        rows = jnp.broadcast_to(power, (Fixed.pad, value.shape[1]))
        return jnp.concatenate([codes, rows]).astype(jnp.int32).astype(I16)

    @staticmethod
    def decode(sent):
        wide = sent.astype(jnp.int32).astype(F32)
        rows = wide.shape[0] - Fixed.pad
        return wide[:rows] * jnp.exp2(wide[rows : rows + 1] * (1.0 / STEPS))


def params(limit=VMEM_BYTES):
    return pltpu.CompilerParams(vmem_limit_bytes=limit)


class Layout:
    def __init__(self, voxels, subjects):
        self.high = subjects // LOW
        unit = subjects * LANES
        for top, bottom in ((2, 3), (1, 2)):
            self.cut = voxels * top // bottom
            self.pair = (voxels - self.cut) // self.high
            if self.cut % unit == 0 and voxels % unit == 0 and self.cut % self.pair == 0:
                break
        self.single = self.cut // subjects

    def columns(self, j):
        return self.pair if j is None else self.single

    def block(self, j, k, pos):
        if j is None:
            return self.cut // self.pair + (pos[1] ^ k)
        return (pos[0] ^ j) * self.high + (pos[1] ^ k)


def sketch_kernel(code, apart, count, pos_ref, scores_ref, *refs):
    for u in range(count):
        product = lax.dot_general(
            scores_ref[...], refs[u][...], (((0,), (0,)), ((), ())), preferred_element_type=F32
        )
        out = refs[count + u] if apart else refs[count].at[u]
        out[...] = code.encode(product.T)


def sketch_part(scans, layout, pos, scores, j, ks, code, apart, per_step):
    time_rows = scans.shape[0]
    rank = scores.shape[1]
    n = layout.columns(j)
    rows = n + code.pad
    steps = len(ks) // per_step

    def column(u):
        return lambda g, pos: (0, layout.block(j, ks[0] + g * per_step + u, pos))

    if apart:
        out_shape = [jax.ShapeDtypeStruct((rows, rank), code.dtype)] * len(ks)
        out_specs = [pl.BlockSpec((rows, rank), lambda g, pos: (0, 0))] * len(ks)
    else:
        out_shape = jax.ShapeDtypeStruct((len(ks), rows, rank), code.dtype)
        out_specs = pl.BlockSpec((per_step, rows, rank), lambda g, pos: (g, 0, 0))
    return pl.pallas_call(
        functools.partial(sketch_kernel, code, apart, per_step),
        out_shape=out_shape,
        grid_spec=pltpu.PrefetchScalarGridSpec(
            num_scalar_prefetch=1,
            grid=(steps,),
            in_specs=[pl.BlockSpec((time_rows, rank), lambda g, pos: (0, 0))]
            + [pl.BlockSpec((time_rows, n), column(u)) for u in range(per_step)],
            out_specs=out_specs,
        ),
        compiler_params=params(),
        cost_estimate=LIGHT,
    )(pos, scores, *([scans] * per_step))


def small_call(kernel, out_shape, *args):
    return pl.pallas_call(
        kernel,
        out_shape=out_shape,
        in_specs=[WHOLE] * len(args),
        out_specs=jax.tree.map(lambda _: WHOLE, out_shape),
        compiler_params=params(),
        cost_estimate=LIGHT,
    )(*args)


def add_pieces_kernel(code, count, own_ref, got_ref, *outs):
    for k in range(count):
        outs[k][...] = code.encode(code.decode(own_ref[k]) + code.decode(got_ref[k]))


def add_all_kernel(code, *refs):
    parts, outs = refs[:-2], refs[-2:]
    total = code.decode(parts[0][...])
    for part in parts[1:]:
        total = total + code.decode(part[...])
    outs[0][...] = code.encode(total)
    outs[1][...] = lax.dot_general(
        total, total, (((0,), (0,)), ((), ())), precision=HIGHEST, preferred_element_type=F32
    )


def add_halves_kernel(code, pos_ref, *refs):
    parts, (keep_ref, send_ref) = refs[:-2], refs[-2:]
    total = code.decode(parts[0][...])
    for part in parts[1:]:
        total = total + code.decode(part[...])
    half = total.shape[0] // 2
    lower = pos_ref[0] == 0
    keep_ref[...] = code.encode(jnp.where(lower, total[:half], total[half:]))
    send_ref[...] = code.encode(jnp.where(lower, total[half:], total[:half]))


def add_all(code, parts):
    rank = parts[0].shape[1]
    out = [jax.ShapeDtypeStruct(parts[0].shape, code.dtype)]
    out.append(jax.ShapeDtypeStruct((rank, rank), F32))
    return small_call(functools.partial(add_all_kernel, code), out, *parts)


def write_halves(pos_ref, value, outs):
    half = value.shape[0] // 2
    lower = pos_ref[2] == 0
    outs[0][...] = jnp.where(lower, value[:half], value[half:])
    outs[1][...] = jnp.where(lower, value[half:], value[:half])


def first_kernel(count, pos_ref, panel_ref, *refs):
    scans, outs, total = refs[:count], refs[count:-1], refs[-1]
    n = scans[0].shape[1]
    g = pl.program_id(0)

    @pl.when(g == 0)
    def _():
        total[...] = jnp.zeros_like(total)

    for u in range(count):
        panel = panel_ref[u * n : (u + 1) * n]
        total[...] += jnp.dot(scans[u][...], panel, preferred_element_type=F32)

    @pl.when(g == pl.num_programs(0) - 1)
    def _():
        write_halves(pos_ref, total[...], outs)


def first_project(scans, pos, panel, steps=3, count=4):
    time_rows, voxels = scans.shape
    rank = panel.shape[1]
    n = voxels // (steps * count)
    half = jax.ShapeDtypeStruct((time_rows // 2, rank), F32)

    def column(u):
        return lambda g, pos: (0, g * count + u)

    return pl.pallas_call(
        functools.partial(first_kernel, count),
        out_shape=[half, half],
        grid_spec=pltpu.PrefetchScalarGridSpec(
            num_scalar_prefetch=1,
            grid=(steps,),
            in_specs=[pl.BlockSpec((count * n, rank), lambda g, pos: (g, 0))]
            + [pl.BlockSpec((time_rows, n), column(u)) for u in range(count)],
            out_specs=[pl.BlockSpec(half.shape, lambda g, pos: (0, 0))] * 2,
            scratch_shapes=[pltpu.VMEM((time_rows, rank), F32)],
        ),
        compiler_params=params(VMEM_FIRST),
        cost_estimate=LIGHT,
    )(pos, panel, *([scans] * count))


def project_kernel(has_base, split, items, pos_ref, *refs):
    refs = list(refs)
    base = refs.pop(0) if has_base else None
    outs = [refs.pop() for _ in range(2 if split else 1)][::-1]
    scans, pieces = refs[: len(items)], refs[len(items) :]
    time_rows = scans[0].shape[0]
    rank = outs[0].shape[1]
    total = jnp.zeros((time_rows, rank), F32)
    for scan, (source, index) in zip(scans, items):
        piece = pieces[source][...] if index is None else pieces[source][index]
        total += jnp.dot(scan[...], piece, preferred_element_type=F32)
    if has_base:
        total += base[...]
    if split:
        write_halves(pos_ref, total, outs)
    else:
        outs[0][...] = total


def project(scans, layout, pos, groups, base=None, split=False):
    time_rows = scans.shape[0]
    rank = groups[0][2].shape[-1]
    items, names = [], []
    for source, (j, ks, array) in enumerate(groups):
        for i, k in enumerate(ks):
            items.append((source, None if array.ndim == 2 else i))
            names.append((j, k))

    def column(j, k):
        return lambda g, pos: (0, layout.block(j, k, pos))

    full = lambda shape: pl.BlockSpec(shape, lambda g, pos: (0,) * len(shape))
    bases = [] if base is None else [base]
    arrays = [array for _, _, array in groups]
    shape = (time_rows // 2, rank) if split else (time_rows, rank)
    out_shape = [jax.ShapeDtypeStruct(shape, F32)] * (2 if split else 1)
    out = pl.pallas_call(
        functools.partial(project_kernel, base is not None, split, items),
        out_shape=out_shape,
        grid_spec=pltpu.PrefetchScalarGridSpec(
            num_scalar_prefetch=1,
            grid=(1,),
            in_specs=[full(b.shape) for b in bases]
            + [pl.BlockSpec((time_rows, layout.columns(j)), column(j, k)) for j, k in names]
            + [full(p.shape) for p in arrays],
            out_specs=[full(shape)] * len(out_shape),
        ),
        compiler_params=params(),
        cost_estimate=LIGHT,
    )(pos, *bases, *([scans] * len(items)), *arrays)
    return out if split else out[0]


def finish_kernel(layout, items, has_base, pos_ref, inverse_ref, *refs):
    refs, (out, held, sems) = refs[:-3], refs[-3:]
    if has_base:
        refs = refs[1:]
    copies = []
    used = 0
    pos = (pos_ref[0], pos_ref[1])
    for number, (source, index, j, k) in enumerate(items):
        n = layout.columns(j)
        codes = refs[source][...] if index is None else refs[source][index]
        if j is None:
            value = jnp.concatenate([Fixed.decode(codes[side]) for side in range(LOW)])
        else:
            value = Fixed.decode(codes)
        rows = pl.ds(used, n)
        held[rows] = times_transpose(value, inverse_ref[...])
        used += n
        start = pl.multiple_of(layout.block(j, k, pos) * n, n)
        copy = pltpu.make_async_copy(held.at[rows], out.at[pl.ds(start, n)], sems.at[number])
        copy.start()
        copies.append(copy)
    for copy in copies:
        copy.wait()


def finish(layout, pos, groups, inverse, voxels, base=None):
    rank = inverse.shape[0]
    items = []
    for source, (j, ks, array) in enumerate(groups):
        alone = array.ndim == (2 if j is not None else 3)
        for i, k in enumerate(ks):
            items.append((source, None if alone else i, j, k))
    columns = sum(layout.columns(j) for _, _, j, _ in items)
    bases = [] if base is None else [base]
    arrays = [array for _, _, array in groups]
    return pl.pallas_call(
        functools.partial(finish_kernel, layout, items, base is not None),
        out_shape=jax.ShapeDtypeStruct((voxels, rank), F32),
        in_specs=[pl.BlockSpec(memory_space=pltpu.SMEM), WHOLE]
        + [pl.BlockSpec(memory_space=pl.ANY)] * len(bases)
        + [WHOLE] * len(arrays),
        out_specs=pl.BlockSpec(memory_space=pl.ANY),
        scratch_shapes=[
            pltpu.VMEM((columns, rank), F32),
            pltpu.SemaphoreType.DMA((len(items),)),
        ],
        input_output_aliases={2: 0} if bases else {},
        compiler_params=params(),
    )(pos, inverse, *bases, *arrays)


def inverse_factor(gram):
    size = gram.shape[0]
    groups = size // GROUP
    shape = (GROUP, size)
    sub = lax.broadcasted_iota(jnp.int32, shape, 0)
    lane = lax.broadcasted_iota(jnp.int32, shape, 1)
    left = [gram[GROUP * i : GROUP * (i + 1)] for i in range(groups)]
    right = [jnp.where(sub + GROUP * i == lane, 1.0, 0.0).astype(F32) for i in range(groups)]
    for g in range(groups):
        first = g * GROUP
        wide = lambda value: jnp.broadcast_to(value, shape)
        rows = [wide(left[g][t : t + 1]) for t in range(GROUP)]
        inverse_rows = [wide(right[g][t : t + 1]) for t in range(GROUP)]
        block = [
            [wide(left[g][t : t + 1, first + u : first + u + 1]) for u in range(GROUP)]
            for t in range(GROUP)
        ]
        below = range(g + 1, groups)
        columns = {
            i: [wide(left[i][:, first + u : first + u + 1]) for u in range(GROUP)] for i in below
        }
        scaled = []
        for t in range(GROUP):
            pivot = 1.0 / block[t][t]
            scaled.append((rows[t] * pivot, inverse_rows[t] * pivot))
            for u in range(t + 1, GROUP):
                factor = block[t][u] * pivot
                for w in range(u, GROUP):
                    block[u][w] = block[u][w] - factor * block[t][w]
                rows[u] = rows[u] - factor * rows[t]
                inverse_rows[u] = inverse_rows[u] - factor * inverse_rows[t]
                for i in below:
                    columns[i][u] = columns[i][u] - factor * columns[i][t]
        for i in below:
            for t in range(GROUP):
                left[i] = left[i] - columns[i][t] * scaled[t][0]
                right[i] = right[i] - columns[i][t] * scaled[t][1]
        for t in range(GROUP):
            left[g] = jnp.where(sub == t, rows[t], left[g])
            right[g] = jnp.where(sub == t, inverse_rows[t], right[g])
    out = []
    for g in range(groups):
        pivots = jnp.sum(
            jnp.where(sub + GROUP * g == lane, left[g], 0.0), axis=1, keepdims=True
        )
        out.append(right[g] * lax.rsqrt(pivots))
    return jnp.concatenate(out)


def times_transpose(value, inverse):
    return lax.dot_general(
        value, inverse, (((1,), (1,)), ((), ())), precision=HIGHEST, preferred_element_type=F32
    )


def scores_kernel(with_factor, lengths_ref, subjects_ref, pos_ref, mine_ref, other_ref, *refs):
    out_ref = refs[-1]
    length = lengths_ref[subjects_ref[pos_ref[1] * LOW + pos_ref[0]]]
    mine, other = mine_ref[...], other_ref[...]
    lower = pos_ref[2] == 0
    scores = jnp.concatenate([jnp.where(lower, mine, other), jnp.where(lower, other, mine)])
    if with_factor:
        scores = times_transpose(scores, refs[0][...])
    live = lax.broadcasted_iota(jnp.int32, scores.shape, 0) < length
    out_ref[...] = jnp.where(live, scores, 0.0).astype(BF16)


def invert_kernel(all_voxels, *refs):
    terms = [ref[...] for ref in refs[:-1]]
    while len(terms) > 1:
        terms = [terms[i] + terms[i + 1] for i in range(0, len(terms), 2)]
    refs[-1][...] = inverse_factor(terms[0] * (1.0 / all_voxels))


def make(mesh):
    subjects, blocks = mesh.shape["subj"], mesh.shape["vox"]
    swap = functools.partial(exchange, axis="subj", size=subjects)
    swap_vox = functools.partial(exchange, axis="vox", size=blocks)

    def on_device(scans, test_matrix, lengths, block_subject):
        time_rows, voxels = scans.shape
        rank = test_matrix.shape[1]
        all_voxels = voxels * blocks
        layout = Layout(voxels, subjects)
        high = layout.high
        ks = list(range(high))
        near, far = ks[: high // 2], ks[high // 2 :]
        me = lax.axis_index("subj")
        core = lax.axis_index("vox") % 2
        pos = jnp.stack([me % LOW, me // LOW, core]).astype(jnp.int32)

        def sketch_sum(scores, code):
            def part(after, j, ks, apart, per_step):
                ordered = scores if after is None else lax.optimization_barrier((scores, after))[0]
                return sketch_part(
                    scans, layout, pos, ordered, j, ks, code, apart, per_step
                )

            away = part(None, 1, ks, False, high // 2)
            got_away = swap(away, mask=1)
            second = part(away, None, ks[1:], True, high - 1)
            got_second = [swap(second[k - 1], mask=k * LOW) for k in ks[1:]]
            home = part(second[0], 0, ks, False, high // 2)
            (second_own,) = part(second[0], None, ks[:1], True, 1)
            got_away, *got_second = lax.optimization_barrier((got_away, *got_second))
            piece = jax.ShapeDtypeStruct((layout.single + code.pad, rank), code.dtype)
            first = small_call(
                functools.partial(add_pieces_kernel, code, high), [piece] * high, home, got_away
            )
            got_first = [swap(first[k], mask=k * LOW) for k in ks[1:]]

            half = jax.ShapeDtypeStruct((layout.pair // 2 + code.pad, rank), code.dtype)
            keep, send = pl.pallas_call(
                functools.partial(add_halves_kernel, code),
                out_shape=[half, half],
                in_specs=[pl.BlockSpec(memory_space=pltpu.SMEM)] + [WHOLE] * high,
                out_specs=[WHOLE, WHOLE],
                compiler_params=params(),
            )(pos, second_own, *got_second)
            got_send = swap(send, mask=1)
            return (
                add_all(code, [first[0], *got_first]),
                add_all(code, [keep, got_send]),
            )

        def gather(first, second, gram):
            far_in = [swap(first, mask=k * LOW) for k in far]
            near_in = [first] + [swap(first, mask=k * LOW) for k in near[1:]]
            got = swap(second, mask=1)
            lower = pos[0] == 0
            pair = jnp.stack([jnp.where(lower, second, got), jnp.where(lower, got, second)])
            mask = 1
            while mask < blocks:
                gram = gram + swap_vox(gram, mask=mask)
                mask *= 2
            near_in, gram = lax.optimization_barrier((near_in, gram))
            low_near = swap(jnp.stack(near_in), mask=1)
            gram = gram + swap(gram, mask=1)
            far_in, pair, gram = lax.optimization_barrier((far_in, pair, gram))
            low_far = swap(jnp.stack(far_in), mask=1)
            seconds = [pair] + [swap(pair, mask=k * LOW) for k in ks[1:]]
            gram = [gram] + [swap(gram, mask=k * LOW) for k in ks[1:]]
            early = [(0, [k], array) for k, array in zip(near + far, near_in + far_in)]
            late = [(1, near, low_near), (1, far, low_far)]
            pairs = [(None, [k], array) for k, array in zip(ks, seconds)]
            return early, late, pairs, gram

        def sum_scores(mine, send, *factor):
            mine = mine + swap_vox(send, mask=1)
            mask = 2
            while mask < blocks:
                mine = mine + swap_vox(mine, mask=mask)
                mask *= 2
            other = swap_vox(mine, mask=1)
            return pl.pallas_call(
                functools.partial(scores_kernel, bool(factor)),
                out_shape=jax.ShapeDtypeStruct((time_rows, rank), BF16),
                in_specs=[pl.BlockSpec(memory_space=pltpu.SMEM)] * 3
                + [WHOLE] * (2 + len(factor)),
                out_specs=WHOLE,
                compiler_params=params(),
                cost_estimate=LIGHT,
            )(lengths, block_subject, pos, mine, other, *factor)

        def pass_over(scores, code):
            (first, gram_first), (second, gram_second) = sketch_sum(scores, code)
            early, late, pairs, grams = gather(first, second, gram_first + gram_second)
            inverse = small_call(
                functools.partial(invert_kernel, all_voxels),
                jax.ShapeDtypeStruct((rank, rank), F32), *grams,
            )
            return early, late, pairs, inverse

        scores = sum_scores(*first_project(scans, pos, test_matrix))
        early, late, pairs, inverse = pass_over(scores, Plain)
        pairs = [(j, k, array.reshape(layout.pair, rank)) for j, k, array in pairs]
        total = project(scans, layout, pos, early)
        total = project(scans, layout, pos, late, total)
        total = project(scans, layout, pos, pairs[: high // 2], total)
        total, inverse = lax.optimization_barrier((total, inverse))
        halves = project(scans, layout, pos, pairs[high // 2 :], total, True)
        scores = sum_scores(*halves, inverse)
        early, late, pairs, inverse = pass_over(scores, Fixed)
        out = finish(layout, pos, early + late, inverse, voxels)
        return finish(layout, pos, pairs, inverse, voxels, out)

    return on_device


def solution(mesh):
    placed = (P("subj", "vox"), P("vox", None), P(), P())
    return jax.shard_map(
        make(mesh), mesh=mesh, in_specs=placed, out_specs=P("vox", None), check_vma=False
    )
```

```python
import functools

import jax
import jax.numpy as jnp
from jax import lax
from jax.experimental import pallas as pl
from jax.experimental.pallas import tpu as pltpu
from jax.sharding import PartitionSpec as P

F32 = jnp.float32
BF16 = jnp.bfloat16
I16 = jnp.int16
HIGHEST = lax.Precision.HIGHEST
STEPS = 64.0
LOW = 2
GROUP = 8
LANES = 128
VMEM_BYTES = 48 << 20
LIGHT = pl.CostEstimate(flops=1, bytes_accessed=1, transcendentals=0)
WHOLE = pl.BlockSpec(memory_space=pltpu.VMEM)


def exchange(value, axis, size, mask):
    return lax.ppermute(value, axis, [(i, i ^ mask) for i in range(size)])


class Plain:
    pad = 0
    dtype = BF16

    @staticmethod
    def encode(value):
        return value.astype(BF16)

    @staticmethod
    def decode(sent):
        return sent.astype(F32)


class Fixed:
    pad = 16
    dtype = I16

    @staticmethod
    def encode(value):
        top = jnp.maximum(jnp.max(jnp.abs(value), axis=0, keepdims=True), 1e-30)
        power = jnp.ceil(jnp.log2(top * (1.0 / 32000.0)) * STEPS)
        codes = jnp.round(value * jnp.exp2(power * (-1.0 / STEPS)))
        codes = jnp.clip(codes, -32767.0, 32767.0)
        rows = jnp.broadcast_to(power, (Fixed.pad, value.shape[1]))
        return jnp.concatenate([codes, rows]).astype(jnp.int32).astype(I16)

    @staticmethod
    def decode(sent):
        wide = sent.astype(jnp.int32).astype(F32)
        rows = wide.shape[0] - Fixed.pad
        return wide[:rows] * jnp.exp2(wide[rows : rows + 1] * (1.0 / STEPS))


def params():
    return pltpu.CompilerParams(vmem_limit_bytes=VMEM_BYTES)


class Layout:
    def __init__(self, voxels, subjects):
        self.high = subjects // LOW
        unit = subjects * LANES
        for top, bottom in ((2, 3), (1, 2)):
            self.cut = voxels * top // bottom
            self.pair = (voxels - self.cut) // self.high
            if self.cut % unit == 0 and voxels % unit == 0 and self.cut % self.pair == 0:
                break
        self.single = self.cut // subjects

    def columns(self, j):
        return self.pair if j is None else self.single

    def block(self, j, k, pos):
        if j is None:
            return self.cut // self.pair + (pos[1] ^ k)
        return (pos[0] ^ j) * self.high + (pos[1] ^ k)


def sketch_kernel(code, apart, count, pos_ref, scores_ref, *refs):
    for u in range(count):
        product = lax.dot_general(
            scores_ref[...], refs[u][...], (((0,), (0,)), ((), ())), preferred_element_type=F32
        )
        out = refs[count + u] if apart else refs[count].at[u]
        out[...] = code.encode(product.T)


def sketch_part(scans, layout, pos, scores, j, ks, code, apart, per_step):
    time_rows = scans.shape[0]
    rank = scores.shape[1]
    n = layout.columns(j)
    rows = n + code.pad
    steps = len(ks) // per_step

    def column(u):
        return lambda g, pos: (0, layout.block(j, ks[0] + g * per_step + u, pos))

    if apart:
        out_shape = [jax.ShapeDtypeStruct((rows, rank), code.dtype)] * len(ks)
        out_specs = [pl.BlockSpec((rows, rank), lambda g, pos: (0, 0))] * len(ks)
    else:
        out_shape = jax.ShapeDtypeStruct((len(ks), rows, rank), code.dtype)
        out_specs = pl.BlockSpec((per_step, rows, rank), lambda g, pos: (g, 0, 0))
    return pl.pallas_call(
        functools.partial(sketch_kernel, code, apart, per_step),
        out_shape=out_shape,
        grid_spec=pltpu.PrefetchScalarGridSpec(
            num_scalar_prefetch=1,
            grid=(steps,),
            in_specs=[pl.BlockSpec((time_rows, rank), lambda g, pos: (0, 0))]
            + [pl.BlockSpec((time_rows, n), column(u)) for u in range(per_step)],
            out_specs=out_specs,
        ),
        compiler_params=params(),
        cost_estimate=LIGHT,
    )(pos, scores, *([scans] * per_step))


def small_call(kernel, out_shape, *args):
    return pl.pallas_call(
        kernel,
        out_shape=out_shape,
        in_specs=[WHOLE] * len(args),
        out_specs=jax.tree.map(lambda _: WHOLE, out_shape),
        compiler_params=params(),
        cost_estimate=LIGHT,
    )(*args)


def add_pieces_kernel(code, count, own_ref, got_ref, *outs):
    for k in range(count):
        outs[k][...] = code.encode(code.decode(own_ref[k]) + code.decode(got_ref[k]))


def add_all_kernel(code, *refs):
    parts, outs = refs[:-2], refs[-2:]
    total = code.decode(parts[0][...])
    for part in parts[1:]:
        total = total + code.decode(part[...])
    outs[0][...] = code.encode(total)
    outs[1][...] = lax.dot_general(
        total, total, (((0,), (0,)), ((), ())), precision=HIGHEST, preferred_element_type=F32
    )


def add_halves_kernel(code, pos_ref, *refs):
    parts, (keep_ref, send_ref) = refs[:-2], refs[-2:]
    total = code.decode(parts[0][...])
    for part in parts[1:]:
        total = total + code.decode(part[...])
    half = total.shape[0] // 2
    lower = pos_ref[0] == 0
    keep_ref[...] = code.encode(jnp.where(lower, total[:half], total[half:]))
    send_ref[...] = code.encode(jnp.where(lower, total[half:], total[:half]))


def add_all(code, parts):
    rank = parts[0].shape[1]
    out = [jax.ShapeDtypeStruct(parts[0].shape, code.dtype)]
    out.append(jax.ShapeDtypeStruct((rank, rank), F32))
    return small_call(functools.partial(add_all_kernel, code), out, *parts)


def write_halves(pos_ref, value, outs):
    half = value.shape[0] // 2
    lower = pos_ref[2] == 0
    outs[0][...] = jnp.where(lower, value[:half], value[half:])
    outs[1][...] = jnp.where(lower, value[half:], value[:half])


def first_kernel(count, pos_ref, panel_ref, *refs):
    scans, outs, total = refs[:count], refs[count:-1], refs[-1]
    n = scans[0].shape[1]
    g = pl.program_id(0)

    @pl.when(g == 0)
    def _():
        total[...] = jnp.zeros_like(total)

    for u in range(count):
        panel = panel_ref[u * n : (u + 1) * n]
        total[...] += jnp.dot(scans[u][...], panel, preferred_element_type=F32)

    @pl.when(g == pl.num_programs(0) - 1)
    def _():
        write_halves(pos_ref, total[...], outs)


def first_project(scans, pos, panel, steps=3, count=4):
    time_rows, voxels = scans.shape
    rank = panel.shape[1]
    n = voxels // (steps * count)
    half = jax.ShapeDtypeStruct((time_rows // 2, rank), F32)

    def column(u):
        return lambda g, pos: (0, g * count + u)

    return pl.pallas_call(
        functools.partial(first_kernel, count),
        out_shape=[half, half],
        grid_spec=pltpu.PrefetchScalarGridSpec(
            num_scalar_prefetch=1,
            grid=(steps,),
            in_specs=[pl.BlockSpec((count * n, rank), lambda g, pos: (g, 0))]
            + [pl.BlockSpec((time_rows, n), column(u)) for u in range(count)],
            out_specs=[pl.BlockSpec(half.shape, lambda g, pos: (0, 0))] * 2,
            scratch_shapes=[pltpu.VMEM((time_rows, rank), F32)],
        ),
        compiler_params=params(),
        cost_estimate=LIGHT,
    )(pos, panel, *([scans] * count))


def project_kernel(has_base, split, items, pos_ref, *refs):
    refs = list(refs)
    base = refs.pop(0) if has_base else None
    outs = [refs.pop() for _ in range(2 if split else 1)][::-1]
    scans, pieces = refs[: len(items)], refs[len(items) :]
    time_rows = scans[0].shape[0]
    rank = outs[0].shape[1]
    total = jnp.zeros((time_rows, rank), F32)
    for scan, (source, index) in zip(scans, items):
        piece = pieces[source][...] if index is None else pieces[source][index]
        total += jnp.dot(scan[...], piece, preferred_element_type=F32)
    if has_base:
        total += base[...]
    if split:
        write_halves(pos_ref, total, outs)
    else:
        outs[0][...] = total


def project(scans, layout, pos, groups, base=None, split=False):
    time_rows = scans.shape[0]
    rank = groups[0][2].shape[-1]
    items, names = [], []
    for source, (j, ks, array) in enumerate(groups):
        for i, k in enumerate(ks):
            items.append((source, None if array.ndim == 2 else i))
            names.append((j, k))

    def column(j, k):
        return lambda g, pos: (0, layout.block(j, k, pos))

    full = lambda shape: pl.BlockSpec(shape, lambda g, pos: (0,) * len(shape))
    bases = [] if base is None else [base]
    arrays = [array for _, _, array in groups]
    shape = (time_rows // 2, rank) if split else (time_rows, rank)
    out_shape = [jax.ShapeDtypeStruct(shape, F32)] * (2 if split else 1)
    out = pl.pallas_call(
        functools.partial(project_kernel, base is not None, split, items),
        out_shape=out_shape,
        grid_spec=pltpu.PrefetchScalarGridSpec(
            num_scalar_prefetch=1,
            grid=(1,),
            in_specs=[full(b.shape) for b in bases]
            + [pl.BlockSpec((time_rows, layout.columns(j)), column(j, k)) for j, k in names]
            + [full(p.shape) for p in arrays],
            out_specs=[full(shape)] * len(out_shape),
        ),
        compiler_params=params(),
        cost_estimate=LIGHT,
    )(pos, *bases, *([scans] * len(items)), *arrays)
    return out if split else out[0]


def finish_kernel(layout, items, has_base, pos_ref, inverse_ref, *refs):
    refs, (out, held, sems) = refs[:-3], refs[-3:]
    if has_base:
        refs = refs[1:]
    copies = []
    used = 0
    pos = (pos_ref[0], pos_ref[1])
    for number, (source, index, j, k) in enumerate(items):
        n = layout.columns(j)
        codes = refs[source][...] if index is None else refs[source][index]
        if j is None:
            value = jnp.concatenate([Fixed.decode(codes[side]) for side in range(LOW)])
        else:
            value = Fixed.decode(codes)
        rows = pl.ds(used, n)
        held[rows] = times_transpose(value, inverse_ref[...])
        used += n
        start = pl.multiple_of(layout.block(j, k, pos) * n, n)
        copy = pltpu.make_async_copy(held.at[rows], out.at[pl.ds(start, n)], sems.at[number])
        copy.start()
        copies.append(copy)
    for copy in copies:
        copy.wait()


def finish(layout, pos, groups, inverse, voxels, base=None):
    rank = inverse.shape[0]
    items = []
    for source, (j, ks, array) in enumerate(groups):
        alone = array.ndim == (2 if j is not None else 3)
        for i, k in enumerate(ks):
            items.append((source, None if alone else i, j, k))
    columns = sum(layout.columns(j) for _, _, j, _ in items)
    bases = [] if base is None else [base]
    arrays = [array for _, _, array in groups]
    return pl.pallas_call(
        functools.partial(finish_kernel, layout, items, base is not None),
        out_shape=jax.ShapeDtypeStruct((voxels, rank), F32),
        in_specs=[pl.BlockSpec(memory_space=pltpu.SMEM), WHOLE]
        + [pl.BlockSpec(memory_space=pl.ANY)] * len(bases)
        + [WHOLE] * len(arrays),
        out_specs=pl.BlockSpec(memory_space=pl.ANY),
        scratch_shapes=[
            pltpu.VMEM((columns, rank), F32),
            pltpu.SemaphoreType.DMA((len(items),)),
        ],
        input_output_aliases={2: 0} if bases else {},
        compiler_params=params(),
        cost_estimate=LIGHT,
    )(pos, inverse, *bases, *arrays)


def inverse_factor(gram):
    size = gram.shape[0]
    groups = size // GROUP
    shape = (GROUP, size)
    sub = lax.broadcasted_iota(jnp.int32, shape, 0)
    lane = lax.broadcasted_iota(jnp.int32, shape, 1)
    left = [gram[GROUP * i : GROUP * (i + 1)] for i in range(groups)]
    right = [jnp.where(sub + GROUP * i == lane, 1.0, 0.0).astype(F32) for i in range(groups)]
    for g in range(groups):
        first = g * GROUP
        wide = lambda value: jnp.broadcast_to(value, shape)
        rows = [wide(left[g][t : t + 1]) for t in range(GROUP)]
        inverse_rows = [wide(right[g][t : t + 1]) for t in range(GROUP)]
        block = [
            [wide(left[g][t : t + 1, first + u : first + u + 1]) for u in range(GROUP)]
            for t in range(GROUP)
        ]
        below = range(g + 1, groups)
        columns = {
            i: [wide(left[i][:, first + u : first + u + 1]) for u in range(GROUP)] for i in below
        }
        scaled = []
        for t in range(GROUP):
            pivot = 1.0 / block[t][t]
            scaled.append((rows[t] * pivot, inverse_rows[t] * pivot))
            for u in range(t + 1, GROUP):
                factor = block[t][u] * pivot
                for w in range(u, GROUP):
                    block[u][w] = block[u][w] - factor * block[t][w]
                rows[u] = rows[u] - factor * rows[t]
                inverse_rows[u] = inverse_rows[u] - factor * inverse_rows[t]
                for i in below:
                    columns[i][u] = columns[i][u] - factor * columns[i][t]
        for i in below:
            for t in range(GROUP):
                left[i] = left[i] - columns[i][t] * scaled[t][0]
                right[i] = right[i] - columns[i][t] * scaled[t][1]
        for t in range(GROUP):
            left[g] = jnp.where(sub == t, rows[t], left[g])
            right[g] = jnp.where(sub == t, inverse_rows[t], right[g])
    out = []
    for g in range(groups):
        pivots = jnp.sum(
            jnp.where(sub + GROUP * g == lane, left[g], 0.0), axis=1, keepdims=True
        )
        out.append(right[g] * lax.rsqrt(pivots))
    return jnp.concatenate(out)


def times_transpose(value, inverse):
    return lax.dot_general(
        value, inverse, (((1,), (1,)), ((), ())), precision=HIGHEST, preferred_element_type=F32
    )


def scores_kernel(with_factor, lengths_ref, subjects_ref, pos_ref, mine_ref, other_ref, *refs):
    out_ref = refs[-1]
    length = lengths_ref[subjects_ref[pos_ref[1] * LOW + pos_ref[0]]]
    mine, other = mine_ref[...], other_ref[...]
    lower = pos_ref[2] == 0
    scores = jnp.concatenate([jnp.where(lower, mine, other), jnp.where(lower, other, mine)])
    if with_factor:
        scores = times_transpose(scores, refs[0][...])
    live = lax.broadcasted_iota(jnp.int32, scores.shape, 0) < length
    out_ref[...] = jnp.where(live, scores, 0.0).astype(BF16)


def invert_kernel(all_voxels, *refs):
    terms = [ref[...] for ref in refs[:-1]]
    while len(terms) > 1:
        terms = [terms[i] + terms[i + 1] for i in range(0, len(terms), 2)]
    refs[-1][...] = inverse_factor(terms[0] * (1.0 / all_voxels))


def make(mesh):
    subjects, blocks = mesh.shape["subj"], mesh.shape["vox"]
    swap = functools.partial(exchange, axis="subj", size=subjects)
    swap_vox = functools.partial(exchange, axis="vox", size=blocks)

    def on_device(scans, test_matrix, lengths, block_subject):
        time_rows, voxels = scans.shape
        rank = test_matrix.shape[1]
        all_voxels = voxels * blocks
        layout = Layout(voxels, subjects)
        high = layout.high
        ks = list(range(high))
        near, far = ks[: high // 2], ks[high // 2 :]
        me = lax.axis_index("subj")
        core = lax.axis_index("vox") % 2
        pos = jnp.stack([me % LOW, me // LOW, core]).astype(jnp.int32)

        def sketch_sum(scores, code):
            def part(after, j, ks, apart, per_step):
                ordered = scores if after is None else lax.optimization_barrier((scores, after))[0]
                return sketch_part(
                    scans, layout, pos, ordered, j, ks, code, apart, per_step
                )

            away = part(None, 1, ks, False, high // 2)
            got_away = swap(away, mask=1)
            second = part(away, None, ks[1:], True, high - 1)
            got_second = [swap(second[k - 1], mask=k * LOW) for k in ks[1:]]
            home = part(second[0], 0, ks, False, high // 2)
            (second_own,) = part(second[0], None, ks[:1], True, 1)
            got_away, got_second, home, second_own = lax.optimization_barrier(
                (got_away, got_second, home, second_own)
            )
            piece = jax.ShapeDtypeStruct((layout.single + code.pad, rank), code.dtype)
            first = small_call(
                functools.partial(add_pieces_kernel, code, high), [piece] * high, home, got_away
            )
            got_first = [swap(first[k], mask=k * LOW) for k in ks[1:]]

            half = jax.ShapeDtypeStruct((layout.pair // 2 + code.pad, rank), code.dtype)
            keep, send = pl.pallas_call(
                functools.partial(add_halves_kernel, code),
                out_shape=[half, half],
                in_specs=[pl.BlockSpec(memory_space=pltpu.SMEM)] + [WHOLE] * high,
                out_specs=[WHOLE, WHOLE],
                compiler_params=params(),
                cost_estimate=LIGHT,
            )(pos, second_own, *got_second)
            got_send = swap(send, mask=1)
            return (
                add_all(code, [first[0], *got_first]),
                add_all(code, [keep, got_send]),
            )

        def gather(first, second, gram):
            gram = gram + swap_vox(gram, mask=1)
            first, second, gram = lax.optimization_barrier((first, second, gram))
            far_in = [swap(first, mask=k * LOW) for k in far]
            near_in = [first] + [swap(first, mask=k * LOW) for k in near[1:]]
            got = swap(second, mask=1)
            lower = pos[0] == 0
            pair = jnp.stack([jnp.where(lower, second, got), jnp.where(lower, got, second)])
            mask = 2
            while mask < blocks:
                gram = gram + swap_vox(gram, mask=mask)
                mask *= 2
            near_in, gram = lax.optimization_barrier((near_in, gram))
            low_near = swap(jnp.stack(near_in), mask=1)
            gram = gram + swap(gram, mask=1)
            far_in, pair, gram = lax.optimization_barrier((far_in, pair, gram))
            low_far = swap(jnp.stack(far_in), mask=1)
            seconds = [pair] + [swap(pair, mask=k * LOW) for k in ks[1:]]
            gram = [gram] + [swap(gram, mask=k * LOW) for k in ks[1:]]
            early = [(0, [k], array) for k, array in zip(near + far, near_in + far_in)]
            late = [(1, near, low_near), (1, far, low_far)]
            pairs = [(None, [k], array) for k, array in zip(ks, seconds)]
            return early, late, pairs, gram

        def sum_scores(mine, send, *factor):
            mine = mine + swap_vox(send, mask=1)
            mask = 2
            while mask < blocks:
                mine = mine + swap_vox(mine, mask=mask)
                mask *= 2
            other = swap_vox(mine, mask=1)
            return pl.pallas_call(
                functools.partial(scores_kernel, bool(factor)),
                out_shape=jax.ShapeDtypeStruct((time_rows, rank), BF16),
                in_specs=[pl.BlockSpec(memory_space=pltpu.SMEM)] * 3
                + [WHOLE] * (2 + len(factor)),
                out_specs=WHOLE,
                compiler_params=params(),
                cost_estimate=LIGHT,
            )(lengths, block_subject, pos, mine, other, *factor)

        def pass_over(scores, code):
            (first, gram_first), (second, gram_second) = sketch_sum(scores, code)
            early, late, pairs, grams = gather(first, second, gram_first + gram_second)
            inverse = small_call(
                functools.partial(invert_kernel, all_voxels),
                jax.ShapeDtypeStruct((rank, rank), F32), *grams,
            )
            return early, late, pairs, inverse

        scores = sum_scores(*first_project(scans, pos, test_matrix))
        early, late, pairs, inverse = pass_over(scores, Plain)
        pairs = [(j, k, array.reshape(layout.pair, rank)) for j, k, array in pairs]
        total = project(scans, layout, pos, early)
        total = project(scans, layout, pos, late, total)
        total = project(scans, layout, pos, pairs[: high // 2], total)
        total, inverse = lax.optimization_barrier((total, inverse))
        halves = project(scans, layout, pos, pairs[high // 2 :], total, True)
        scores = sum_scores(*halves, inverse)
        early, late, pairs, inverse = pass_over(scores, Fixed)
        out = finish(layout, pos, early + late, inverse, voxels)
        return finish(layout, pos, pairs, inverse, voxels, out)

    return on_device


def solution(mesh):
    placed = (P("subj", "vox"), P("vox", None), P(), P())
    return jax.shard_map(
        make(mesh), mesh=mesh, in_specs=placed, out_specs=P("vox", None), check_vma=False
    )
```

```python
import functools

import jax
import jax.numpy as jnp
from jax import lax
from jax.experimental import pallas as pl
from jax.experimental.pallas import tpu as pltpu
from jax.sharding import PartitionSpec as P

F32 = jnp.float32
BF16 = jnp.bfloat16
I16 = jnp.int16
HIGHEST = lax.Precision.HIGHEST
STEPS = 64.0
LOW = 2
GROUP = 8
LANES = 128
VMEM_BYTES = 20 << 20
VMEM_FIRST = 48 << 20
LIGHT = pl.CostEstimate(flops=1, bytes_accessed=1, transcendentals=0)
WHOLE = pl.BlockSpec(memory_space=pltpu.VMEM)


def exchange(value, axis, size, mask):
    return lax.ppermute(value, axis, [(i, i ^ mask) for i in range(size)])


class Plain:
    pad = 0
    dtype = BF16
    limit = VMEM_FIRST

    @staticmethod
    def encode(value):
        return value.astype(BF16)

    @staticmethod
    def decode(sent):
        return sent.astype(F32)


class Fixed:
    pad = 16
    dtype = I16
    limit = VMEM_BYTES

    @staticmethod
    def encode(value):
        top = jnp.maximum(jnp.max(jnp.abs(value), axis=0, keepdims=True), 1e-30)
        power = jnp.ceil(jnp.log2(top * (1.0 / 32000.0)) * STEPS)
        codes = jnp.round(value * jnp.exp2(power * (-1.0 / STEPS)))
        codes = jnp.clip(codes, -32767.0, 32767.0)
        rows = jnp.broadcast_to(power, (Fixed.pad, value.shape[1]))
        return jnp.concatenate([codes, rows]).astype(jnp.int32).astype(I16)

    @staticmethod
    def decode(sent):
        wide = sent.astype(jnp.int32).astype(F32)
        rows = wide.shape[0] - Fixed.pad
        return wide[:rows] * jnp.exp2(wide[rows : rows + 1] * (1.0 / STEPS))


def params(limit=VMEM_BYTES):
    return pltpu.CompilerParams(vmem_limit_bytes=limit)


class Layout:
    def __init__(self, voxels, subjects):
        self.high = subjects // LOW
        unit = subjects * LANES
        for top, bottom in ((2, 3), (1, 2)):
            self.cut = voxels * top // bottom
            self.pair = (voxels - self.cut) // self.high
            if self.cut % unit == 0 and voxels % unit == 0 and self.cut % self.pair == 0:
                break
        self.single = self.cut // subjects

    def columns(self, j):
        return self.pair if j is None else self.single

    def block(self, j, k, pos):
        if j is None:
            return self.cut // self.pair + (pos[1] ^ k)
        return (pos[0] ^ j) * self.high + (pos[1] ^ k)


def sketch_kernel(code, apart, count, pos_ref, scores_ref, *refs):
    for u in range(count):
        product = lax.dot_general(
            scores_ref[...], refs[u][...], (((0,), (0,)), ((), ())), preferred_element_type=F32
        )
        out = refs[count + u] if apart else refs[count].at[u]
        out[...] = code.encode(product.T)


def sketch_part(scans, layout, pos, scores, j, ks, code, apart, per_step):
    time_rows = scans.shape[0]
    rank = scores.shape[1]
    n = layout.columns(j)
    rows = n + code.pad
    steps = len(ks) // per_step

    def column(u):
        return lambda g, pos: (0, layout.block(j, ks[0] + g * per_step + u, pos))

    if apart:
        out_shape = [jax.ShapeDtypeStruct((rows, rank), code.dtype)] * len(ks)
        out_specs = [pl.BlockSpec((rows, rank), lambda g, pos: (0, 0))] * len(ks)
    else:
        out_shape = jax.ShapeDtypeStruct((len(ks), rows, rank), code.dtype)
        out_specs = pl.BlockSpec((per_step, rows, rank), lambda g, pos: (g, 0, 0))
    return pl.pallas_call(
        functools.partial(sketch_kernel, code, apart, per_step),
        out_shape=out_shape,
        grid_spec=pltpu.PrefetchScalarGridSpec(
            num_scalar_prefetch=1,
            grid=(steps,),
            in_specs=[pl.BlockSpec((time_rows, rank), lambda g, pos: (0, 0))]
            + [pl.BlockSpec((time_rows, n), column(u)) for u in range(per_step)],
            out_specs=out_specs,
        ),
        compiler_params=params(code.limit),
        cost_estimate=LIGHT,
    )(pos, scores, *([scans] * per_step))


def small_call(kernel, out_shape, *args):
    return pl.pallas_call(
        kernel,
        out_shape=out_shape,
        in_specs=[WHOLE] * len(args),
        out_specs=jax.tree.map(lambda _: WHOLE, out_shape),
        compiler_params=params(),
        cost_estimate=LIGHT,
    )(*args)


def add_pieces_kernel(code, count, own_ref, got_ref, *outs):
    for k in range(count):
        outs[k][...] = code.encode(code.decode(own_ref[k]) + code.decode(got_ref[k]))


def add_all_kernel(code, *refs):
    parts, outs = refs[:-2], refs[-2:]
    total = code.decode(parts[0][...])
    for part in parts[1:]:
        total = total + code.decode(part[...])
    outs[0][...] = code.encode(total)
    outs[1][...] = lax.dot_general(
        total, total, (((0,), (0,)), ((), ())), precision=HIGHEST, preferred_element_type=F32
    )


def add_halves_kernel(code, pos_ref, *refs):
    parts, (keep_ref, send_ref) = refs[:-2], refs[-2:]
    total = code.decode(parts[0][...])
    for part in parts[1:]:
        total = total + code.decode(part[...])
    half = total.shape[0] // 2
    lower = pos_ref[0] == 0
    keep_ref[...] = code.encode(jnp.where(lower, total[:half], total[half:]))
    send_ref[...] = code.encode(jnp.where(lower, total[half:], total[:half]))


def add_all(code, parts):
    rank = parts[0].shape[1]
    out = [jax.ShapeDtypeStruct(parts[0].shape, code.dtype)]
    out.append(jax.ShapeDtypeStruct((rank, rank), F32))
    return small_call(functools.partial(add_all_kernel, code), out, *parts)


def write_halves(pos_ref, value, outs):
    half = value.shape[0] // 2
    lower = pos_ref[2] == 0
    outs[0][...] = jnp.where(lower, value[:half], value[half:])
    outs[1][...] = jnp.where(lower, value[half:], value[:half])


def first_kernel(count, pos_ref, panel_ref, *refs):
    scans, outs, total = refs[:count], refs[count:-1], refs[-1]
    n = scans[0].shape[1]
    g = pl.program_id(0)

    @pl.when(g == 0)
    def _():
        total[...] = jnp.zeros_like(total)

    for u in range(count):
        panel = panel_ref[u * n : (u + 1) * n]
        total[...] += jnp.dot(scans[u][...], panel, preferred_element_type=F32)

    @pl.when(g == pl.num_programs(0) - 1)
    def _():
        write_halves(pos_ref, total[...], outs)


def first_project(scans, pos, panel, steps=3, count=4):
    time_rows, voxels = scans.shape
    rank = panel.shape[1]
    n = voxels // (steps * count)
    half = jax.ShapeDtypeStruct((time_rows // 2, rank), F32)

    def column(u):
        return lambda g, pos: (0, g * count + u)

    return pl.pallas_call(
        functools.partial(first_kernel, count),
        out_shape=[half, half],
        grid_spec=pltpu.PrefetchScalarGridSpec(
            num_scalar_prefetch=1,
            grid=(steps,),
            in_specs=[pl.BlockSpec((count * n, rank), lambda g, pos: (g, 0))]
            + [pl.BlockSpec((time_rows, n), column(u)) for u in range(count)],
            out_specs=[pl.BlockSpec(half.shape, lambda g, pos: (0, 0))] * 2,
            scratch_shapes=[pltpu.VMEM((time_rows, rank), F32)],
        ),
        compiler_params=params(VMEM_FIRST),
        cost_estimate=LIGHT,
    )(pos, panel, *([scans] * count))


def project_kernel(has_base, split, items, pos_ref, *refs):
    refs = list(refs)
    base = refs.pop(0) if has_base else None
    outs = [refs.pop() for _ in range(2 if split else 1)][::-1]
    scans, pieces = refs[: len(items)], refs[len(items) :]
    time_rows = scans[0].shape[0]
    rank = outs[0].shape[1]
    total = jnp.zeros((time_rows, rank), F32)
    for scan, (source, index) in zip(scans, items):
        piece = pieces[source][...] if index is None else pieces[source][index]
        total += jnp.dot(scan[...], piece, preferred_element_type=F32)
    if has_base:
        total += base[...]
    if split:
        write_halves(pos_ref, total, outs)
    else:
        outs[0][...] = total


def project(scans, layout, pos, groups, base=None, split=False):
    time_rows = scans.shape[0]
    rank = groups[0][2].shape[-1]
    items, names = [], []
    for source, (j, ks, array) in enumerate(groups):
        for i, k in enumerate(ks):
            items.append((source, None if array.ndim == 2 else i))
            names.append((j, k))

    def column(j, k):
        return lambda g, pos: (0, layout.block(j, k, pos))

    full = lambda shape: pl.BlockSpec(shape, lambda g, pos: (0,) * len(shape))
    bases = [] if base is None else [base]
    arrays = [array for _, _, array in groups]
    shape = (time_rows // 2, rank) if split else (time_rows, rank)
    out_shape = [jax.ShapeDtypeStruct(shape, F32)] * (2 if split else 1)
    out = pl.pallas_call(
        functools.partial(project_kernel, base is not None, split, items),
        out_shape=out_shape,
        grid_spec=pltpu.PrefetchScalarGridSpec(
            num_scalar_prefetch=1,
            grid=(1,),
            in_specs=[full(b.shape) for b in bases]
            + [pl.BlockSpec((time_rows, layout.columns(j)), column(j, k)) for j, k in names]
            + [full(p.shape) for p in arrays],
            out_specs=[full(shape)] * len(out_shape),
        ),
        compiler_params=params(),
        cost_estimate=LIGHT,
    )(pos, *bases, *([scans] * len(items)), *arrays)
    return out if split else out[0]


def finish_kernel(layout, items, has_base, pos_ref, inverse_ref, *refs):
    refs, (out, held, sems) = refs[:-3], refs[-3:]
    if has_base:
        refs = refs[1:]
    copies = []
    used = 0
    pos = (pos_ref[0], pos_ref[1])
    for number, (source, index, j, k) in enumerate(items):
        n = layout.columns(j)
        codes = refs[source][...] if index is None else refs[source][index]
        if j is None:
            value = jnp.concatenate([Fixed.decode(codes[side]) for side in range(LOW)])
        else:
            value = Fixed.decode(codes)
        rows = pl.ds(used, n)
        held[rows] = times_transpose(value, inverse_ref[...])
        used += n
        start = pl.multiple_of(layout.block(j, k, pos) * n, n)
        copy = pltpu.make_async_copy(held.at[rows], out.at[pl.ds(start, n)], sems.at[number])
        copy.start()
        copies.append(copy)
    for copy in copies:
        copy.wait()


def finish(layout, pos, groups, inverse, voxels, base=None):
    rank = inverse.shape[0]
    items = []
    for source, (j, ks, array) in enumerate(groups):
        alone = array.ndim == (2 if j is not None else 3)
        for i, k in enumerate(ks):
            items.append((source, None if alone else i, j, k))
    columns = sum(layout.columns(j) for _, _, j, _ in items)
    bases = [] if base is None else [base]
    arrays = [array for _, _, array in groups]
    return pl.pallas_call(
        functools.partial(finish_kernel, layout, items, base is not None),
        out_shape=jax.ShapeDtypeStruct((voxels, rank), F32),
        in_specs=[pl.BlockSpec(memory_space=pltpu.SMEM), WHOLE]
        + [pl.BlockSpec(memory_space=pl.ANY)] * len(bases)
        + [WHOLE] * len(arrays),
        out_specs=pl.BlockSpec(memory_space=pl.ANY),
        scratch_shapes=[
            pltpu.VMEM((columns, rank), F32),
            pltpu.SemaphoreType.DMA((len(items),)),
        ],
        input_output_aliases={2: 0} if bases else {},
        compiler_params=params(),
        cost_estimate=LIGHT,
    )(pos, inverse, *bases, *arrays)


def inverse_factor(gram):
    size = gram.shape[0]
    groups = size // GROUP
    shape = (GROUP, size)
    sub = lax.broadcasted_iota(jnp.int32, shape, 0)
    lane = lax.broadcasted_iota(jnp.int32, shape, 1)
    left = [gram[GROUP * i : GROUP * (i + 1)] for i in range(groups)]
    right = [jnp.where(sub + GROUP * i == lane, 1.0, 0.0).astype(F32) for i in range(groups)]
    for g in range(groups):
        first = g * GROUP
        wide = lambda value: jnp.broadcast_to(value, shape)
        rows = [wide(left[g][t : t + 1]) for t in range(GROUP)]
        inverse_rows = [wide(right[g][t : t + 1]) for t in range(GROUP)]
        block = [
            [wide(left[g][t : t + 1, first + u : first + u + 1]) for u in range(GROUP)]
            for t in range(GROUP)
        ]
        below = range(g + 1, groups)
        columns = {
            i: [wide(left[i][:, first + u : first + u + 1]) for u in range(GROUP)] for i in below
        }
        scaled = []
        for t in range(GROUP):
            pivot = 1.0 / block[t][t]
            scaled.append((rows[t] * pivot, inverse_rows[t] * pivot))
            for u in range(t + 1, GROUP):
                factor = block[t][u] * pivot
                for w in range(u, GROUP):
                    block[u][w] = block[u][w] - factor * block[t][w]
                rows[u] = rows[u] - factor * rows[t]
                inverse_rows[u] = inverse_rows[u] - factor * inverse_rows[t]
                for i in below:
                    columns[i][u] = columns[i][u] - factor * columns[i][t]
        for i in below:
            for t in range(GROUP):
                left[i] = left[i] - columns[i][t] * scaled[t][0]
                right[i] = right[i] - columns[i][t] * scaled[t][1]
        for t in range(GROUP):
            left[g] = jnp.where(sub == t, rows[t], left[g])
            right[g] = jnp.where(sub == t, inverse_rows[t], right[g])
    out = []
    for g in range(groups):
        pivots = jnp.sum(
            jnp.where(sub + GROUP * g == lane, left[g], 0.0), axis=1, keepdims=True
        )
        out.append(right[g] * lax.rsqrt(pivots))
    return jnp.concatenate(out)


def times_transpose(value, inverse):
    return lax.dot_general(
        value, inverse, (((1,), (1,)), ((), ())), precision=HIGHEST, preferred_element_type=F32
    )


def scores_kernel(with_factor, lengths_ref, subjects_ref, pos_ref, mine_ref, other_ref, *refs):
    out_ref = refs[-1]
    length = lengths_ref[subjects_ref[pos_ref[1] * LOW + pos_ref[0]]]
    mine, other = mine_ref[...], other_ref[...]
    lower = pos_ref[2] == 0
    scores = jnp.concatenate([jnp.where(lower, mine, other), jnp.where(lower, other, mine)])
    if with_factor:
        scores = times_transpose(scores, refs[0][...])
    live = lax.broadcasted_iota(jnp.int32, scores.shape, 0) < length
    out_ref[...] = jnp.where(live, scores, 0.0).astype(BF16)


def invert_kernel(all_voxels, *refs):
    terms = [ref[...] for ref in refs[:-1]]
    while len(terms) > 1:
        terms = [terms[i] + terms[i + 1] for i in range(0, len(terms), 2)]
    refs[-1][...] = inverse_factor(terms[0] * (1.0 / all_voxels))


def make(mesh):
    subjects, blocks = mesh.shape["subj"], mesh.shape["vox"]
    swap = functools.partial(exchange, axis="subj", size=subjects)
    swap_vox = functools.partial(exchange, axis="vox", size=blocks)

    def on_device(scans, test_matrix, lengths, block_subject):
        time_rows, voxels = scans.shape
        rank = test_matrix.shape[1]
        all_voxels = voxels * blocks
        layout = Layout(voxels, subjects)
        high = layout.high
        ks = list(range(high))
        me = lax.axis_index("subj")
        core = lax.axis_index("vox") % 2
        pos = jnp.stack([me % LOW, me // LOW, core]).astype(jnp.int32)

        def sketch_sum(scores, code):
            def part(after, j, ks, apart, per_step):
                ordered = scores if after is None else lax.optimization_barrier((scores, after))[0]
                return sketch_part(
                    scans, layout, pos, ordered, j, ks, code, apart, per_step
                )

            away = part(None, 1, ks, False, high // 2)
            got_away = swap(away, mask=1)
            second = part(away, None, ks[1:], True, high - 1)
            got_second = [swap(second[k - 1], mask=k * LOW) for k in ks[1:]]
            home = part(second[0], 0, ks, False, high // 2)
            (second_own,) = part(second[0], None, ks[:1], True, 1)
            got_away, got_second, home, second_own = lax.optimization_barrier(
                (got_away, got_second, home, second_own)
            )
            piece = jax.ShapeDtypeStruct((layout.single + code.pad, rank), code.dtype)
            first = small_call(
                functools.partial(add_pieces_kernel, code, high), [piece] * high, home, got_away
            )
            got_first = [swap(first[k], mask=k * LOW) for k in ks[1:]]

            half = jax.ShapeDtypeStruct((layout.pair // 2 + code.pad, rank), code.dtype)
            keep, send = pl.pallas_call(
                functools.partial(add_halves_kernel, code),
                out_shape=[half, half],
                in_specs=[pl.BlockSpec(memory_space=pltpu.SMEM)] + [WHOLE] * high,
                out_specs=[WHOLE, WHOLE],
                compiler_params=params(),
                cost_estimate=LIGHT,
            )(pos, second_own, *got_second)
            got_send = swap(send, mask=1)
            return (
                add_all(code, [first[0], *got_first]),
                add_all(code, [keep, got_send]),
            )

        def gather(first, second, gram):
            gram = gram + swap_vox(gram, mask=1)
            first, second, gram = lax.optimization_barrier((first, second, gram))
            low_own = swap(first, mask=1)
            pieces = [swap(first, mask=k * LOW) for k in ks[1:]]
            got = swap(second, mask=1)
            lower = pos[0] == 0
            pair = jnp.stack([jnp.where(lower, second, got), jnp.where(lower, got, second)])
            mask = 2
            while mask < blocks:
                gram = gram + swap_vox(gram, mask=mask)
                mask *= 2
            gram = gram + swap(gram, mask=1)
            grams = [gram] + [swap(gram, mask=k * LOW) for k in ks[1:]]
            pieces, pair, grams = lax.optimization_barrier((pieces, pair, grams))
            low_rest = swap(jnp.stack(pieces), mask=1)
            seconds = [pair] + [swap(pair, mask=k * LOW) for k in ks[1:]]
            early = [(0, [k], array) for k, array in zip(ks, [first] + pieces)]
            late = [(1, ks[:1], low_own), (1, ks[1:], low_rest)]
            pairs = [(None, [k], array) for k, array in zip(ks, seconds)]
            return early, late, pairs, grams

        def sum_scores(mine, send, *factor):
            mine = mine + swap_vox(send, mask=1)
            mask = 2
            while mask < blocks:
                mine = mine + swap_vox(mine, mask=mask)
                mask *= 2
            other = swap_vox(mine, mask=1)
            return pl.pallas_call(
                functools.partial(scores_kernel, bool(factor)),
                out_shape=jax.ShapeDtypeStruct((time_rows, rank), BF16),
                in_specs=[pl.BlockSpec(memory_space=pltpu.SMEM)] * 3
                + [WHOLE] * (2 + len(factor)),
                out_specs=WHOLE,
                compiler_params=params(),
                cost_estimate=LIGHT,
            )(lengths, block_subject, pos, mine, other, *factor)

        def pass_over(scores, code):
            (first, gram_first), (second, gram_second) = sketch_sum(scores, code)
            early, late, pairs, grams = gather(first, second, gram_first + gram_second)
            inverse = small_call(
                functools.partial(invert_kernel, all_voxels),
                jax.ShapeDtypeStruct((rank, rank), F32), *grams,
            )
            return early, late, pairs, inverse

        scores = sum_scores(*first_project(scans, pos, test_matrix))
        early, late, pairs, inverse = pass_over(scores, Plain)
        pairs = [(j, k, array.reshape(layout.pair, rank)) for j, k, array in pairs]
        total = project(scans, layout, pos, early)
        total = project(scans, layout, pos, late, total)
        total = project(scans, layout, pos, pairs[: high // 2], total)
        total, inverse = lax.optimization_barrier((total, inverse))
        halves = project(scans, layout, pos, pairs[high // 2 :], total, True)
        scores = sum_scores(*halves, inverse)
        early, late, pairs, inverse = pass_over(scores, Fixed)
        out = finish(layout, pos, early + late, inverse, voxels)
        return finish(layout, pos, pairs, inverse, voxels, out)

    return on_device


def solution(mesh):
    placed = (P("subj", "vox"), P("vox", None), P(), P())
    return jax.shard_map(
        make(mesh), mesh=mesh, in_specs=placed, out_specs=P("vox", None), check_vma=False
    )
```

```python
import functools

import jax
import jax.numpy as jnp
from jax import lax
from jax.experimental import pallas as pl
from jax.experimental.pallas import tpu as pltpu
from jax.sharding import PartitionSpec as P

F32 = jnp.float32
BF16 = jnp.bfloat16
I16 = jnp.int16
HIGHEST = lax.Precision.HIGHEST
STEPS = 64.0
LOW = 2
GROUP = 8
LANES = 128
VMEM_BYTES = 20 << 20
VMEM_FIRST = 48 << 20
LIGHT = pl.CostEstimate(flops=1, bytes_accessed=1, transcendentals=0)
WHOLE = pl.BlockSpec(memory_space=pltpu.VMEM)


def exchange(value, axis, size, mask):
    return lax.ppermute(value, axis, [(i, i ^ mask) for i in range(size)])


class Plain:
    pad = 0
    dtype = BF16
    limit = VMEM_FIRST

    @staticmethod
    def encode(value):
        return value.astype(BF16)

    @staticmethod
    def decode(sent):
        return sent.astype(F32)


class Fixed:
    pad = 16
    dtype = I16
    limit = VMEM_BYTES

    @staticmethod
    def encode(value):
        top = jnp.maximum(jnp.max(jnp.abs(value), axis=0, keepdims=True), 1e-30)
        power = jnp.ceil(jnp.log2(top * (1.0 / 32000.0)) * STEPS)
        codes = jnp.round(value * jnp.exp2(power * (-1.0 / STEPS)))
        codes = jnp.clip(codes, -32767.0, 32767.0)
        rows = jnp.broadcast_to(power, (Fixed.pad, value.shape[1]))
        return jnp.concatenate([codes, rows]).astype(jnp.int32).astype(I16)

    @staticmethod
    def decode(sent):
        wide = sent.astype(jnp.int32).astype(F32)
        rows = wide.shape[0] - Fixed.pad
        return wide[:rows] * jnp.exp2(wide[rows : rows + 1] * (1.0 / STEPS))


def params(limit=VMEM_BYTES):
    return pltpu.CompilerParams(vmem_limit_bytes=limit)


class Layout:
    def __init__(self, voxels, subjects):
        self.high = subjects // LOW
        unit = subjects * LANES
        for top, bottom in ((2, 3), (1, 2)):
            self.cut = voxels * top // bottom
            self.pair = (voxels - self.cut) // self.high
            if self.cut % unit == 0 and voxels % unit == 0 and self.cut % self.pair == 0:
                break
        self.single = self.cut // subjects

    def columns(self, j):
        return self.pair if j is None else self.single

    def block(self, j, k, pos):
        if j is None:
            return self.cut // self.pair + (pos[1] ^ k)
        return (pos[0] ^ j) * self.high + (pos[1] ^ k)


def sketch_kernel(code, apart, count, pos_ref, scores_ref, *refs):
    for u in range(count):
        product = lax.dot_general(
            scores_ref[...], refs[u][...], (((0,), (0,)), ((), ())), preferred_element_type=F32
        )
        out = refs[count + u] if apart else refs[count].at[u]
        out[...] = code.encode(product.T)


def sketch_part(scans, layout, pos, scores, j, ks, code, apart, per_step):
    time_rows = scans.shape[0]
    rank = scores.shape[1]
    n = layout.columns(j)
    rows = n + code.pad
    steps = len(ks) // per_step

    def column(u):
        return lambda g, pos: (0, layout.block(j, ks[0] + g * per_step + u, pos))

    if apart:
        out_shape = [jax.ShapeDtypeStruct((rows, rank), code.dtype)] * len(ks)
        out_specs = [pl.BlockSpec((rows, rank), lambda g, pos: (0, 0))] * len(ks)
    else:
        out_shape = jax.ShapeDtypeStruct((len(ks), rows, rank), code.dtype)
        out_specs = pl.BlockSpec((per_step, rows, rank), lambda g, pos: (g, 0, 0))
    return pl.pallas_call(
        functools.partial(sketch_kernel, code, apart, per_step),
        out_shape=out_shape,
        grid_spec=pltpu.PrefetchScalarGridSpec(
            num_scalar_prefetch=1,
            grid=(steps,),
            in_specs=[pl.BlockSpec((time_rows, rank), lambda g, pos: (0, 0))]
            + [pl.BlockSpec((time_rows, n), column(u)) for u in range(per_step)],
            out_specs=out_specs,
        ),
        compiler_params=params(code.limit),
        cost_estimate=LIGHT,
    )(pos, scores, *([scans] * per_step))


def small_call(kernel, out_shape, *args):
    return pl.pallas_call(
        kernel,
        out_shape=out_shape,
        in_specs=[WHOLE] * len(args),
        out_specs=jax.tree.map(lambda _: WHOLE, out_shape),
        compiler_params=params(),
        cost_estimate=LIGHT,
    )(*args)


def add_pieces_kernel(code, count, own_ref, got_ref, *outs):
    for k in range(count):
        outs[k][...] = code.encode(code.decode(own_ref[k]) + code.decode(got_ref[k]))


def add_all_kernel(code, *refs):
    parts, outs = refs[:-2], refs[-2:]
    total = code.decode(parts[0][...])
    for part in parts[1:]:
        total = total + code.decode(part[...])
    outs[0][...] = code.encode(total)
    outs[1][...] = lax.dot_general(
        total, total, (((0,), (0,)), ((), ())), precision=HIGHEST, preferred_element_type=F32
    )


def add_halves_kernel(code, pos_ref, *refs):
    parts, (keep_ref, send_ref) = refs[:-2], refs[-2:]
    total = code.decode(parts[0][...])
    for part in parts[1:]:
        total = total + code.decode(part[...])
    half = total.shape[0] // 2
    lower = pos_ref[0] == 0
    keep_ref[...] = code.encode(jnp.where(lower, total[:half], total[half:]))
    send_ref[...] = code.encode(jnp.where(lower, total[half:], total[:half]))


def add_all(code, parts):
    rank = parts[0].shape[1]
    out = [jax.ShapeDtypeStruct(parts[0].shape, code.dtype)]
    out.append(jax.ShapeDtypeStruct((rank, rank), F32))
    return small_call(functools.partial(add_all_kernel, code), out, *parts)


def write_halves(pos_ref, value, outs):
    half = value.shape[0] // 2
    lower = pos_ref[2] == 0
    outs[0][...] = jnp.where(lower, value[:half], value[half:])
    outs[1][...] = jnp.where(lower, value[half:], value[:half])


def first_kernel(count, pos_ref, panel_ref, *refs):
    scans, outs, total = refs[:count], refs[count:-1], refs[-1]
    n = scans[0].shape[1]
    g = pl.program_id(0)

    @pl.when(g == 0)
    def _():
        total[...] = jnp.zeros_like(total)

    for u in range(count):
        panel = panel_ref[u * n : (u + 1) * n]
        total[...] += jnp.dot(scans[u][...], panel, preferred_element_type=F32)

    @pl.when(g == pl.num_programs(0) - 1)
    def _():
        write_halves(pos_ref, total[...], outs)


def first_project(scans, pos, panel, steps=3, count=4):
    time_rows, voxels = scans.shape
    rank = panel.shape[1]
    n = voxels // (steps * count)
    half = jax.ShapeDtypeStruct((time_rows // 2, rank), F32)

    def column(u):
        return lambda g, pos: (0, g * count + u)

    return pl.pallas_call(
        functools.partial(first_kernel, count),
        out_shape=[half, half],
        grid_spec=pltpu.PrefetchScalarGridSpec(
            num_scalar_prefetch=1,
            grid=(steps,),
            in_specs=[pl.BlockSpec((count * n, rank), lambda g, pos: (g, 0))]
            + [pl.BlockSpec((time_rows, n), column(u)) for u in range(count)],
            out_specs=[pl.BlockSpec(half.shape, lambda g, pos: (0, 0))] * 2,
            scratch_shapes=[pltpu.VMEM((time_rows, rank), F32)],
        ),
        compiler_params=params(VMEM_FIRST),
        cost_estimate=LIGHT,
    )(pos, panel, *([scans] * count))


def project_kernel(has_base, split, items, pos_ref, *refs):
    refs = list(refs)
    base = refs.pop(0) if has_base else None
    outs = [refs.pop() for _ in range(2 if split else 1)][::-1]
    scans, pieces = refs[: len(items)], refs[len(items) :]
    time_rows = scans[0].shape[0]
    rank = outs[0].shape[1]
    total = jnp.zeros((time_rows, rank), F32)
    for scan, (source, index) in zip(scans, items):
        piece = pieces[source][...] if index is None else pieces[source][index]
        total += jnp.dot(scan[...], piece, preferred_element_type=F32)
    if has_base:
        total += base[...]
    if split:
        write_halves(pos_ref, total, outs)
    else:
        outs[0][...] = total


def project(scans, layout, pos, groups, base=None, split=False):
    time_rows = scans.shape[0]
    rank = groups[0][2].shape[-1]
    items, names = [], []
    for source, (j, ks, array) in enumerate(groups):
        for i, k in enumerate(ks):
            items.append((source, None if array.ndim == 2 else i))
            names.append((j, k))

    def column(j, k):
        return lambda g, pos: (0, layout.block(j, k, pos))

    full = lambda shape: pl.BlockSpec(shape, lambda g, pos: (0,) * len(shape))
    bases = [] if base is None else [base]
    arrays = [array for _, _, array in groups]
    shape = (time_rows // 2, rank) if split else (time_rows, rank)
    out_shape = [jax.ShapeDtypeStruct(shape, F32)] * (2 if split else 1)
    out = pl.pallas_call(
        functools.partial(project_kernel, base is not None, split, items),
        out_shape=out_shape,
        grid_spec=pltpu.PrefetchScalarGridSpec(
            num_scalar_prefetch=1,
            grid=(1,),
            in_specs=[full(b.shape) for b in bases]
            + [pl.BlockSpec((time_rows, layout.columns(j)), column(j, k)) for j, k in names]
            + [full(p.shape) for p in arrays],
            out_specs=[full(shape)] * len(out_shape),
        ),
        compiler_params=params(),
        cost_estimate=LIGHT,
    )(pos, *bases, *([scans] * len(items)), *arrays)
    return out if split else out[0]


def finish_kernel(layout, items, has_base, pos_ref, inverse_ref, *refs):
    refs, (out, held, sems) = refs[:-3], refs[-3:]
    if has_base:
        refs = refs[1:]
    copies = []
    used = 0
    pos = (pos_ref[0], pos_ref[1])
    for number, (source, index, j, k) in enumerate(items):
        n = layout.columns(j)
        codes = refs[source][...] if index is None else refs[source][index]
        if j is None:
            value = jnp.concatenate([Fixed.decode(codes[side]) for side in range(LOW)])
        else:
            value = Fixed.decode(codes)
        rows = pl.ds(used, n)
        held[rows] = times_transpose(value, inverse_ref[...])
        used += n
        start = pl.multiple_of(layout.block(j, k, pos) * n, n)
        copy = pltpu.make_async_copy(held.at[rows], out.at[pl.ds(start, n)], sems.at[number])
        copy.start()
        copies.append(copy)
    for copy in copies:
        copy.wait()


def finish(layout, pos, groups, inverse, voxels, base=None):
    rank = inverse.shape[0]
    items = []
    for source, (j, ks, array) in enumerate(groups):
        alone = array.ndim == (2 if j is not None else 3)
        for i, k in enumerate(ks):
            items.append((source, None if alone else i, j, k))
    columns = sum(layout.columns(j) for _, _, j, _ in items)
    bases = [] if base is None else [base]
    arrays = [array for _, _, array in groups]
    return pl.pallas_call(
        functools.partial(finish_kernel, layout, items, base is not None),
        out_shape=jax.ShapeDtypeStruct((voxels, rank), F32),
        in_specs=[pl.BlockSpec(memory_space=pltpu.SMEM), WHOLE]
        + [pl.BlockSpec(memory_space=pl.ANY)] * len(bases)
        + [WHOLE] * len(arrays),
        out_specs=pl.BlockSpec(memory_space=pl.ANY),
        scratch_shapes=[
            pltpu.VMEM((columns, rank), F32),
            pltpu.SemaphoreType.DMA((len(items),)),
        ],
        input_output_aliases={2: 0} if bases else {},
        compiler_params=params(),
        cost_estimate=LIGHT,
    )(pos, inverse, *bases, *arrays)


def inverse_factor(gram):
    size = gram.shape[0]
    groups = size // GROUP
    shape = (GROUP, size)
    sub = lax.broadcasted_iota(jnp.int32, shape, 0)
    lane = lax.broadcasted_iota(jnp.int32, shape, 1)
    left = [gram[GROUP * i : GROUP * (i + 1)] for i in range(groups)]
    right = [jnp.where(sub + GROUP * i == lane, 1.0, 0.0).astype(F32) for i in range(groups)]
    for g in range(groups):
        first = g * GROUP
        wide = lambda value: jnp.broadcast_to(value, shape)
        rows = [wide(left[g][t : t + 1]) for t in range(GROUP)]
        inverse_rows = [wide(right[g][t : t + 1]) for t in range(GROUP)]
        block = [
            [wide(left[g][t : t + 1, first + u : first + u + 1]) for u in range(GROUP)]
            for t in range(GROUP)
        ]
        below = range(g + 1, groups)
        columns = {
            i: [wide(left[i][:, first + u : first + u + 1]) for u in range(GROUP)] for i in below
        }
        scaled = []
        for t in range(GROUP):
            pivot = 1.0 / block[t][t]
            scaled.append((rows[t] * pivot, inverse_rows[t] * pivot))
            for u in range(t + 1, GROUP):
                factor = block[t][u] * pivot
                for w in range(u, GROUP):
                    block[u][w] = block[u][w] - factor * block[t][w]
                rows[u] = rows[u] - factor * rows[t]
                inverse_rows[u] = inverse_rows[u] - factor * inverse_rows[t]
                for i in below:
                    columns[i][u] = columns[i][u] - factor * columns[i][t]
        for i in below:
            for t in range(GROUP):
                left[i] = left[i] - columns[i][t] * scaled[t][0]
                right[i] = right[i] - columns[i][t] * scaled[t][1]
        for t in range(GROUP):
            left[g] = jnp.where(sub == t, rows[t], left[g])
            right[g] = jnp.where(sub == t, inverse_rows[t], right[g])
    out = []
    for g in range(groups):
        pivots = jnp.sum(
            jnp.where(sub + GROUP * g == lane, left[g], 0.0), axis=1, keepdims=True
        )
        out.append(right[g] * lax.rsqrt(pivots))
    return jnp.concatenate(out)


def times_transpose(value, inverse):
    return lax.dot_general(
        value, inverse, (((1,), (1,)), ((), ())), precision=HIGHEST, preferred_element_type=F32
    )


def scores_kernel(with_factor, lengths_ref, subjects_ref, pos_ref, mine_ref, other_ref, *refs):
    out_ref = refs[-1]
    length = lengths_ref[subjects_ref[pos_ref[1] * LOW + pos_ref[0]]]
    mine, other = mine_ref[...], other_ref[...]
    lower = pos_ref[2] == 0
    scores = jnp.concatenate([jnp.where(lower, mine, other), jnp.where(lower, other, mine)])
    if with_factor:
        scores = times_transpose(scores, refs[0][...])
    live = lax.broadcasted_iota(jnp.int32, scores.shape, 0) < length
    out_ref[...] = jnp.where(live, scores, 0.0).astype(BF16)


def invert_kernel(all_voxels, *refs):
    terms = [ref[...] for ref in refs[:-1]]
    while len(terms) > 1:
        terms = [terms[i] + terms[i + 1] for i in range(0, len(terms), 2)]
    refs[-1][...] = inverse_factor(terms[0] * (1.0 / all_voxels))


def make(mesh):
    subjects, blocks = mesh.shape["subj"], mesh.shape["vox"]
    swap = functools.partial(exchange, axis="subj", size=subjects)
    swap_vox = functools.partial(exchange, axis="vox", size=blocks)

    def on_device(scans, test_matrix, lengths, block_subject):
        time_rows, voxels = scans.shape
        rank = test_matrix.shape[1]
        all_voxels = voxels * blocks
        layout = Layout(voxels, subjects)
        high = layout.high
        ks = list(range(high))
        me = lax.axis_index("subj")
        core = lax.axis_index("vox") % 2
        pos = jnp.stack([me % LOW, me // LOW, core]).astype(jnp.int32)

        def sketch_sum(scores, code):
            def part(after, j, ks, apart, per_step):
                ordered = scores if after is None else lax.optimization_barrier((scores, after))[0]
                return sketch_part(
                    scans, layout, pos, ordered, j, ks, code, apart, per_step
                )

            away = part(None, 1, ks, False, high // 2)
            got_away = swap(away, mask=1)
            second = part(away, None, ks[1:], True, high - 1)
            got_second = [swap(second[k - 1], mask=k * LOW) for k in ks[1:]]
            home = part(second[0], 0, ks, False, high // 2)
            (second_own,) = part(second[0], None, ks[:1], True, 1)
            got_away, got_second, home, second_own = lax.optimization_barrier(
                (got_away, got_second, home, second_own)
            )
            piece = jax.ShapeDtypeStruct((layout.single + code.pad, rank), code.dtype)
            first = small_call(
                functools.partial(add_pieces_kernel, code, high), [piece] * high, home, got_away
            )
            got_first = [swap(first[k], mask=k * LOW) for k in ks[1:]]

            half = jax.ShapeDtypeStruct((layout.pair // 2 + code.pad, rank), code.dtype)
            keep, send = pl.pallas_call(
                functools.partial(add_halves_kernel, code),
                out_shape=[half, half],
                in_specs=[pl.BlockSpec(memory_space=pltpu.SMEM)] + [WHOLE] * high,
                out_specs=[WHOLE, WHOLE],
                compiler_params=params(),
                cost_estimate=LIGHT,
            )(pos, second_own, *got_second)
            got_send = swap(send, mask=1)
            return (
                add_all(code, [first[0], *got_first]),
                add_all(code, [keep, got_send]),
            )

        def gather(first, second, gram):
            gram = gram + swap_vox(gram, mask=1)
            first, second, gram = lax.optimization_barrier((first, second, gram))
            pieces = [swap(first, mask=k * LOW) for k in ks[1:]]
            got = swap(second, mask=1)
            lower = pos[0] == 0
            pair = jnp.stack([jnp.where(lower, second, got), jnp.where(lower, got, second)])
            mask = 2
            while mask < blocks:
                gram = gram + swap_vox(gram, mask=mask)
                mask *= 2
            gram = gram + swap(gram, mask=1)
            gram = gram + swap(gram, mask=LOW)
            pieces, pair, gram = lax.optimization_barrier((pieces, pair, gram))
            low_got = swap(jnp.stack([first] + pieces), mask=1)
            seconds = [pair] + [swap(pair, mask=k * LOW) for k in ks[1:]]
            mask = 2
            while 2 * mask < high:
                gram = gram + swap(gram, mask=mask * LOW)
                mask *= 2
            grams = [gram, swap(gram, mask=mask * LOW)]
            early = [(0, [k], array) for k, array in zip(ks, [first] + pieces)]
            late = [(1, ks, low_got)]
            pairs = [(None, [k], array) for k, array in zip(ks, seconds)]
            return early, late, pairs, grams

        def sum_scores(mine, send, *factor):
            mine = mine + swap_vox(send, mask=1)
            mask = 2
            while mask < blocks:
                mine = mine + swap_vox(mine, mask=mask)
                mask *= 2
            other = swap_vox(mine, mask=1)
            return pl.pallas_call(
                functools.partial(scores_kernel, bool(factor)),
                out_shape=jax.ShapeDtypeStruct((time_rows, rank), BF16),
                in_specs=[pl.BlockSpec(memory_space=pltpu.SMEM)] * 3
                + [WHOLE] * (2 + len(factor)),
                out_specs=WHOLE,
                compiler_params=params(),
                cost_estimate=LIGHT,
            )(lengths, block_subject, pos, mine, other, *factor)

        def pass_over(scores, code):
            (first, gram_first), (second, gram_second) = sketch_sum(scores, code)
            early, late, pairs, grams = gather(first, second, gram_first + gram_second)
            inverse = small_call(
                functools.partial(invert_kernel, all_voxels),
                jax.ShapeDtypeStruct((rank, rank), F32), *grams,
            )
            return early, late, pairs, inverse

        scores = sum_scores(*first_project(scans, pos, test_matrix))
        early, late, pairs, inverse = pass_over(scores, Plain)
        pairs = [(j, k, array.reshape(layout.pair, rank)) for j, k, array in pairs]
        total = project(scans, layout, pos, early)
        total = project(scans, layout, pos, late, total)
        total = project(scans, layout, pos, pairs[: high // 2], total)
        total, inverse = lax.optimization_barrier((total, inverse))
        halves = project(scans, layout, pos, pairs[high // 2 :], total, True)
        scores = sum_scores(*halves, inverse)
        early, late, pairs, inverse = pass_over(scores, Fixed)
        out = finish(layout, pos, early + late, inverse, voxels)
        return finish(layout, pos, pairs, inverse, voxels, out)

    return on_device


def solution(mesh):
    placed = (P("subj", "vox"), P("vox", None), P(), P())
    return jax.shard_map(
        make(mesh), mesh=mesh, in_specs=placed, out_specs=P("vox", None), check_vma=False
    )
```

```python
import functools

import jax
import jax.numpy as jnp
from jax import lax
from jax.experimental import pallas as pl
from jax.experimental.pallas import tpu as pltpu
from jax.sharding import PartitionSpec as P

F32 = jnp.float32
BF16 = jnp.bfloat16
I16 = jnp.int16
HIGHEST = lax.Precision.HIGHEST
STEPS = 64.0
LOW = 2
GROUP = 8
LANES = 128
VMEM_BYTES = 20 << 20
VMEM_FIRST = 48 << 20
LIGHT = pl.CostEstimate(flops=1, bytes_accessed=1, transcendentals=0)
WHOLE = pl.BlockSpec(memory_space=pltpu.VMEM)


def exchange(value, axis, size, mask):
    return lax.ppermute(value, axis, [(i, i ^ mask) for i in range(size)])


class Plain:
    pad = 0
    dtype = BF16
    limit = VMEM_FIRST

    @staticmethod
    def encode(value):
        return value.astype(BF16)

    @staticmethod
    def decode(sent):
        return sent.astype(F32)


class Fixed:
    pad = 16
    dtype = I16
    limit = VMEM_BYTES

    @staticmethod
    def encode(value):
        top = jnp.maximum(jnp.max(jnp.abs(value), axis=0, keepdims=True), 1e-30)
        power = jnp.ceil(jnp.log2(top * (1.0 / 32000.0)) * STEPS)
        codes = jnp.round(value * jnp.exp2(power * (-1.0 / STEPS)))
        codes = jnp.clip(codes, -32767.0, 32767.0)
        rows = jnp.broadcast_to(power, (Fixed.pad, value.shape[1]))
        return jnp.concatenate([codes, rows]).astype(jnp.int32).astype(I16)

    @staticmethod
    def decode(sent):
        wide = sent.astype(jnp.int32).astype(F32)
        rows = wide.shape[0] - Fixed.pad
        return wide[:rows] * jnp.exp2(wide[rows : rows + 1] * (1.0 / STEPS))


def params(limit=VMEM_BYTES):
    return pltpu.CompilerParams(vmem_limit_bytes=limit)


class Layout:
    def __init__(self, voxels, subjects):
        self.high = subjects // LOW
        unit = subjects * LANES
        for top, bottom in ((3, 4), (2, 3), (1, 2)):
            self.cut = voxels * top // bottom
            self.pair = (voxels - self.cut) // self.high
            if self.cut % unit == 0 and voxels % unit == 0 and self.cut % self.pair == 0:
                break
        self.single = self.cut // subjects

    def columns(self, j):
        return self.pair if j is None else self.single

    def block(self, j, k, pos):
        if j is None:
            return self.cut // self.pair + (pos[1] ^ k)
        return (pos[0] ^ j) * self.high + (pos[1] ^ k)


def sketch_kernel(code, apart, count, pos_ref, scores_ref, *refs):
    for u in range(count):
        product = lax.dot_general(
            scores_ref[...], refs[u][...], (((0,), (0,)), ((), ())), preferred_element_type=F32
        )
        out = refs[count + u] if apart else refs[count].at[u]
        out[...] = code.encode(product.T)


def sketch_part(scans, layout, pos, scores, j, ks, code, apart, per_step):
    time_rows = scans.shape[0]
    rank = scores.shape[1]
    n = layout.columns(j)
    rows = n + code.pad
    steps = len(ks) // per_step

    def column(u):
        return lambda g, pos: (0, layout.block(j, ks[0] + g * per_step + u, pos))

    if apart:
        out_shape = [jax.ShapeDtypeStruct((rows, rank), code.dtype)] * len(ks)
        out_specs = [pl.BlockSpec((rows, rank), lambda g, pos: (0, 0))] * len(ks)
    else:
        out_shape = jax.ShapeDtypeStruct((len(ks), rows, rank), code.dtype)
        out_specs = pl.BlockSpec((per_step, rows, rank), lambda g, pos: (g, 0, 0))
    return pl.pallas_call(
        functools.partial(sketch_kernel, code, apart, per_step),
        out_shape=out_shape,
        grid_spec=pltpu.PrefetchScalarGridSpec(
            num_scalar_prefetch=1,
            grid=(steps,),
            in_specs=[pl.BlockSpec((time_rows, rank), lambda g, pos: (0, 0))]
            + [pl.BlockSpec((time_rows, n), column(u)) for u in range(per_step)],
            out_specs=out_specs,
        ),
        compiler_params=params(code.limit),
        cost_estimate=LIGHT,
    )(pos, scores, *([scans] * per_step))


def small_call(kernel, out_shape, *args):
    return pl.pallas_call(
        kernel,
        out_shape=out_shape,
        in_specs=[WHOLE] * len(args),
        out_specs=jax.tree.map(lambda _: WHOLE, out_shape),
        compiler_params=params(),
        cost_estimate=LIGHT,
    )(*args)


def add_pieces_kernel(code, count, own_ref, got_ref, *outs):
    for k in range(count):
        outs[k][...] = code.encode(code.decode(own_ref[k]) + code.decode(got_ref[k]))


def add_all_kernel(code, *refs):
    parts, outs = refs[:-2], refs[-2:]
    total = code.decode(parts[0][...])
    for part in parts[1:]:
        total = total + code.decode(part[...])
    outs[0][...] = code.encode(total)
    outs[1][...] = lax.dot_general(
        total, total, (((0,), (0,)), ((), ())), precision=HIGHEST, preferred_element_type=F32
    )


def add_halves_kernel(code, pos_ref, *refs):
    parts, (keep_ref, send_ref) = refs[:-2], refs[-2:]
    total = code.decode(parts[0][...])
    for part in parts[1:]:
        total = total + code.decode(part[...])
    half = total.shape[0] // 2
    lower = pos_ref[0] == 0
    keep_ref[...] = code.encode(jnp.where(lower, total[:half], total[half:]))
    send_ref[...] = code.encode(jnp.where(lower, total[half:], total[:half]))


def add_all(code, parts):
    rank = parts[0].shape[1]
    out = [jax.ShapeDtypeStruct(parts[0].shape, code.dtype)]
    out.append(jax.ShapeDtypeStruct((rank, rank), F32))
    return small_call(functools.partial(add_all_kernel, code), out, *parts)


def write_halves(pos_ref, value, outs):
    half = value.shape[0] // 2
    lower = pos_ref[2] == 0
    outs[0][...] = jnp.where(lower, value[:half], value[half:])
    outs[1][...] = jnp.where(lower, value[half:], value[:half])


def first_kernel(count, pos_ref, panel_ref, *refs):
    scans, outs, total = refs[:count], refs[count:-1], refs[-1]
    n = scans[0].shape[1]
    g = pl.program_id(0)

    @pl.when(g == 0)
    def _():
        total[...] = jnp.zeros_like(total)

    for u in range(count):
        panel = panel_ref[u * n : (u + 1) * n]
        total[...] += jnp.dot(scans[u][...], panel, preferred_element_type=F32)

    @pl.when(g == pl.num_programs(0) - 1)
    def _():
        write_halves(pos_ref, total[...], outs)


def first_project(scans, pos, panel, steps=3, count=4):
    time_rows, voxels = scans.shape
    rank = panel.shape[1]
    n = voxels // (steps * count)
    half = jax.ShapeDtypeStruct((time_rows // 2, rank), F32)

    def column(u):
        return lambda g, pos: (0, g * count + u)

    return pl.pallas_call(
        functools.partial(first_kernel, count),
        out_shape=[half, half],
        grid_spec=pltpu.PrefetchScalarGridSpec(
            num_scalar_prefetch=1,
            grid=(steps,),
            in_specs=[pl.BlockSpec((count * n, rank), lambda g, pos: (g, 0))]
            + [pl.BlockSpec((time_rows, n), column(u)) for u in range(count)],
            out_specs=[pl.BlockSpec(half.shape, lambda g, pos: (0, 0))] * 2,
            scratch_shapes=[pltpu.VMEM((time_rows, rank), F32)],
        ),
        compiler_params=params(VMEM_FIRST),
        cost_estimate=LIGHT,
    )(pos, panel, *([scans] * count))


def project_kernel(has_base, split, items, pos_ref, *refs):
    refs = list(refs)
    base = refs.pop(0) if has_base else None
    outs = [refs.pop() for _ in range(2 if split else 1)][::-1]
    scans, pieces = refs[: len(items)], refs[len(items) :]
    time_rows = scans[0].shape[0]
    rank = outs[0].shape[1]
    total = jnp.zeros((time_rows, rank), F32)
    for scan, (source, index) in zip(scans, items):
        piece = pieces[source][...] if index is None else pieces[source][index]
        total += jnp.dot(scan[...], piece, preferred_element_type=F32)
    if has_base:
        total += base[...]
    if split:
        write_halves(pos_ref, total, outs)
    else:
        outs[0][...] = total


def project(scans, layout, pos, groups, base=None, split=False):
    time_rows = scans.shape[0]
    rank = groups[0][2].shape[-1]
    items, names = [], []
    for source, (j, ks, array) in enumerate(groups):
        for i, k in enumerate(ks):
            items.append((source, None if array.ndim == 2 else i))
            names.append((j, k))

    def column(j, k):
        return lambda g, pos: (0, layout.block(j, k, pos))

    full = lambda shape: pl.BlockSpec(shape, lambda g, pos: (0,) * len(shape))
    bases = [] if base is None else [base]
    arrays = [array for _, _, array in groups]
    shape = (time_rows // 2, rank) if split else (time_rows, rank)
    out_shape = [jax.ShapeDtypeStruct(shape, F32)] * (2 if split else 1)
    out = pl.pallas_call(
        functools.partial(project_kernel, base is not None, split, items),
        out_shape=out_shape,
        grid_spec=pltpu.PrefetchScalarGridSpec(
            num_scalar_prefetch=1,
            grid=(1,),
            in_specs=[full(b.shape) for b in bases]
            + [pl.BlockSpec((time_rows, layout.columns(j)), column(j, k)) for j, k in names]
            + [full(p.shape) for p in arrays],
            out_specs=[full(shape)] * len(out_shape),
        ),
        compiler_params=params(),
        cost_estimate=LIGHT,
    )(pos, *bases, *([scans] * len(items)), *arrays)
    return out if split else out[0]


def finish_kernel(layout, items, has_base, pos_ref, inverse_ref, *refs):
    refs, (out, held, sems) = refs[:-3], refs[-3:]
    if has_base:
        refs = refs[1:]
    copies = []
    used = 0
    pos = (pos_ref[0], pos_ref[1])
    for number, (source, index, j, k) in enumerate(items):
        n = layout.columns(j)
        codes = refs[source][...] if index is None else refs[source][index]
        if j is None:
            value = jnp.concatenate([Fixed.decode(codes[side]) for side in range(LOW)])
        else:
            value = Fixed.decode(codes)
        rows = pl.ds(used, n)
        held[rows] = times_transpose(value, inverse_ref[...])
        used += n
        start = pl.multiple_of(layout.block(j, k, pos) * n, n)
        copy = pltpu.make_async_copy(held.at[rows], out.at[pl.ds(start, n)], sems.at[number])
        copy.start()
        copies.append(copy)
    for copy in copies:
        copy.wait()


def finish(layout, pos, groups, inverse, voxels, base=None):
    rank = inverse.shape[0]
    items = []
    for source, (j, ks, array) in enumerate(groups):
        alone = array.ndim == (2 if j is not None else 3)
        for i, k in enumerate(ks):
            items.append((source, None if alone else i, j, k))
    columns = sum(layout.columns(j) for _, _, j, _ in items)
    bases = [] if base is None else [base]
    arrays = [array for _, _, array in groups]
    return pl.pallas_call(
        functools.partial(finish_kernel, layout, items, base is not None),
        out_shape=jax.ShapeDtypeStruct((voxels, rank), F32),
        in_specs=[pl.BlockSpec(memory_space=pltpu.SMEM), WHOLE]
        + [pl.BlockSpec(memory_space=pl.ANY)] * len(bases)
        + [WHOLE] * len(arrays),
        out_specs=pl.BlockSpec(memory_space=pl.ANY),
        scratch_shapes=[
            pltpu.VMEM((columns, rank), F32),
            pltpu.SemaphoreType.DMA((len(items),)),
        ],
        input_output_aliases={2: 0} if bases else {},
        compiler_params=params(),
        cost_estimate=LIGHT,
    )(pos, inverse, *bases, *arrays)


def inverse_factor(gram):
    size = gram.shape[0]
    groups = size // GROUP
    shape = (GROUP, size)
    sub = lax.broadcasted_iota(jnp.int32, shape, 0)
    lane = lax.broadcasted_iota(jnp.int32, shape, 1)
    left = [gram[GROUP * i : GROUP * (i + 1)] for i in range(groups)]
    right = [jnp.where(sub + GROUP * i == lane, 1.0, 0.0).astype(F32) for i in range(groups)]
    for g in range(groups):
        first = g * GROUP
        wide = lambda value: jnp.broadcast_to(value, shape)
        rows = [wide(left[g][t : t + 1]) for t in range(GROUP)]
        inverse_rows = [wide(right[g][t : t + 1]) for t in range(GROUP)]
        block = [
            [wide(left[g][t : t + 1, first + u : first + u + 1]) for u in range(GROUP)]
            for t in range(GROUP)
        ]
        below = range(g + 1, groups)
        columns = {
            i: [wide(left[i][:, first + u : first + u + 1]) for u in range(GROUP)] for i in below
        }
        scaled = []
        for t in range(GROUP):
            pivot = 1.0 / block[t][t]
            scaled.append((rows[t] * pivot, inverse_rows[t] * pivot))
            for u in range(t + 1, GROUP):
                factor = block[t][u] * pivot
                for w in range(u, GROUP):
                    block[u][w] = block[u][w] - factor * block[t][w]
                rows[u] = rows[u] - factor * rows[t]
                inverse_rows[u] = inverse_rows[u] - factor * inverse_rows[t]
                for i in below:
                    columns[i][u] = columns[i][u] - factor * columns[i][t]
        for i in below:
            for t in range(GROUP):
                left[i] = left[i] - columns[i][t] * scaled[t][0]
                right[i] = right[i] - columns[i][t] * scaled[t][1]
        for t in range(GROUP):
            left[g] = jnp.where(sub == t, rows[t], left[g])
            right[g] = jnp.where(sub == t, inverse_rows[t], right[g])
    out = []
    for g in range(groups):
        pivots = jnp.sum(
            jnp.where(sub + GROUP * g == lane, left[g], 0.0), axis=1, keepdims=True
        )
        out.append(right[g] * lax.rsqrt(pivots))
    return jnp.concatenate(out)


def times_transpose(value, inverse):
    return lax.dot_general(
        value, inverse, (((1,), (1,)), ((), ())), precision=HIGHEST, preferred_element_type=F32
    )


def scores_kernel(with_factor, lengths_ref, subjects_ref, pos_ref, mine_ref, other_ref, *refs):
    out_ref = refs[-1]
    length = lengths_ref[subjects_ref[pos_ref[1] * LOW + pos_ref[0]]]
    mine, other = mine_ref[...], other_ref[...]
    lower = pos_ref[2] == 0
    scores = jnp.concatenate([jnp.where(lower, mine, other), jnp.where(lower, other, mine)])
    if with_factor:
        scores = times_transpose(scores, refs[0][...])
    live = lax.broadcasted_iota(jnp.int32, scores.shape, 0) < length
    out_ref[...] = jnp.where(live, scores, 0.0).astype(BF16)


def invert_kernel(all_voxels, *refs):
    terms = [ref[...] for ref in refs[:-1]]
    while len(terms) > 1:
        terms = [terms[i] + terms[i + 1] for i in range(0, len(terms), 2)]
    refs[-1][...] = inverse_factor(terms[0] * (1.0 / all_voxels))


def make(mesh):
    subjects, blocks = mesh.shape["subj"], mesh.shape["vox"]
    swap = functools.partial(exchange, axis="subj", size=subjects)
    swap_vox = functools.partial(exchange, axis="vox", size=blocks)

    def on_device(scans, test_matrix, lengths, block_subject):
        time_rows, voxels = scans.shape
        rank = test_matrix.shape[1]
        all_voxels = voxels * blocks
        layout = Layout(voxels, subjects)
        high = layout.high
        ks = list(range(high))
        me = lax.axis_index("subj")
        core = lax.axis_index("vox") % 2
        pos = jnp.stack([me % LOW, me // LOW, core]).astype(jnp.int32)

        def sketch_sum(scores, code):
            def part(after, j, ks, apart, per_step):
                ordered = scores if after is None else lax.optimization_barrier((scores, after))[0]
                return sketch_part(
                    scans, layout, pos, ordered, j, ks, code, apart, per_step
                )

            away = part(None, 1, ks, False, high // 2)
            got_away = swap(away, mask=1)
            second = part(away, None, ks[1:], True, high - 1)
            got_second = [swap(second[k - 1], mask=k * LOW) for k in ks[1:]]
            home = part(second[0], 0, ks, False, high // 2)
            (second_own,) = part(second[0], None, ks[:1], True, 1)
            got_away, got_second, home, second_own = lax.optimization_barrier(
                (got_away, got_second, home, second_own)
            )
            piece = jax.ShapeDtypeStruct((layout.single + code.pad, rank), code.dtype)
            first = small_call(
                functools.partial(add_pieces_kernel, code, high), [piece] * high, home, got_away
            )
            got_first = [swap(first[k], mask=k * LOW) for k in ks[1:]]

            half = jax.ShapeDtypeStruct((layout.pair // 2 + code.pad, rank), code.dtype)
            keep, send = pl.pallas_call(
                functools.partial(add_halves_kernel, code),
                out_shape=[half, half],
                in_specs=[pl.BlockSpec(memory_space=pltpu.SMEM)] + [WHOLE] * high,
                out_specs=[WHOLE, WHOLE],
                compiler_params=params(),
                cost_estimate=LIGHT,
            )(pos, second_own, *got_second)
            got_send = swap(send, mask=1)
            return (
                add_all(code, [first[0], *got_first]),
                add_all(code, [keep, got_send]),
            )

        def gather(first, second, gram):
            gram = gram + swap_vox(gram, mask=1)
            first, second, gram = lax.optimization_barrier((first, second, gram))
            pieces = [swap(first, mask=k * LOW) for k in ks[1:]]
            got = swap(second, mask=1)
            lower = pos[0] == 0
            pair = jnp.stack([jnp.where(lower, second, got), jnp.where(lower, got, second)])
            mask = 2
            while mask < blocks:
                gram = gram + swap_vox(gram, mask=mask)
                mask *= 2
            gram = gram + swap(gram, mask=1)
            pieces, pair, gram = lax.optimization_barrier((pieces, pair, gram))
            near, far = ks[: high // 2], ks[high // 2 :]
            low_near = swap(jnp.stack([first] + pieces[: len(near) - 1]), mask=1)
            low_far = swap(jnp.stack(pieces[len(near) - 1 :]), mask=1)
            grams = [gram] + [swap(gram, mask=k * LOW) for k in ks[1:]]
            pair, grams = lax.optimization_barrier((pair, grams))
            seconds = [pair] + [swap(pair, mask=k * LOW) for k in ks[1:]]
            early = [(0, [k], array) for k, array in zip(ks, [first] + pieces)]
            pairs = [(None, [k], array) for k, array in zip(ks, seconds)]
            return early, (1, near, low_near), (1, far, low_far), pairs, grams

        def sum_scores(mine, send, *factor):
            mine = mine + swap_vox(send, mask=1)
            mask = 2
            while mask < blocks:
                mine = mine + swap_vox(mine, mask=mask)
                mask *= 2
            other = swap_vox(mine, mask=1)
            return pl.pallas_call(
                functools.partial(scores_kernel, bool(factor)),
                out_shape=jax.ShapeDtypeStruct((time_rows, rank), BF16),
                in_specs=[pl.BlockSpec(memory_space=pltpu.SMEM)] * 3
                + [WHOLE] * (2 + len(factor)),
                out_specs=WHOLE,
                compiler_params=params(),
                cost_estimate=LIGHT,
            )(lengths, block_subject, pos, mine, other, *factor)

        def pass_over(scores, code):
            (first, gram_first), (second, gram_second) = sketch_sum(scores, code)
            early, near, far, pairs, grams = gather(first, second, gram_first + gram_second)
            inverse = small_call(
                functools.partial(invert_kernel, all_voxels),
                jax.ShapeDtypeStruct((rank, rank), F32), *grams,
            )
            return early, near, [far] + pairs, inverse

        scores = sum_scores(*first_project(scans, pos, test_matrix))
        early, near, last, inverse = pass_over(scores, Plain)
        last = last[:1] + [(j, k, array.reshape(-1, rank)) for j, k, array in last[1:]]
        total = project(scans, layout, pos, early)
        total = project(scans, layout, pos, [near], total)
        total, inverse = lax.optimization_barrier((total, inverse))
        scores = sum_scores(*project(scans, layout, pos, last, total, True), inverse)
        early, near, last, inverse = pass_over(scores, Fixed)
        out = finish(layout, pos, early + [near], inverse, voxels)
        return finish(layout, pos, last, inverse, voxels, out)

    return on_device


def solution(mesh):
    placed = (P("subj", "vox"), P("vox", None), P(), P())
    return jax.shard_map(
        make(mesh), mesh=mesh, in_specs=placed, out_specs=P("vox", None), check_vma=False
    )
```

```python
import functools

import jax
import jax.numpy as jnp
from jax import lax
from jax.experimental import pallas as pl
from jax.experimental.pallas import tpu as pltpu
from jax.sharding import PartitionSpec as P

F32 = jnp.float32
BF16 = jnp.bfloat16
I16 = jnp.int16
HIGHEST = lax.Precision.HIGHEST
STEPS = 64.0
LOW = 2
GROUP = 8
LANES = 128
VMEM_BYTES = 48 << 20
LIGHT = pl.CostEstimate(flops=1, bytes_accessed=1, transcendentals=0)
WHOLE = pl.BlockSpec(memory_space=pltpu.VMEM)


def exchange(value, axis, size, mask):
    return lax.ppermute(value, axis, [(i, i ^ mask) for i in range(size)])


class Plain:
    pad = 0
    dtype = BF16

    @staticmethod
    def encode(value):
        return value.astype(BF16)

    @staticmethod
    def decode(sent):
        return sent.astype(F32)


class Fixed:
    pad = 16
    dtype = I16

    @staticmethod
    def encode(value):
        top = jnp.maximum(jnp.max(jnp.abs(value), axis=0, keepdims=True), 1e-30)
        power = jnp.ceil(jnp.log2(top * (1.0 / 32000.0)) * STEPS)
        codes = jnp.round(value * jnp.exp2(power * (-1.0 / STEPS)))
        codes = jnp.clip(codes, -32767.0, 32767.0)
        rows = jnp.broadcast_to(power, (Fixed.pad, value.shape[1]))
        return jnp.concatenate([codes, rows]).astype(jnp.int32).astype(I16)

    @staticmethod
    def decode(sent):
        wide = sent.astype(jnp.int32).astype(F32)
        rows = wide.shape[0] - Fixed.pad
        return wide[:rows] * jnp.exp2(wide[rows : rows + 1] * (1.0 / STEPS))


def params():
    return pltpu.CompilerParams(vmem_limit_bytes=VMEM_BYTES)


class Layout:
    def __init__(self, voxels, subjects):
        self.high = subjects // LOW
        unit = subjects * LANES
        for top, bottom in ((2, 3), (1, 2)):
            self.cut = voxels * top // bottom
            self.pair = (voxels - self.cut) // self.high
            if self.cut % unit == 0 and voxels % unit == 0 and self.cut % self.pair == 0:
                break
        self.single = self.cut // subjects

    def columns(self, j):
        return self.pair if j is None else self.single

    def block(self, j, k, pos):
        if j is None:
            return self.cut // self.pair + (pos[1] ^ k)
        return (pos[0] ^ j) * self.high + (pos[1] ^ k)


def sketch_kernel(code, apart, count, pos_ref, scores_ref, *refs):
    for u in range(count):
        product = lax.dot_general(
            scores_ref[...], refs[u][...], (((0,), (0,)), ((), ())), preferred_element_type=F32
        )
        out = refs[count + u] if apart else refs[count].at[u]
        out[...] = code.encode(product.T)


def sketch_part(scans, layout, pos, scores, j, ks, code, apart, per_step):
    time_rows = scans.shape[0]
    rank = scores.shape[1]
    n = layout.columns(j)
    rows = n + code.pad
    steps = len(ks) // per_step

    def column(u):
        return lambda g, pos: (0, layout.block(j, ks[0] + g * per_step + u, pos))

    if apart:
        out_shape = [jax.ShapeDtypeStruct((rows, rank), code.dtype)] * len(ks)
        out_specs = [pl.BlockSpec((rows, rank), lambda g, pos: (0, 0))] * len(ks)
    else:
        out_shape = jax.ShapeDtypeStruct((len(ks), rows, rank), code.dtype)
        out_specs = pl.BlockSpec((per_step, rows, rank), lambda g, pos: (g, 0, 0))
    return pl.pallas_call(
        functools.partial(sketch_kernel, code, apart, per_step),
        out_shape=out_shape,
        grid_spec=pltpu.PrefetchScalarGridSpec(
            num_scalar_prefetch=1,
            grid=(steps,),
            in_specs=[pl.BlockSpec((time_rows, rank), lambda g, pos: (0, 0))]
            + [pl.BlockSpec((time_rows, n), column(u)) for u in range(per_step)],
            out_specs=out_specs,
        ),
        compiler_params=params(),
        cost_estimate=LIGHT,
    )(pos, scores, *([scans] * per_step))


def small_call(kernel, out_shape, *args):
    return pl.pallas_call(
        kernel,
        out_shape=out_shape,
        in_specs=[WHOLE] * len(args),
        out_specs=jax.tree.map(lambda _: WHOLE, out_shape),
        compiler_params=params(),
        cost_estimate=LIGHT,
    )(*args)


def add_pieces_kernel(code, count, own_ref, got_ref, *outs):
    for k in range(count):
        outs[k][...] = code.encode(code.decode(own_ref[k]) + code.decode(got_ref[k]))


def add_all_kernel(code, *refs):
    parts, outs = refs[:-2], refs[-2:]
    total = code.decode(parts[0][...])
    for part in parts[1:]:
        total = total + code.decode(part[...])
    outs[0][...] = code.encode(total)
    outs[1][...] = lax.dot_general(
        total, total, (((0,), (0,)), ((), ())), precision=HIGHEST, preferred_element_type=F32
    )


def add_halves_kernel(code, pos_ref, *refs):
    parts, (keep_ref, send_ref) = refs[:-2], refs[-2:]
    total = code.decode(parts[0][...])
    for part in parts[1:]:
        total = total + code.decode(part[...])
    half = total.shape[0] // 2
    lower = pos_ref[0] == 0
    keep_ref[...] = code.encode(jnp.where(lower, total[:half], total[half:]))
    send_ref[...] = code.encode(jnp.where(lower, total[half:], total[:half]))


def add_all(code, parts):
    rank = parts[0].shape[1]
    out = [jax.ShapeDtypeStruct(parts[0].shape, code.dtype)]
    out.append(jax.ShapeDtypeStruct((rank, rank), F32))
    return small_call(functools.partial(add_all_kernel, code), out, *parts)


def write_halves(pos_ref, value, outs):
    half = value.shape[0] // 2
    lower = pos_ref[2] == 0
    outs[0][...] = jnp.where(lower, value[:half], value[half:])
    outs[1][...] = jnp.where(lower, value[half:], value[:half])


def first_kernel(count, pos_ref, panel_ref, *refs):
    scans, outs, total = refs[:count], refs[count:-1], refs[-1]
    n = scans[0].shape[1]
    g = pl.program_id(0)

    @pl.when(g == 0)
    def _():
        total[...] = jnp.zeros_like(total)

    for u in range(count):
        panel = panel_ref[u * n : (u + 1) * n]
        total[...] += jnp.dot(scans[u][...], panel, preferred_element_type=F32)

    @pl.when(g == pl.num_programs(0) - 1)
    def _():
        write_halves(pos_ref, total[...], outs)


def first_project(scans, pos, panel, steps=3, count=4):
    time_rows, voxels = scans.shape
    rank = panel.shape[1]
    n = voxels // (steps * count)
    half = jax.ShapeDtypeStruct((time_rows // 2, rank), F32)

    def column(u):
        return lambda g, pos: (0, g * count + u)

    return pl.pallas_call(
        functools.partial(first_kernel, count),
        out_shape=[half, half],
        grid_spec=pltpu.PrefetchScalarGridSpec(
            num_scalar_prefetch=1,
            grid=(steps,),
            in_specs=[pl.BlockSpec((count * n, rank), lambda g, pos: (g, 0))]
            + [pl.BlockSpec((time_rows, n), column(u)) for u in range(count)],
            out_specs=[pl.BlockSpec(half.shape, lambda g, pos: (0, 0))] * 2,
            scratch_shapes=[pltpu.VMEM((time_rows, rank), F32)],
        ),
        compiler_params=params(),
        cost_estimate=LIGHT,
    )(pos, panel, *([scans] * count))


def project_kernel(has_base, split, items, pos_ref, *refs):
    refs = list(refs)
    base = refs.pop(0) if has_base else None
    outs = [refs.pop() for _ in range(2 if split else 1)][::-1]
    scans, pieces = refs[: len(items)], refs[len(items) :]
    time_rows = scans[0].shape[0]
    rank = outs[0].shape[1]
    total = jnp.zeros((time_rows, rank), F32)
    for scan, (source, index) in zip(scans, items):
        piece = pieces[source][...] if index is None else pieces[source][index]
        total += jnp.dot(scan[...], piece, preferred_element_type=F32)
    if has_base:
        total += base[...]
    if split:
        write_halves(pos_ref, total, outs)
    else:
        outs[0][...] = total


def project(scans, layout, pos, groups, base=None, split=False):
    time_rows = scans.shape[0]
    rank = groups[0][2].shape[-1]
    items, names = [], []
    for source, (j, ks, array) in enumerate(groups):
        for i, k in enumerate(ks):
            items.append((source, None if array.ndim == 2 else i))
            names.append((j, k))

    def column(j, k):
        return lambda g, pos: (0, layout.block(j, k, pos))

    full = lambda shape: pl.BlockSpec(shape, lambda g, pos: (0,) * len(shape))
    bases = [] if base is None else [base]
    arrays = [array for _, _, array in groups]
    shape = (time_rows // 2, rank) if split else (time_rows, rank)
    out_shape = [jax.ShapeDtypeStruct(shape, F32)] * (2 if split else 1)
    out = pl.pallas_call(
        functools.partial(project_kernel, base is not None, split, items),
        out_shape=out_shape,
        grid_spec=pltpu.PrefetchScalarGridSpec(
            num_scalar_prefetch=1,
            grid=(1,),
            in_specs=[full(b.shape) for b in bases]
            + [pl.BlockSpec((time_rows, layout.columns(j)), column(j, k)) for j, k in names]
            + [full(p.shape) for p in arrays],
            out_specs=[full(shape)] * len(out_shape),
        ),
        compiler_params=params(),
        cost_estimate=LIGHT,
    )(pos, *bases, *([scans] * len(items)), *arrays)
    return out if split else out[0]


def finish_kernel(layout, items, has_base, pos_ref, inverse_ref, *refs):
    refs, (out, held, sems) = refs[:-3], refs[-3:]
    if has_base:
        refs = refs[1:]
    copies = []
    used = 0
    pos = (pos_ref[0], pos_ref[1])
    for number, (source, index, j, k) in enumerate(items):
        n = layout.columns(j)
        codes = refs[source][...] if index is None else refs[source][index]
        if j is None:
            value = jnp.concatenate([Fixed.decode(codes[side]) for side in range(LOW)])
        else:
            value = Fixed.decode(codes)
        rows = pl.ds(used, n)
        held[rows] = times_transpose(value, inverse_ref[...])
        used += n
        start = pl.multiple_of(layout.block(j, k, pos) * n, n)
        copy = pltpu.make_async_copy(held.at[rows], out.at[pl.ds(start, n)], sems.at[number])
        copy.start()
        copies.append(copy)
    for copy in copies:
        copy.wait()


def finish(layout, pos, groups, inverse, voxels, base=None):
    rank = inverse.shape[0]
    items = []
    for source, (j, ks, array) in enumerate(groups):
        alone = array.ndim == (2 if j is not None else 3)
        for i, k in enumerate(ks):
            items.append((source, None if alone else i, j, k))
    columns = sum(layout.columns(j) for _, _, j, _ in items)
    bases = [] if base is None else [base]
    arrays = [array for _, _, array in groups]
    return pl.pallas_call(
        functools.partial(finish_kernel, layout, items, base is not None),
        out_shape=jax.ShapeDtypeStruct((voxels, rank), F32),
        in_specs=[pl.BlockSpec(memory_space=pltpu.SMEM), WHOLE]
        + [pl.BlockSpec(memory_space=pl.ANY)] * len(bases)
        + [WHOLE] * len(arrays),
        out_specs=pl.BlockSpec(memory_space=pl.ANY),
        scratch_shapes=[
            pltpu.VMEM((columns, rank), F32),
            pltpu.SemaphoreType.DMA((len(items),)),
        ],
        input_output_aliases={2: 0} if bases else {},
        compiler_params=params(),
        cost_estimate=LIGHT,
    )(pos, inverse, *bases, *arrays)


def inverse_factor(gram):
    size = gram.shape[0]
    groups = size // GROUP
    shape = (GROUP, size)
    sub = lax.broadcasted_iota(jnp.int32, shape, 0)
    lane = lax.broadcasted_iota(jnp.int32, shape, 1)
    left = [gram[GROUP * i : GROUP * (i + 1)] for i in range(groups)]
    right = [jnp.where(sub + GROUP * i == lane, 1.0, 0.0).astype(F32) for i in range(groups)]
    for g in range(groups):
        first = g * GROUP
        wide = lambda value: jnp.broadcast_to(value, shape)
        rows = [wide(left[g][t : t + 1]) for t in range(GROUP)]
        inverse_rows = [wide(right[g][t : t + 1]) for t in range(GROUP)]
        block = [
            [wide(left[g][t : t + 1, first + u : first + u + 1]) for u in range(GROUP)]
            for t in range(GROUP)
        ]
        below = range(g + 1, groups)
        columns = {
            i: [wide(left[i][:, first + u : first + u + 1]) for u in range(GROUP)] for i in below
        }
        scaled = []
        for t in range(GROUP):
            pivot = 1.0 / block[t][t]
            scaled.append((rows[t] * pivot, inverse_rows[t] * pivot))
            for u in range(t + 1, GROUP):
                factor = block[t][u] * pivot
                for w in range(u, GROUP):
                    block[u][w] = block[u][w] - factor * block[t][w]
                rows[u] = rows[u] - factor * rows[t]
                inverse_rows[u] = inverse_rows[u] - factor * inverse_rows[t]
                for i in below:
                    columns[i][u] = columns[i][u] - factor * columns[i][t]
        for i in below:
            for t in range(GROUP):
                left[i] = left[i] - columns[i][t] * scaled[t][0]
                right[i] = right[i] - columns[i][t] * scaled[t][1]
        for t in range(GROUP):
            left[g] = jnp.where(sub == t, rows[t], left[g])
            right[g] = jnp.where(sub == t, inverse_rows[t], right[g])
    out = []
    for g in range(groups):
        pivots = jnp.sum(
            jnp.where(sub + GROUP * g == lane, left[g], 0.0), axis=1, keepdims=True
        )
        out.append(right[g] * lax.rsqrt(pivots))
    return jnp.concatenate(out)


def times_transpose(value, inverse):
    return lax.dot_general(
        value, inverse, (((1,), (1,)), ((), ())), precision=HIGHEST, preferred_element_type=F32
    )


def scores_kernel(with_factor, lengths_ref, subjects_ref, pos_ref, mine_ref, other_ref, *refs):
    out_ref = refs[-1]
    length = lengths_ref[subjects_ref[pos_ref[1] * LOW + pos_ref[0]]]
    mine, other = mine_ref[...], other_ref[...]
    lower = pos_ref[2] == 0
    scores = jnp.concatenate([jnp.where(lower, mine, other), jnp.where(lower, other, mine)])
    if with_factor:
        scores = times_transpose(scores, refs[0][...])
    live = lax.broadcasted_iota(jnp.int32, scores.shape, 0) < length
    out_ref[...] = jnp.where(live, scores, 0.0).astype(BF16)


def invert_kernel(all_voxels, *refs):
    terms = [ref[...] for ref in refs[:-1]]
    while len(terms) > 1:
        terms = [terms[i] + terms[i + 1] for i in range(0, len(terms), 2)]
    refs[-1][...] = inverse_factor(terms[0] * (1.0 / all_voxels))


def make(mesh):
    subjects, blocks = mesh.shape["subj"], mesh.shape["vox"]
    swap = functools.partial(exchange, axis="subj", size=subjects)
    swap_vox = functools.partial(exchange, axis="vox", size=blocks)

    def on_device(scans, test_matrix, lengths, block_subject):
        time_rows, voxels = scans.shape
        rank = test_matrix.shape[1]
        all_voxels = voxels * blocks
        layout = Layout(voxels, subjects)
        high = layout.high
        ks = list(range(high))
        me = lax.axis_index("subj")
        core = lax.axis_index("vox") % 2
        pos = jnp.stack([me % LOW, me // LOW, core]).astype(jnp.int32)

        def sketch_sum(scores, code):
            def part(after, j, ks, apart, per_step):
                ordered = scores if after is None else lax.optimization_barrier((scores, after))[0]
                return sketch_part(
                    scans, layout, pos, ordered, j, ks, code, apart, per_step
                )

            away = part(None, 1, ks, False, high // 2)
            got_away = swap(away, mask=1)
            second = part(away, None, ks[1:], True, high - 1)
            got_second = [swap(second[k - 1], mask=k * LOW) for k in ks[1:]]
            home = part(second[0], 0, ks, False, high // 2)
            (second_own,) = part(second[0], None, ks[:1], True, 1)
            got_away, got_second, home, second_own = lax.optimization_barrier(
                (got_away, got_second, home, second_own)
            )
            piece = jax.ShapeDtypeStruct((layout.single + code.pad, rank), code.dtype)
            first = small_call(
                functools.partial(add_pieces_kernel, code, high), [piece] * high, home, got_away
            )
            got_first = [swap(first[k], mask=k * LOW) for k in ks[1:]]

            half = jax.ShapeDtypeStruct((layout.pair // 2 + code.pad, rank), code.dtype)
            keep, send = pl.pallas_call(
                functools.partial(add_halves_kernel, code),
                out_shape=[half, half],
                in_specs=[pl.BlockSpec(memory_space=pltpu.SMEM)] + [WHOLE] * high,
                out_specs=[WHOLE, WHOLE],
                compiler_params=params(),
                cost_estimate=LIGHT,
            )(pos, second_own, *got_second)
            got_send = swap(send, mask=1)
            return (
                add_all(code, [first[0], *got_first]),
                add_all(code, [keep, got_send]),
            )

        def gather(first, second, gram, gram_last):
            gram = gram + swap_vox(gram, mask=1)
            first, second, gram = lax.optimization_barrier((first, second, gram))
            pieces = [swap(first, mask=k * LOW) for k in ks[1:]]
            got = swap(second, mask=1)
            lower = pos[0] == 0
            pair = jnp.stack([jnp.where(lower, second, got), jnp.where(lower, got, second)])
            mask = 2
            while mask < blocks:
                gram = gram + swap_vox(gram, mask=mask)
                mask *= 2
            gram = gram + swap(gram, mask=1)
            pieces, pair, gram = lax.optimization_barrier((pieces, pair, gram))
            near, far = ks[: high // 2], ks[high // 2 :]
            low_near = swap(jnp.stack([first] + pieces[: len(near) - 1]), mask=1)
            low_far = swap(jnp.stack(pieces[len(near) - 1 :]), mask=1)
            if not gram_last:
                grams = [gram] + [swap(gram, mask=k * LOW) for k in ks[1:]]
                pair, grams = lax.optimization_barrier((pair, grams))
            seconds = [pair] + [swap(pair, mask=k * LOW) for k in ks[1:]]
            if gram_last:
                seconds, gram = lax.optimization_barrier((seconds, gram))
                grams = [gram] + [swap(gram, mask=k * LOW) for k in ks[1:]]
            early = [(0, [k], array) for k, array in zip(ks, [first] + pieces)]
            pairs = [(None, [k], array) for k, array in zip(ks, seconds)]
            return early, (1, near, low_near), (1, far, low_far), pairs, grams

        def invert(grams):
            return small_call(
                functools.partial(invert_kernel, all_voxels),
                jax.ShapeDtypeStruct((rank, rank), F32), *grams,
            )

        def sum_scores(mine, send, grams=None):
            mine = mine + swap_vox(send, mask=1)
            factor = []
            if grams is not None:
                mine, grams = lax.optimization_barrier((mine, grams))
                factor = [invert(grams)]
            mask = 2
            while mask < blocks:
                mine = mine + swap_vox(mine, mask=mask)
                mask *= 2
            other = swap_vox(mine, mask=1)
            return pl.pallas_call(
                functools.partial(scores_kernel, bool(factor)),
                out_shape=jax.ShapeDtypeStruct((time_rows, rank), BF16),
                in_specs=[pl.BlockSpec(memory_space=pltpu.SMEM)] * 3
                + [WHOLE] * (2 + len(factor)),
                out_specs=WHOLE,
                compiler_params=params(),
                cost_estimate=LIGHT,
            )(lengths, block_subject, pos, mine, other, *factor)

        def pass_over(scores, code, gram_last):
            (first, gram_first), (second, gram_second) = sketch_sum(scores, code)
            return gather(first, second, gram_first + gram_second, gram_last)

        scores = sum_scores(*first_project(scans, pos, test_matrix))
        early, near, far, pairs, grams = pass_over(scores, Plain, True)
        pairs = [(j, k, array.reshape(-1, rank)) for j, k, array in pairs]
        total = project(scans, layout, pos, early)
        total = project(scans, layout, pos, [near], total)
        total = project(scans, layout, pos, [far], total)
        scores = sum_scores(*project(scans, layout, pos, pairs, total, True), grams)
        early, near, far, pairs, grams = pass_over(scores, Fixed, False)
        inverse = invert(grams)
        out = finish(layout, pos, early + [near], inverse, voxels)
        return finish(layout, pos, [far] + pairs, inverse, voxels, out)

    return on_device


def solution(mesh):
    placed = (P("subj", "vox"), P("vox", None), P(), P())
    return jax.shard_map(
        make(mesh), mesh=mesh, in_specs=placed, out_specs=P("vox", None), check_vma=False
    )
```

```python
import functools

import jax
import jax.numpy as jnp
from jax import lax
from jax.experimental import pallas as pl
from jax.experimental.pallas import tpu as pltpu
from jax.sharding import PartitionSpec as P

F32 = jnp.float32
BF16 = jnp.bfloat16
I16 = jnp.int16
HIGHEST = lax.Precision.HIGHEST
STEPS = 64.0
LOW = 2
GROUP = 8
SYNC_ROWS = 16
LANES = 128
VMEM_BYTES = 48 << 20
LIGHT = pl.CostEstimate(flops=1, bytes_accessed=1, transcendentals=0)
WHOLE = pl.BlockSpec(memory_space=pltpu.VMEM)


def exchange(value, axis, size, mask):
    return lax.ppermute(value, axis, [(i, i ^ mask) for i in range(size)])


class Plain:
    pad = 0
    dtype = BF16

    @staticmethod
    def encode(value):
        return value.astype(BF16)

    @staticmethod
    def decode(sent):
        return sent.astype(F32)


class Fixed:
    pad = 16
    dtype = I16

    @staticmethod
    def encode(value):
        top = jnp.maximum(jnp.max(jnp.abs(value), axis=0, keepdims=True), 1e-30)
        power = jnp.ceil(jnp.log2(top * (1.0 / 32000.0)) * STEPS)
        codes = jnp.round(value * jnp.exp2(power * (-1.0 / STEPS)))
        codes = jnp.clip(codes, -32767.0, 32767.0)
        rows = jnp.broadcast_to(power, (Fixed.pad, value.shape[1]))
        return jnp.concatenate([codes, rows]).astype(jnp.int32).astype(I16)

    @staticmethod
    def decode(sent):
        wide = sent.astype(jnp.int32).astype(F32)
        rows = wide.shape[0] - Fixed.pad
        return wide[:rows] * jnp.exp2(wide[rows : rows + 1] * (1.0 / STEPS))


def params():
    return pltpu.CompilerParams(vmem_limit_bytes=VMEM_BYTES)


class Layout:
    def __init__(self, voxels, subjects):
        self.high = subjects // LOW
        unit = subjects * LANES
        for top, bottom in ((2, 3), (1, 2)):
            self.cut = voxels * top // bottom
            self.pair = (voxels - self.cut) // self.high
            if self.cut % unit == 0 and voxels % unit == 0 and self.cut % self.pair == 0:
                break
        self.single = self.cut // subjects

    def columns(self, j):
        return self.pair if j is None else self.single

    def block(self, j, k, pos):
        if j is None:
            return self.cut // self.pair + (pos[1] ^ k)
        return (pos[0] ^ j) * self.high + (pos[1] ^ k)


def sketch_kernel(code, apart, count, pos_ref, scores_ref, *refs):
    for u in range(count):
        product = lax.dot_general(
            scores_ref[...], refs[u][...], (((0,), (0,)), ((), ())), preferred_element_type=F32
        )
        out = refs[count + u] if apart else refs[count].at[u]
        out[...] = code.encode(product.T)


def sketch_part(scans, layout, pos, scores, j, ks, code, apart, per_step):
    time_rows = scans.shape[0]
    rank = scores.shape[1]
    n = layout.columns(j)
    rows = n + code.pad
    steps = len(ks) // per_step

    def column(u):
        return lambda g, pos: (0, layout.block(j, ks[0] + g * per_step + u, pos))

    if apart:
        out_shape = [jax.ShapeDtypeStruct((rows, rank), code.dtype)] * len(ks)
        out_specs = [pl.BlockSpec((rows, rank), lambda g, pos: (0, 0))] * len(ks)
    else:
        out_shape = jax.ShapeDtypeStruct((len(ks), rows, rank), code.dtype)
        out_specs = pl.BlockSpec((per_step, rows, rank), lambda g, pos: (g, 0, 0))
    return pl.pallas_call(
        functools.partial(sketch_kernel, code, apart, per_step),
        out_shape=out_shape,
        grid_spec=pltpu.PrefetchScalarGridSpec(
            num_scalar_prefetch=1,
            grid=(steps,),
            in_specs=[pl.BlockSpec((time_rows, rank), lambda g, pos: (0, 0))]
            + [pl.BlockSpec((time_rows, n), column(u)) for u in range(per_step)],
            out_specs=out_specs,
        ),
        compiler_params=params(),
        cost_estimate=LIGHT,
    )(pos, scores, *([scans] * per_step))


def small_call(kernel, out_shape, *args):
    return pl.pallas_call(
        kernel,
        out_shape=out_shape,
        in_specs=[WHOLE] * len(args),
        out_specs=jax.tree.map(lambda _: WHOLE, out_shape),
        compiler_params=params(),
        cost_estimate=LIGHT,
    )(*args)


def add_pieces_kernel(code, count, own_ref, got_ref, *outs):
    for k in range(count):
        outs[k][...] = code.encode(code.decode(own_ref[k]) + code.decode(got_ref[k]))


def add_all_kernel(code, *refs):
    parts, outs = refs[:-2], refs[-2:]
    total = code.decode(parts[0][...])
    for part in parts[1:]:
        total = total + code.decode(part[...])
    outs[0][...] = code.encode(total)
    outs[1][...] = lax.dot_general(
        total, total, (((0,), (0,)), ((), ())), precision=HIGHEST, preferred_element_type=F32
    )


def add_halves_kernel(code, pos_ref, *refs):
    parts, (keep_ref, send_ref) = refs[:-2], refs[-2:]
    total = code.decode(parts[0][...])
    for part in parts[1:]:
        total = total + code.decode(part[...])
    half = total.shape[0] // 2
    lower = pos_ref[0] == 0
    keep_ref[...] = code.encode(jnp.where(lower, total[:half], total[half:]))
    send_ref[...] = code.encode(jnp.where(lower, total[half:], total[:half]))


def add_all(code, parts):
    rank = parts[0].shape[1]
    out = [jax.ShapeDtypeStruct(parts[0].shape, code.dtype)]
    out.append(jax.ShapeDtypeStruct((rank, rank), F32))
    return small_call(functools.partial(add_all_kernel, code), out, *parts)


def write_halves(pos_ref, value, outs):
    half = value.shape[0] // 2
    lower = pos_ref[2] == 0
    outs[0][...] = jnp.where(lower, value[:half], value[half:])
    outs[1][...] = jnp.where(lower, value[half:], value[:half])


def first_kernel(count, pos_ref, panel_ref, *refs):
    scans, outs, total = refs[:count], refs[count:-1], refs[-1]
    n = scans[0].shape[1]
    g = pl.program_id(0)

    @pl.when(g == 0)
    def _():
        total[...] = jnp.zeros_like(total)

    for u in range(count):
        panel = panel_ref[u * n : (u + 1) * n]
        total[...] += jnp.dot(scans[u][...], panel, preferred_element_type=F32)

    @pl.when(g == pl.num_programs(0) - 1)
    def _():
        write_halves(pos_ref, total[...], outs)


def first_project(scans, pos, panel, steps=3, count=4):
    time_rows, voxels = scans.shape
    rank = panel.shape[1]
    n = voxels // (steps * count)
    half = jax.ShapeDtypeStruct((time_rows // 2, rank), F32)

    def column(u):
        return lambda g, pos: (0, g * count + u)

    return pl.pallas_call(
        functools.partial(first_kernel, count),
        out_shape=[half, half],
        grid_spec=pltpu.PrefetchScalarGridSpec(
            num_scalar_prefetch=1,
            grid=(steps,),
            in_specs=[pl.BlockSpec((count * n, rank), lambda g, pos: (g, 0))]
            + [pl.BlockSpec((time_rows, n), column(u)) for u in range(count)],
            out_specs=[pl.BlockSpec(half.shape, lambda g, pos: (0, 0))] * 2,
            scratch_shapes=[pltpu.VMEM((time_rows, rank), F32)],
        ),
        compiler_params=params(),
        cost_estimate=LIGHT,
    )(pos, panel, *([scans] * count))


def project_kernel(has_base, has_after, split, items, pos_ref, *refs):
    refs = list(refs)
    base = refs.pop(0) if has_base else None
    if has_after:
        refs.pop(0)
    outs = [refs.pop() for _ in range(2 if split else 1)][::-1]
    scans, pieces = refs[: len(items)], refs[len(items) :]
    time_rows = scans[0].shape[0]
    rank = outs[0].shape[1]
    total = jnp.zeros((time_rows, rank), F32)
    gram = jnp.zeros((rank, rank), F32)
    for scan, (source, index) in zip(scans, items):
        piece = pieces[source][...] if index is None else pieces[source][index]
        total += jnp.dot(scan[...], piece, preferred_element_type=F32)
        gram += lax.dot_general(
            piece, piece, (((0,), (0,)), ((), ())), preferred_element_type=F32
        )
    if has_base:
        total += base[:time_rows]
        gram += base[time_rows:]
    if split:
        write_halves(pos_ref, jnp.concatenate([total, gram]), outs)
    else:
        outs[0][:time_rows] = total
        outs[0][time_rows:] = gram


def project(scans, layout, pos, groups, base=None, split=False, after=None):
    time_rows = scans.shape[0]
    rank = groups[0][2].shape[-1]
    items, names = [], []
    for source, (j, ks, array) in enumerate(groups):
        for i, k in enumerate(ks):
            items.append((source, None if array.ndim == 2 else i))
            names.append((j, k))

    def column(j, k):
        return lambda g, pos: (0, layout.block(j, k, pos))

    full = lambda shape: pl.BlockSpec(shape, lambda g, pos: (0,) * len(shape))
    bases = [] if base is None else [base]
    afters = [] if after is None else [after]
    arrays = [array for _, _, array in groups]
    rows = time_rows + rank
    shape = (rows // 2, rank) if split else (rows, rank)
    out_shape = [jax.ShapeDtypeStruct(shape, F32)] * (2 if split else 1)
    out = pl.pallas_call(
        functools.partial(project_kernel, base is not None, after is not None, split, items),
        out_shape=out_shape,
        grid_spec=pltpu.PrefetchScalarGridSpec(
            num_scalar_prefetch=1,
            grid=(1,),
            in_specs=[full(b.shape) for b in bases]
            + [pl.BlockSpec(memory_space=pl.ANY)] * len(afters)
            + [pl.BlockSpec((time_rows, layout.columns(j)), column(j, k)) for j, k in names]
            + [full(p.shape) for p in arrays],
            out_specs=[full(shape)] * len(out_shape),
        ),
        compiler_params=params(),
        cost_estimate=LIGHT,
    )(pos, *bases, *afters, *([scans] * len(items)), *arrays)
    return out if split else out[0]


def finish_kernel(layout, items, has_base, pos_ref, inverse_ref, *refs):
    refs, (out, held, sems) = refs[:-3], refs[-3:]
    if has_base:
        refs = refs[1:]
    copies = []
    used = 0
    pos = (pos_ref[0], pos_ref[1])
    for number, (source, index, j, k) in enumerate(items):
        n = layout.columns(j)
        codes = refs[source][...] if index is None else refs[source][index]
        if j is None:
            value = jnp.concatenate([Fixed.decode(codes[side]) for side in range(LOW)])
        else:
            value = Fixed.decode(codes)
        rows = pl.ds(used, n)
        held[rows] = times_transpose(value, inverse_ref[...])
        used += n
        start = pl.multiple_of(layout.block(j, k, pos) * n, n)
        copy = pltpu.make_async_copy(held.at[rows], out.at[pl.ds(start, n)], sems.at[number])
        copy.start()
        copies.append(copy)
    for copy in copies:
        copy.wait()


def finish(layout, pos, groups, inverse, voxels, base=None):
    rank = inverse.shape[0]
    items = []
    for source, (j, ks, array) in enumerate(groups):
        alone = array.ndim == (2 if j is not None else 3)
        for i, k in enumerate(ks):
            items.append((source, None if alone else i, j, k))
    columns = sum(layout.columns(j) for _, _, j, _ in items)
    bases = [] if base is None else [base]
    arrays = [array for _, _, array in groups]
    return pl.pallas_call(
        functools.partial(finish_kernel, layout, items, base is not None),
        out_shape=jax.ShapeDtypeStruct((voxels, rank), F32),
        in_specs=[pl.BlockSpec(memory_space=pltpu.SMEM), WHOLE]
        + [pl.BlockSpec(memory_space=pl.ANY)] * len(bases)
        + [WHOLE] * len(arrays),
        out_specs=pl.BlockSpec(memory_space=pl.ANY),
        scratch_shapes=[
            pltpu.VMEM((columns, rank), F32),
            pltpu.SemaphoreType.DMA((len(items),)),
        ],
        input_output_aliases={2: 0} if bases else {},
        compiler_params=params(),
        cost_estimate=LIGHT,
    )(pos, inverse, *bases, *arrays)


def inverse_factor(gram):
    size = gram.shape[0]
    groups = size // GROUP
    shape = (GROUP, size)
    sub = lax.broadcasted_iota(jnp.int32, shape, 0)
    lane = lax.broadcasted_iota(jnp.int32, shape, 1)
    left = [gram[GROUP * i : GROUP * (i + 1)] for i in range(groups)]
    right = [jnp.where(sub + GROUP * i == lane, 1.0, 0.0).astype(F32) for i in range(groups)]
    for g in range(groups):
        first = g * GROUP
        wide = lambda value: jnp.broadcast_to(value, shape)
        rows = [wide(left[g][t : t + 1]) for t in range(GROUP)]
        inverse_rows = [wide(right[g][t : t + 1]) for t in range(GROUP)]
        block = [
            [wide(left[g][t : t + 1, first + u : first + u + 1]) for u in range(GROUP)]
            for t in range(GROUP)
        ]
        below = range(g + 1, groups)
        columns = {
            i: [wide(left[i][:, first + u : first + u + 1]) for u in range(GROUP)] for i in below
        }
        scaled = []
        for t in range(GROUP):
            pivot = 1.0 / block[t][t]
            scaled.append((rows[t] * pivot, inverse_rows[t] * pivot))
            for u in range(t + 1, GROUP):
                factor = block[t][u] * pivot
                for w in range(u, GROUP):
                    block[u][w] = block[u][w] - factor * block[t][w]
                rows[u] = rows[u] - factor * rows[t]
                inverse_rows[u] = inverse_rows[u] - factor * inverse_rows[t]
                for i in below:
                    columns[i][u] = columns[i][u] - factor * columns[i][t]
        for i in below:
            for t in range(GROUP):
                left[i] = left[i] - columns[i][t] * scaled[t][0]
                right[i] = right[i] - columns[i][t] * scaled[t][1]
        for t in range(GROUP):
            left[g] = jnp.where(sub == t, rows[t], left[g])
            right[g] = jnp.where(sub == t, inverse_rows[t], right[g])
    out = []
    for g in range(groups):
        pivots = jnp.sum(
            jnp.where(sub + GROUP * g == lane, left[g], 0.0), axis=1, keepdims=True
        )
        out.append(right[g] * lax.rsqrt(pivots))
    return jnp.concatenate(out)


def times_transpose(value, inverse):
    return lax.dot_general(
        value, inverse, (((1,), (1,)), ((), ())), precision=HIGHEST, preferred_element_type=F32
    )


def scores_kernel(all_voxels, lengths_ref, subjects_ref, pos_ref, mine_ref, other_ref, out_ref):
    length = lengths_ref[subjects_ref[pos_ref[1] * LOW + pos_ref[0]]]
    time_rows = out_ref.shape[0]
    mine, other = mine_ref[...], other_ref[...]
    lower = pos_ref[2] == 0
    both = jnp.concatenate([jnp.where(lower, mine, other), jnp.where(lower, other, mine)])
    scores = both[:time_rows]
    if both.shape[0] > time_rows:
        inverse = inverse_factor(both[time_rows:] * (1.0 / all_voxels))
        scores = times_transpose(scores, inverse)
    live = lax.broadcasted_iota(jnp.int32, scores.shape, 0) < length
    out_ref[...] = jnp.where(live, scores, 0.0).astype(BF16)


def invert_kernel(all_voxels, *refs):
    terms = [ref[...] for ref in refs[:-1]]
    while len(terms) > 1:
        terms = [terms[i] + terms[i + 1] for i in range(0, len(terms), 2)]
    refs[-1][...] = inverse_factor(terms[0] * (1.0 / all_voxels))


def make(mesh):
    subjects, blocks = mesh.shape["subj"], mesh.shape["vox"]
    swap = functools.partial(exchange, axis="subj", size=subjects)
    swap_vox = functools.partial(exchange, axis="vox", size=blocks)

    def on_device(scans, test_matrix, lengths, block_subject):
        time_rows, voxels = scans.shape
        rank = test_matrix.shape[1]
        all_voxels = voxels * blocks
        layout = Layout(voxels, subjects)
        high = layout.high
        ks = list(range(high))
        near, far = ks[: high // 2], ks[high // 2 :]
        me = lax.axis_index("subj")
        core = lax.axis_index("vox") % 2
        pos = jnp.stack([me % LOW, me // LOW, core]).astype(jnp.int32)

        def sketch_sum(scores, code):
            def part(after, j, ks, apart, per_step):
                ordered = scores if after is None else lax.optimization_barrier((scores, after))[0]
                return sketch_part(
                    scans, layout, pos, ordered, j, ks, code, apart, per_step
                )

            away = part(None, 1, ks, False, high // 2)
            got_away = swap(away, mask=1)
            second = part(away, None, ks[1:], True, high - 1)
            got_second = [swap(second[k - 1], mask=k * LOW) for k in ks[1:]]
            home = part(second[0], 0, ks, False, high // 2)
            (second_own,) = part(second[0], None, ks[:1], True, 1)
            got_away, got_second, home, second_own = lax.optimization_barrier(
                (got_away, got_second, home, second_own)
            )
            piece = jax.ShapeDtypeStruct((layout.single + code.pad, rank), code.dtype)
            first = small_call(
                functools.partial(add_pieces_kernel, code, high), [piece] * high, home, got_away
            )
            got_first = [swap(first[k], mask=k * LOW) for k in ks[1:]]

            half = jax.ShapeDtypeStruct((layout.pair // 2 + code.pad, rank), code.dtype)
            keep, send = pl.pallas_call(
                functools.partial(add_halves_kernel, code),
                out_shape=[half, half],
                in_specs=[pl.BlockSpec(memory_space=pltpu.SMEM)] + [WHOLE] * high,
                out_specs=[WHOLE, WHOLE],
                compiler_params=params(),
                cost_estimate=LIGHT,
            )(pos, second_own, *got_second)
            got_send = swap(send, mask=1)
            return (
                add_all(code, [first[0], *got_first]),
                add_all(code, [keep, got_send]),
            )

        def gather(first, second, gram=None):
            meet = swap_vox(first[:SYNC_ROWS] if gram is None else gram, mask=1)
            first, second, meet = lax.optimization_barrier((first, second, meet))
            far_in = [swap(first, mask=k * LOW) for k in far]
            near_in = [first] + [swap(first, mask=k * LOW) for k in near[1:]]
            got = swap(second, mask=1)
            lower = pos[0] == 0
            pair = jnp.stack([jnp.where(lower, second, got), jnp.where(lower, got, second)])
            if gram is not None:
                gram = gram + meet
                mask = 2
                while mask < blocks:
                    gram = gram + swap_vox(gram, mask=mask)
                    mask *= 2
                gram = gram + swap(gram, mask=1)
            far_in, near_in, pair, gram = lax.optimization_barrier((far_in, near_in, pair, gram))
            low_near = swap(jnp.stack(near_in), mask=1)
            low_far = swap(jnp.stack(far_in), mask=1)
            if gram is not None:
                gram = [gram] + [swap(gram, mask=k * LOW) for k in ks[1:]]
            seconds = [pair] + [swap(pair, mask=k * LOW) for k in ks[1:]]
            early = [(0, [k], array) for k, array in zip(near + far, near_in + far_in)]
            late = [(1, near, low_near), (1, far, low_far)]
            pairs = [(None, [k], array) for k, array in zip(ks, seconds)]
            return early, late, pairs, meet if gram is None else gram

        def sum_scores(mine, send):
            mine = mine + swap_vox(send, mask=1)
            mask = 2
            while mask < blocks:
                mine = mine + swap_vox(mine, mask=mask)
                mask *= 2
            other = swap_vox(mine, mask=1)
            return pl.pallas_call(
                functools.partial(scores_kernel, all_voxels),
                out_shape=jax.ShapeDtypeStruct((time_rows, rank), BF16),
                in_specs=[pl.BlockSpec(memory_space=pltpu.SMEM)] * 3 + [WHOLE] * 2,
                out_specs=WHOLE,
                compiler_params=params(),
                cost_estimate=LIGHT,
            )(lengths, block_subject, pos, mine, other)

        scores = sum_scores(*first_project(scans, pos, test_matrix))
        (first, _), (second, _) = sketch_sum(scores, Plain)
        early, late, pairs, meet = gather(first, second)
        pairs = [(j, k, array.reshape(layout.pair, rank)) for j, k, array in pairs]
        total = project(scans, layout, pos, early, after=meet)
        total = project(scans, layout, pos, late, total)
        total = project(scans, layout, pos, pairs[: high // 2], total)
        halves = project(scans, layout, pos, pairs[high // 2 :], total, True)
        scores = sum_scores(*halves)

        (first, gram_first), (second, gram_second) = sketch_sum(scores, Fixed)
        early, late, pairs, grams = gather(first, second, gram_first + gram_second)
        inverse = small_call(
            functools.partial(invert_kernel, all_voxels),
            jax.ShapeDtypeStruct((rank, rank), F32), *grams,
        )
        out = finish(layout, pos, early + late, inverse, voxels)
        return finish(layout, pos, pairs, inverse, voxels, out)

    return on_device


def solution(mesh):
    placed = (P("subj", "vox"), P("vox", None), P(), P())
    return jax.shard_map(
        make(mesh), mesh=mesh, in_specs=placed, out_specs=P("vox", None), check_vma=False
    )
```

```python
import functools

import jax
import jax.numpy as jnp
from jax import lax
from jax.experimental import pallas as pl
from jax.experimental.pallas import tpu as pltpu
from jax.sharding import PartitionSpec as P

F32 = jnp.float32
BF16 = jnp.bfloat16
I16 = jnp.int16
HIGHEST = lax.Precision.HIGHEST
STEPS = 64.0
LOW = 2
GROUP = 8
LANES = 128
VMEM_BYTES = 20 << 20
VMEM_FIRST = 48 << 20
LIGHT = pl.CostEstimate(flops=1, bytes_accessed=1, transcendentals=0)
WHOLE = pl.BlockSpec(memory_space=pltpu.VMEM)


def exchange(value, axis, size, mask):
    return lax.ppermute(value, axis, [(i, i ^ mask) for i in range(size)])


class Plain:
    pad = 0
    dtype = BF16
    limit = VMEM_FIRST

    @staticmethod
    def encode(value):
        return value.astype(BF16)

    @staticmethod
    def decode(sent):
        return sent.astype(F32)


class Fixed:
    pad = 16
    dtype = I16
    limit = VMEM_BYTES

    @staticmethod
    def encode(value):
        top = jnp.maximum(jnp.max(jnp.abs(value), axis=0, keepdims=True), 1e-30)
        power = jnp.ceil(jnp.log2(top * (1.0 / 32000.0)) * STEPS)
        codes = jnp.round(value * jnp.exp2(power * (-1.0 / STEPS)))
        codes = jnp.clip(codes, -32767.0, 32767.0)
        rows = jnp.broadcast_to(power, (Fixed.pad, value.shape[1]))
        return jnp.concatenate([codes, rows]).astype(jnp.int32).astype(I16)

    @staticmethod
    def decode(sent):
        wide = sent.astype(jnp.int32).astype(F32)
        rows = wide.shape[0] - Fixed.pad
        return wide[:rows] * jnp.exp2(wide[rows : rows + 1] * (1.0 / STEPS))


def params(limit=VMEM_BYTES):
    return pltpu.CompilerParams(vmem_limit_bytes=limit)


class Layout:
    def __init__(self, voxels, subjects):
        self.high = subjects // LOW
        unit = subjects * LANES
        for top, bottom in ((2, 3), (1, 2)):
            self.cut = voxels * top // bottom
            self.pair = (voxels - self.cut) // self.high
            if self.cut % unit == 0 and voxels % unit == 0 and self.cut % self.pair == 0:
                break
        self.single = self.cut // subjects

    def columns(self, j):
        return self.pair if j is None else self.single

    def block(self, j, k, pos):
        if j is None:
            return self.cut // self.pair + (pos[1] ^ k)
        return (pos[0] ^ j) * self.high + (pos[1] ^ k)


def sketch_kernel(code, apart, count, pos_ref, scores_ref, *refs):
    for u in range(count):
        product = lax.dot_general(
            scores_ref[...], refs[u][...], (((0,), (0,)), ((), ())), preferred_element_type=F32
        )
        out = refs[count + u] if apart else refs[count].at[u]
        out[...] = code.encode(product.T)


def sketch_part(scans, layout, pos, scores, j, ks, code, apart, per_step):
    time_rows = scans.shape[0]
    rank = scores.shape[1]
    n = layout.columns(j)
    rows = n + code.pad
    steps = len(ks) // per_step

    def column(u):
        return lambda g, pos: (0, layout.block(j, ks[0] + g * per_step + u, pos))

    if apart:
        out_shape = [jax.ShapeDtypeStruct((rows, rank), code.dtype)] * len(ks)
        out_specs = [pl.BlockSpec((rows, rank), lambda g, pos: (0, 0))] * len(ks)
    else:
        out_shape = jax.ShapeDtypeStruct((len(ks), rows, rank), code.dtype)
        out_specs = pl.BlockSpec((per_step, rows, rank), lambda g, pos: (g, 0, 0))
    return pl.pallas_call(
        functools.partial(sketch_kernel, code, apart, per_step),
        out_shape=out_shape,
        grid_spec=pltpu.PrefetchScalarGridSpec(
            num_scalar_prefetch=1,
            grid=(steps,),
            in_specs=[pl.BlockSpec((time_rows, rank), lambda g, pos: (0, 0))]
            + [pl.BlockSpec((time_rows, n), column(u)) for u in range(per_step)],
            out_specs=out_specs,
        ),
        compiler_params=params(code.limit),
        cost_estimate=LIGHT,
    )(pos, scores, *([scans] * per_step))


def small_call(kernel, out_shape, *args):
    return pl.pallas_call(
        kernel,
        out_shape=out_shape,
        in_specs=[WHOLE] * len(args),
        out_specs=jax.tree.map(lambda _: WHOLE, out_shape),
        compiler_params=params(),
        cost_estimate=LIGHT,
    )(*args)


def add_pieces_kernel(code, count, own_ref, got_ref, *outs):
    for k in range(count):
        outs[k][...] = code.encode(code.decode(own_ref[k]) + code.decode(got_ref[k]))


def add_all_kernel(code, *refs):
    parts, outs = refs[:-2], refs[-2:]
    total = code.decode(parts[0][...])
    for part in parts[1:]:
        total = total + code.decode(part[...])
    outs[0][...] = code.encode(total)
    outs[1][...] = lax.dot_general(
        total, total, (((0,), (0,)), ((), ())), precision=HIGHEST, preferred_element_type=F32
    )


def add_halves_kernel(code, pos_ref, *refs):
    parts, (keep_ref, send_ref) = refs[:-2], refs[-2:]
    total = code.decode(parts[0][...])
    for part in parts[1:]:
        total = total + code.decode(part[...])
    half = total.shape[0] // 2
    lower = pos_ref[0] == 0
    keep_ref[...] = code.encode(jnp.where(lower, total[:half], total[half:]))
    send_ref[...] = code.encode(jnp.where(lower, total[half:], total[:half]))


def add_all(code, parts):
    rank = parts[0].shape[1]
    out = [jax.ShapeDtypeStruct(parts[0].shape, code.dtype)]
    out.append(jax.ShapeDtypeStruct((rank, rank), F32))
    return small_call(functools.partial(add_all_kernel, code), out, *parts)


def write_halves(pos_ref, value, outs):
    half = value.shape[0] // 2
    lower = pos_ref[2] == 0
    outs[0][...] = jnp.where(lower, value[:half], value[half:])
    outs[1][...] = jnp.where(lower, value[half:], value[:half])


def first_kernel(count, pos_ref, panel_ref, *refs):
    scans, outs, total = refs[:count], refs[count:-1], refs[-1]
    n = scans[0].shape[1]
    g = pl.program_id(0)

    @pl.when(g == 0)
    def _():
        total[...] = jnp.zeros_like(total)

    for u in range(count):
        panel = panel_ref[u * n : (u + 1) * n]
        total[...] += jnp.dot(scans[u][...], panel, preferred_element_type=F32)

    @pl.when(g == pl.num_programs(0) - 1)
    def _():
        write_halves(pos_ref, total[...], outs)


def first_project(scans, pos, panel, steps=3, count=4):
    time_rows, voxels = scans.shape
    rank = panel.shape[1]
    n = voxels // (steps * count)
    half = jax.ShapeDtypeStruct((time_rows // 2, rank), F32)

    def column(u):
        return lambda g, pos: (0, g * count + u)

    return pl.pallas_call(
        functools.partial(first_kernel, count),
        out_shape=[half, half],
        grid_spec=pltpu.PrefetchScalarGridSpec(
            num_scalar_prefetch=1,
            grid=(steps,),
            in_specs=[pl.BlockSpec((count * n, rank), lambda g, pos: (g, 0))]
            + [pl.BlockSpec((time_rows, n), column(u)) for u in range(count)],
            out_specs=[pl.BlockSpec(half.shape, lambda g, pos: (0, 0))] * 2,
            scratch_shapes=[pltpu.VMEM((time_rows, rank), F32)],
        ),
        compiler_params=params(VMEM_FIRST),
        cost_estimate=LIGHT,
    )(pos, panel, *([scans] * count))


def project_kernel(has_base, split, items, pos_ref, *refs):
    refs = list(refs)
    base = refs.pop(0) if has_base else None
    outs = [refs.pop() for _ in range(2 if split else 1)][::-1]
    scans, pieces = refs[: len(items)], refs[len(items) :]
    time_rows = scans[0].shape[0]
    rank = outs[0].shape[1]
    total = jnp.zeros((time_rows, rank), F32)
    for scan, (source, index) in zip(scans, items):
        piece = pieces[source][...] if index is None else pieces[source][index]
        total += jnp.dot(scan[...], piece, preferred_element_type=F32)
    if has_base:
        total += base[...]
    if split:
        write_halves(pos_ref, total, outs)
    else:
        outs[0][...] = total


def project(scans, layout, pos, groups, base=None, split=False):
    time_rows = scans.shape[0]
    rank = groups[0][2].shape[-1]
    items, names = [], []
    for source, (j, ks, array) in enumerate(groups):
        for i, k in enumerate(ks):
            items.append((source, None if array.ndim == 2 else i))
            names.append((j, k))

    def column(j, k):
        return lambda g, pos: (0, layout.block(j, k, pos))

    full = lambda shape: pl.BlockSpec(shape, lambda g, pos: (0,) * len(shape))
    bases = [] if base is None else [base]
    arrays = [array for _, _, array in groups]
    shape = (time_rows // 2, rank) if split else (time_rows, rank)
    out_shape = [jax.ShapeDtypeStruct(shape, F32)] * (2 if split else 1)
    out = pl.pallas_call(
        functools.partial(project_kernel, base is not None, split, items),
        out_shape=out_shape,
        grid_spec=pltpu.PrefetchScalarGridSpec(
            num_scalar_prefetch=1,
            grid=(1,),
            in_specs=[full(b.shape) for b in bases]
            + [pl.BlockSpec((time_rows, layout.columns(j)), column(j, k)) for j, k in names]
            + [full(p.shape) for p in arrays],
            out_specs=[full(shape)] * len(out_shape),
        ),
        compiler_params=params(),
        cost_estimate=LIGHT,
    )(pos, *bases, *([scans] * len(items)), *arrays)
    return out if split else out[0]


def finish_kernel(layout, items, has_base, pos_ref, inverse_ref, *refs):
    refs, (out, held, sems) = refs[:-3], refs[-3:]
    if has_base:
        refs = refs[1:]
    copies = []
    used = 0
    pos = (pos_ref[0], pos_ref[1])
    for number, (source, index, j, k) in enumerate(items):
        n = layout.columns(j)
        codes = refs[source][...] if index is None else refs[source][index]
        if j is None:
            value = jnp.concatenate([Fixed.decode(codes[side]) for side in range(LOW)])
        else:
            value = Fixed.decode(codes)
        rows = pl.ds(used, n)
        held[rows] = times_transpose(value, inverse_ref[...])
        used += n
        start = pl.multiple_of(layout.block(j, k, pos) * n, n)
        copy = pltpu.make_async_copy(held.at[rows], out.at[pl.ds(start, n)], sems.at[number])
        copy.start()
        copies.append(copy)
    for copy in copies:
        copy.wait()


def finish(layout, pos, groups, inverse, voxels, base=None):
    rank = inverse.shape[0]
    items = []
    for source, (j, ks, array) in enumerate(groups):
        alone = array.ndim == (2 if j is not None else 3)
        for i, k in enumerate(ks):
            items.append((source, None if alone else i, j, k))
    columns = sum(layout.columns(j) for _, _, j, _ in items)
    bases = [] if base is None else [base]
    arrays = [array for _, _, array in groups]
    return pl.pallas_call(
        functools.partial(finish_kernel, layout, items, base is not None),
        out_shape=jax.ShapeDtypeStruct((voxels, rank), F32),
        in_specs=[pl.BlockSpec(memory_space=pltpu.SMEM), WHOLE]
        + [pl.BlockSpec(memory_space=pl.ANY)] * len(bases)
        + [WHOLE] * len(arrays),
        out_specs=pl.BlockSpec(memory_space=pl.ANY),
        scratch_shapes=[
            pltpu.VMEM((columns, rank), F32),
            pltpu.SemaphoreType.DMA((len(items),)),
        ],
        input_output_aliases={2: 0} if bases else {},
        compiler_params=params(),
    )(pos, inverse, *bases, *arrays)


def inverse_factor(gram):
    size = gram.shape[0]
    groups = size // GROUP
    shape = (GROUP, size)
    sub = lax.broadcasted_iota(jnp.int32, shape, 0)
    lane = lax.broadcasted_iota(jnp.int32, shape, 1)
    left = [gram[GROUP * i : GROUP * (i + 1)] for i in range(groups)]
    right = [jnp.where(sub + GROUP * i == lane, 1.0, 0.0).astype(F32) for i in range(groups)]
    for g in range(groups):
        first = g * GROUP
        wide = lambda value: jnp.broadcast_to(value, shape)
        rows = [wide(left[g][t : t + 1]) for t in range(GROUP)]
        inverse_rows = [wide(right[g][t : t + 1]) for t in range(GROUP)]
        block = [
            [wide(left[g][t : t + 1, first + u : first + u + 1]) for u in range(GROUP)]
            for t in range(GROUP)
        ]
        below = range(g + 1, groups)
        columns = {
            i: [wide(left[i][:, first + u : first + u + 1]) for u in range(GROUP)] for i in below
        }
        scaled = []
        for t in range(GROUP):
            pivot = 1.0 / block[t][t]
            scaled.append((rows[t] * pivot, inverse_rows[t] * pivot))
            for u in range(t + 1, GROUP):
                factor = block[t][u] * pivot
                for w in range(u, GROUP):
                    block[u][w] = block[u][w] - factor * block[t][w]
                rows[u] = rows[u] - factor * rows[t]
                inverse_rows[u] = inverse_rows[u] - factor * inverse_rows[t]
                for i in below:
                    columns[i][u] = columns[i][u] - factor * columns[i][t]
        for i in below:
            for t in range(GROUP):
                left[i] = left[i] - columns[i][t] * scaled[t][0]
                right[i] = right[i] - columns[i][t] * scaled[t][1]
        for t in range(GROUP):
            left[g] = jnp.where(sub == t, rows[t], left[g])
            right[g] = jnp.where(sub == t, inverse_rows[t], right[g])
    out = []
    for g in range(groups):
        pivots = jnp.sum(
            jnp.where(sub + GROUP * g == lane, left[g], 0.0), axis=1, keepdims=True
        )
        out.append(right[g] * lax.rsqrt(pivots))
    return jnp.concatenate(out)


def times_transpose(value, inverse):
    return lax.dot_general(
        value, inverse, (((1,), (1,)), ((), ())), precision=HIGHEST, preferred_element_type=F32
    )


def scores_kernel(with_factor, lengths_ref, subjects_ref, pos_ref, mine_ref, other_ref, *refs):
    out_ref = refs[-1]
    length = lengths_ref[subjects_ref[pos_ref[1] * LOW + pos_ref[0]]]
    mine, other = mine_ref[...], other_ref[...]
    lower = pos_ref[2] == 0
    scores = jnp.concatenate([jnp.where(lower, mine, other), jnp.where(lower, other, mine)])
    if with_factor:
        scores = times_transpose(scores, refs[0][...])
    live = lax.broadcasted_iota(jnp.int32, scores.shape, 0) < length
    out_ref[...] = jnp.where(live, scores, 0.0).astype(BF16)


def invert_kernel(all_voxels, *refs):
    terms = [ref[...] for ref in refs[:-1]]
    while len(terms) > 1:
        terms = [terms[i] + terms[i + 1] for i in range(0, len(terms), 2)]
    refs[-1][...] = inverse_factor(terms[0] * (1.0 / all_voxels))


def make(mesh):
    subjects, blocks = mesh.shape["subj"], mesh.shape["vox"]
    swap = functools.partial(exchange, axis="subj", size=subjects)
    swap_vox = functools.partial(exchange, axis="vox", size=blocks)

    def on_device(scans, test_matrix, lengths, block_subject):
        time_rows, voxels = scans.shape
        rank = test_matrix.shape[1]
        all_voxels = voxels * blocks
        layout = Layout(voxels, subjects)
        high = layout.high
        ks = list(range(high))
        near, far = ks[: high // 2], ks[high // 2 :]
        me = lax.axis_index("subj")
        core = lax.axis_index("vox") % 2
        pos = jnp.stack([me % LOW, me // LOW, core]).astype(jnp.int32)

        def sketch_sum(scores, code):
            def part(after, j, ks, apart, per_step):
                ordered = scores if after is None else lax.optimization_barrier((scores, after))[0]
                return sketch_part(
                    scans, layout, pos, ordered, j, ks, code, apart, per_step
                )

            away = part(None, 1, ks, False, high // 2)
            got_away = swap(away, mask=1)
            second = part(away, None, ks[1:], True, high - 1)
            got_second = [swap(second[k - 1], mask=k * LOW) for k in ks[1:]]
            home = part(second[0], 0, ks, False, high // 2)
            (second_own,) = part(second[0], None, ks[:1], True, 1)
            got_away, got_second, home, second_own = lax.optimization_barrier(
                (got_away, got_second, home, second_own)
            )
            piece = jax.ShapeDtypeStruct((layout.single + code.pad, rank), code.dtype)
            first = small_call(
                functools.partial(add_pieces_kernel, code, high), [piece] * high, home, got_away
            )
            got_first = [swap(first[k], mask=k * LOW) for k in ks[1:]]

            half = jax.ShapeDtypeStruct((layout.pair // 2 + code.pad, rank), code.dtype)
            keep, send = pl.pallas_call(
                functools.partial(add_halves_kernel, code),
                out_shape=[half, half],
                in_specs=[pl.BlockSpec(memory_space=pltpu.SMEM)] + [WHOLE] * high,
                out_specs=[WHOLE, WHOLE],
                compiler_params=params(),
            )(pos, second_own, *got_second)
            got_send = swap(send, mask=1)
            return (
                add_all(code, [first[0], *got_first]),
                add_all(code, [keep, got_send]),
            )

        def gather(first, second, gram):
            far_in = [swap(first, mask=k * LOW) for k in far]
            near_in = [first] + [swap(first, mask=k * LOW) for k in near[1:]]
            got = swap(second, mask=1)
            lower = pos[0] == 0
            pair = jnp.stack([jnp.where(lower, second, got), jnp.where(lower, got, second)])
            mask = 1
            while mask < blocks:
                gram = gram + swap_vox(gram, mask=mask)
                mask *= 2
            near_in, gram = lax.optimization_barrier((near_in, gram))
            low_near = swap(jnp.stack(near_in), mask=1)
            gram = gram + swap(gram, mask=1)
            far_in, pair, gram = lax.optimization_barrier((far_in, pair, gram))
            low_far = swap(jnp.stack(far_in), mask=1)
            seconds = [pair] + [swap(pair, mask=k * LOW) for k in ks[1:]]
            gram = [gram] + [swap(gram, mask=k * LOW) for k in ks[1:]]
            early = [(0, [k], array) for k, array in zip(near + far, near_in + far_in)]
            late = [(1, near, low_near), (1, far, low_far)]
            pairs = [(None, [k], array) for k, array in zip(ks, seconds)]
            return early, late, pairs, gram

        def sum_scores(mine, send, *factor):
            mine = mine + swap_vox(send, mask=1)
            mask = 2
            while mask < blocks:
                mine = mine + swap_vox(mine, mask=mask)
                mask *= 2
            other = swap_vox(mine, mask=1)
            return pl.pallas_call(
                functools.partial(scores_kernel, bool(factor)),
                out_shape=jax.ShapeDtypeStruct((time_rows, rank), BF16),
                in_specs=[pl.BlockSpec(memory_space=pltpu.SMEM)] * 3
                + [WHOLE] * (2 + len(factor)),
                out_specs=WHOLE,
                compiler_params=params(),
                cost_estimate=LIGHT,
            )(lengths, block_subject, pos, mine, other, *factor)

        def pass_over(scores, code):
            (first, gram_first), (second, gram_second) = sketch_sum(scores, code)
            early, late, pairs, grams = gather(first, second, gram_first + gram_second)
            inverse = small_call(
                functools.partial(invert_kernel, all_voxels),
                jax.ShapeDtypeStruct((rank, rank), F32), *grams,
            )
            return early, late, pairs, inverse

        scores = sum_scores(*first_project(scans, pos, test_matrix))
        early, late, pairs, inverse = pass_over(scores, Plain)
        pairs = [(j, k, array.reshape(layout.pair, rank)) for j, k, array in pairs]
        total = project(scans, layout, pos, early)
        total = project(scans, layout, pos, late, total)
        total = project(scans, layout, pos, pairs[: high // 2], total)
        total, inverse = lax.optimization_barrier((total, inverse))
        halves = project(scans, layout, pos, pairs[high // 2 :], total, True)
        scores = sum_scores(*halves, inverse)
        early, late, pairs, inverse = pass_over(scores, Fixed)
        out = finish(layout, pos, early + late, inverse, voxels)
        return finish(layout, pos, pairs, inverse, voxels, out)

    return on_device


def solution(mesh):
    placed = (P("subj", "vox"), P("vox", None), P(), P())
    return jax.shard_map(
        make(mesh), mesh=mesh, in_specs=placed, out_specs=P("vox", None), check_vma=False
    )
```

```python
import functools

import jax
import jax.numpy as jnp
from jax import lax
from jax.experimental import pallas as pl
from jax.experimental.pallas import tpu as pltpu
from jax.sharding import PartitionSpec as P

F32 = jnp.float32
BF16 = jnp.bfloat16
I16 = jnp.int16
HIGHEST = lax.Precision.HIGHEST
STEPS = 64.0
LOW = 2
GROUP = 8
LANES = 128
VMEM_BYTES = 20 << 20
VMEM_FIRST = 48 << 20
LIGHT = pl.CostEstimate(flops=1, bytes_accessed=1, transcendentals=0)
WHOLE = pl.BlockSpec(memory_space=pltpu.VMEM)


def exchange(value, axis, size, mask):
    return lax.ppermute(value, axis, [(i, i ^ mask) for i in range(size)])


class Plain:
    pad = 0
    dtype = BF16
    limit = VMEM_FIRST

    @staticmethod
    def encode(value):
        return value.astype(BF16)

    @staticmethod
    def decode(sent):
        return sent.astype(F32)


class Fixed:
    pad = 16
    dtype = I16
    limit = VMEM_BYTES

    @staticmethod
    def encode(value):
        top = jnp.maximum(jnp.max(jnp.abs(value), axis=0, keepdims=True), 1e-30)
        power = jnp.ceil(jnp.log2(top * (1.0 / 32000.0)) * STEPS)
        codes = jnp.round(value * jnp.exp2(power * (-1.0 / STEPS)))
        codes = jnp.clip(codes, -32767.0, 32767.0)
        rows = jnp.broadcast_to(power, (Fixed.pad, value.shape[1]))
        return jnp.concatenate([codes, rows]).astype(jnp.int32).astype(I16)

    @staticmethod
    def decode(sent):
        wide = sent.astype(jnp.int32).astype(F32)
        rows = wide.shape[0] - Fixed.pad
        return wide[:rows] * jnp.exp2(wide[rows : rows + 1] * (1.0 / STEPS))


def params(limit=VMEM_BYTES):
    return pltpu.CompilerParams(vmem_limit_bytes=limit)


class Layout:
    def __init__(self, voxels, subjects):
        self.high = subjects // LOW
        unit = subjects * LANES
        for top, bottom in ((2, 3), (1, 2)):
            self.cut = voxels * top // bottom
            self.pair = (voxels - self.cut) // self.high
            if self.cut % unit == 0 and voxels % unit == 0 and self.cut % self.pair == 0:
                break
        self.single = self.cut // subjects

    def columns(self, j):
        return self.pair if j is None else self.single

    def block(self, j, k, pos):
        if j is None:
            return self.cut // self.pair + (pos[1] ^ k)
        return (pos[0] ^ j) * self.high + (pos[1] ^ k)


def sketch_kernel(code, apart, count, pos_ref, scores_ref, *refs):
    for u in range(count):
        product = lax.dot_general(
            scores_ref[...], refs[u][...], (((0,), (0,)), ((), ())), preferred_element_type=F32
        )
        out = refs[count + u] if apart else refs[count].at[u]
        out[...] = code.encode(product.T)


def sketch_part(scans, layout, pos, scores, j, ks, code, apart, per_step):
    time_rows = scans.shape[0]
    rank = scores.shape[1]
    n = layout.columns(j)
    rows = n + code.pad
    steps = len(ks) // per_step

    def column(u):
        return lambda g, pos: (0, layout.block(j, ks[0] + g * per_step + u, pos))

    if apart:
        out_shape = [jax.ShapeDtypeStruct((rows, rank), code.dtype)] * len(ks)
        out_specs = [pl.BlockSpec((rows, rank), lambda g, pos: (0, 0))] * len(ks)
    else:
        out_shape = jax.ShapeDtypeStruct((len(ks), rows, rank), code.dtype)
        out_specs = pl.BlockSpec((per_step, rows, rank), lambda g, pos: (g, 0, 0))
    return pl.pallas_call(
        functools.partial(sketch_kernel, code, apart, per_step),
        out_shape=out_shape,
        grid_spec=pltpu.PrefetchScalarGridSpec(
            num_scalar_prefetch=1,
            grid=(steps,),
            in_specs=[pl.BlockSpec((time_rows, rank), lambda g, pos: (0, 0))]
            + [pl.BlockSpec((time_rows, n), column(u)) for u in range(per_step)],
            out_specs=out_specs,
        ),
        compiler_params=params(code.limit),
        cost_estimate=LIGHT,
    )(pos, scores, *([scans] * per_step))


def small_call(kernel, out_shape, *args):
    return pl.pallas_call(
        kernel,
        out_shape=out_shape,
        in_specs=[WHOLE] * len(args),
        out_specs=jax.tree.map(lambda _: WHOLE, out_shape),
        compiler_params=params(),
        cost_estimate=LIGHT,
    )(*args)


def add_pieces_kernel(code, count, own_ref, got_ref, *outs):
    for k in range(count):
        outs[k][...] = code.encode(code.decode(own_ref[k]) + code.decode(got_ref[k]))


def add_all_kernel(code, *refs):
    parts, outs = refs[:-2], refs[-2:]
    total = code.decode(parts[0][...])
    for part in parts[1:]:
        total = total + code.decode(part[...])
    outs[0][...] = code.encode(total)
    outs[1][...] = lax.dot_general(
        total, total, (((0,), (0,)), ((), ())), precision=HIGHEST, preferred_element_type=F32
    )


def add_halves_kernel(code, pos_ref, *refs):
    parts, (keep_ref, send_ref) = refs[:-2], refs[-2:]
    total = code.decode(parts[0][...])
    for part in parts[1:]:
        total = total + code.decode(part[...])
    half = total.shape[0] // 2
    lower = pos_ref[0] == 0
    keep_ref[...] = code.encode(jnp.where(lower, total[:half], total[half:]))
    send_ref[...] = code.encode(jnp.where(lower, total[half:], total[:half]))


def add_all(code, parts):
    rank = parts[0].shape[1]
    out = [jax.ShapeDtypeStruct(parts[0].shape, code.dtype)]
    out.append(jax.ShapeDtypeStruct((rank, rank), F32))
    return small_call(functools.partial(add_all_kernel, code), out, *parts)


def write_halves(pos_ref, value, outs):
    half = value.shape[0] // 2
    lower = pos_ref[2] == 0
    outs[0][...] = jnp.where(lower, value[:half], value[half:])
    outs[1][...] = jnp.where(lower, value[half:], value[:half])


def first_kernel(count, pos_ref, panel_ref, *refs):
    scans, outs, total = refs[:count], refs[count:-1], refs[-1]
    n = scans[0].shape[1]
    g = pl.program_id(0)

    @pl.when(g == 0)
    def _():
        total[...] = jnp.zeros_like(total)

    for u in range(count):
        panel = panel_ref[u * n : (u + 1) * n]
        total[...] += jnp.dot(scans[u][...], panel, preferred_element_type=F32)

    @pl.when(g == pl.num_programs(0) - 1)
    def _():
        write_halves(pos_ref, total[...], outs)


def first_project(scans, pos, panel, steps=3, count=4):
    time_rows, voxels = scans.shape
    rank = panel.shape[1]
    n = voxels // (steps * count)
    half = jax.ShapeDtypeStruct((time_rows // 2, rank), F32)

    def column(u):
        return lambda g, pos: (0, g * count + u)

    return pl.pallas_call(
        functools.partial(first_kernel, count),
        out_shape=[half, half],
        grid_spec=pltpu.PrefetchScalarGridSpec(
            num_scalar_prefetch=1,
            grid=(steps,),
            in_specs=[pl.BlockSpec((count * n, rank), lambda g, pos: (g, 0))]
            + [pl.BlockSpec((time_rows, n), column(u)) for u in range(count)],
            out_specs=[pl.BlockSpec(half.shape, lambda g, pos: (0, 0))] * 2,
            scratch_shapes=[pltpu.VMEM((time_rows, rank), F32)],
        ),
        compiler_params=params(VMEM_FIRST),
        cost_estimate=LIGHT,
    )(pos, panel, *([scans] * count))


def project_kernel(has_base, split, items, pos_ref, *refs):
    refs = list(refs)
    base = refs.pop(0) if has_base else None
    outs = [refs.pop() for _ in range(2 if split else 1)][::-1]
    scans, pieces = refs[: len(items)], refs[len(items) :]
    time_rows = scans[0].shape[0]
    rank = outs[0].shape[1]
    total = jnp.zeros((time_rows, rank), F32)
    for scan, (source, index) in zip(scans, items):
        piece = pieces[source][...] if index is None else pieces[source][index]
        total += jnp.dot(scan[...], piece, preferred_element_type=F32)
    if has_base:
        total += base[...]
    if split:
        write_halves(pos_ref, total, outs)
    else:
        outs[0][...] = total


def project(scans, layout, pos, groups, base=None, split=False):
    time_rows = scans.shape[0]
    rank = groups[0][2].shape[-1]
    items, names = [], []
    for source, (j, ks, array) in enumerate(groups):
        for i, k in enumerate(ks):
            items.append((source, None if array.ndim == 2 else i))
            names.append((j, k))

    def column(j, k):
        return lambda g, pos: (0, layout.block(j, k, pos))

    full = lambda shape: pl.BlockSpec(shape, lambda g, pos: (0,) * len(shape))
    bases = [] if base is None else [base]
    arrays = [array for _, _, array in groups]
    shape = (time_rows // 2, rank) if split else (time_rows, rank)
    out_shape = [jax.ShapeDtypeStruct(shape, F32)] * (2 if split else 1)
    out = pl.pallas_call(
        functools.partial(project_kernel, base is not None, split, items),
        out_shape=out_shape,
        grid_spec=pltpu.PrefetchScalarGridSpec(
            num_scalar_prefetch=1,
            grid=(1,),
            in_specs=[full(b.shape) for b in bases]
            + [pl.BlockSpec((time_rows, layout.columns(j)), column(j, k)) for j, k in names]
            + [full(p.shape) for p in arrays],
            out_specs=[full(shape)] * len(out_shape),
        ),
        compiler_params=params(),
        cost_estimate=LIGHT,
    )(pos, *bases, *([scans] * len(items)), *arrays)
    return out if split else out[0]


def finish_kernel(layout, items, has_base, pos_ref, inverse_ref, *refs):
    refs, (out, held, sems) = refs[:-3], refs[-3:]
    if has_base:
        refs = refs[1:]
    copies = []
    used = 0
    pos = (pos_ref[0], pos_ref[1])
    for number, (source, index, j, k) in enumerate(items):
        n = layout.columns(j)
        codes = refs[source][...] if index is None else refs[source][index]
        if j is None:
            value = jnp.concatenate([Fixed.decode(codes[side]) for side in range(LOW)])
        else:
            value = Fixed.decode(codes)
        rows = pl.ds(used, n)
        held[rows] = times_transpose(value, inverse_ref[...])
        used += n
        start = pl.multiple_of(layout.block(j, k, pos) * n, n)
        copy = pltpu.make_async_copy(held.at[rows], out.at[pl.ds(start, n)], sems.at[number])
        copy.start()
        copies.append(copy)
    for copy in copies:
        copy.wait()


def finish(layout, pos, groups, inverse, voxels, base=None):
    rank = inverse.shape[0]
    items = []
    for source, (j, ks, array) in enumerate(groups):
        alone = array.ndim == (2 if j is not None else 3)
        for i, k in enumerate(ks):
            items.append((source, None if alone else i, j, k))
    columns = sum(layout.columns(j) for _, _, j, _ in items)
    bases = [] if base is None else [base]
    arrays = [array for _, _, array in groups]
    return pl.pallas_call(
        functools.partial(finish_kernel, layout, items, base is not None),
        out_shape=jax.ShapeDtypeStruct((voxels, rank), F32),
        in_specs=[pl.BlockSpec(memory_space=pltpu.SMEM), WHOLE]
        + [pl.BlockSpec(memory_space=pl.ANY)] * len(bases)
        + [WHOLE] * len(arrays),
        out_specs=pl.BlockSpec(memory_space=pl.ANY),
        scratch_shapes=[
            pltpu.VMEM((columns, rank), F32),
            pltpu.SemaphoreType.DMA((len(items),)),
        ],
        input_output_aliases={2: 0} if bases else {},
        compiler_params=params(),
    )(pos, inverse, *bases, *arrays)


def inverse_factor(gram):
    size = gram.shape[0]
    groups = size // GROUP
    shape = (GROUP, size)
    sub = lax.broadcasted_iota(jnp.int32, shape, 0)
    lane = lax.broadcasted_iota(jnp.int32, shape, 1)
    left = [gram[GROUP * i : GROUP * (i + 1)] for i in range(groups)]
    right = [jnp.where(sub + GROUP * i == lane, 1.0, 0.0).astype(F32) for i in range(groups)]
    for g in range(groups):
        first = g * GROUP
        wide = lambda value: jnp.broadcast_to(value, shape)
        rows = [wide(left[g][t : t + 1]) for t in range(GROUP)]
        inverse_rows = [wide(right[g][t : t + 1]) for t in range(GROUP)]
        block = [
            [wide(left[g][t : t + 1, first + u : first + u + 1]) for u in range(GROUP)]
            for t in range(GROUP)
        ]
        below = range(g + 1, groups)
        columns = {
            i: [wide(left[i][:, first + u : first + u + 1]) for u in range(GROUP)] for i in below
        }
        scaled = []
        for t in range(GROUP):
            pivot = 1.0 / block[t][t]
            scaled.append((rows[t] * pivot, inverse_rows[t] * pivot))
            for u in range(t + 1, GROUP):
                factor = block[t][u] * pivot
                for w in range(u, GROUP):
                    block[u][w] = block[u][w] - factor * block[t][w]
                rows[u] = rows[u] - factor * rows[t]
                inverse_rows[u] = inverse_rows[u] - factor * inverse_rows[t]
                for i in below:
                    columns[i][u] = columns[i][u] - factor * columns[i][t]
        for i in below:
            for t in range(GROUP):
                left[i] = left[i] - columns[i][t] * scaled[t][0]
                right[i] = right[i] - columns[i][t] * scaled[t][1]
        for t in range(GROUP):
            left[g] = jnp.where(sub == t, rows[t], left[g])
            right[g] = jnp.where(sub == t, inverse_rows[t], right[g])
    out = []
    for g in range(groups):
        pivots = jnp.sum(
            jnp.where(sub + GROUP * g == lane, left[g], 0.0), axis=1, keepdims=True
        )
        out.append(right[g] * lax.rsqrt(pivots))
    return jnp.concatenate(out)


def times_transpose(value, inverse):
    return lax.dot_general(
        value, inverse, (((1,), (1,)), ((), ())), precision=HIGHEST, preferred_element_type=F32
    )


def scores_kernel(with_factor, lengths_ref, subjects_ref, pos_ref, mine_ref, other_ref, *refs):
    out_ref = refs[-1]
    length = lengths_ref[subjects_ref[pos_ref[1] * LOW + pos_ref[0]]]
    mine, other = mine_ref[...], other_ref[...]
    lower = pos_ref[2] == 0
    scores = jnp.concatenate([jnp.where(lower, mine, other), jnp.where(lower, other, mine)])
    if with_factor:
        scores = times_transpose(scores, refs[0][...])
    live = lax.broadcasted_iota(jnp.int32, scores.shape, 0) < length
    out_ref[...] = jnp.where(live, scores, 0.0).astype(BF16)


def invert_kernel(all_voxels, *refs):
    terms = [ref[...] for ref in refs[:-1]]
    while len(terms) > 1:
        terms = [terms[i] + terms[i + 1] for i in range(0, len(terms), 2)]
    refs[-1][...] = inverse_factor(terms[0] * (1.0 / all_voxels))


def make(mesh):
    subjects, blocks = mesh.shape["subj"], mesh.shape["vox"]
    swap = functools.partial(exchange, axis="subj", size=subjects)
    swap_vox = functools.partial(exchange, axis="vox", size=blocks)

    def on_device(scans, test_matrix, lengths, block_subject):
        time_rows, voxels = scans.shape
        rank = test_matrix.shape[1]
        all_voxels = voxels * blocks
        layout = Layout(voxels, subjects)
        high = layout.high
        ks = list(range(high))
        near, far = ks[: high // 2], ks[high // 2 :]
        me = lax.axis_index("subj")
        core = lax.axis_index("vox") % 2
        pos = jnp.stack([me % LOW, me // LOW, core]).astype(jnp.int32)

        def sketch_sum(scores, code):
            def part(after, j, ks, apart, per_step):
                ordered = scores if after is None else lax.optimization_barrier((scores, after))[0]
                return sketch_part(
                    scans, layout, pos, ordered, j, ks, code, apart, per_step
                )

            away = part(None, 1, ks, False, high // 2)
            got_away = swap(away, mask=1)
            second = part(away, None, ks[1:], True, high - 1)
            got_second = [swap(second[k - 1], mask=k * LOW) for k in ks[1:]]
            home = part(second[0], 0, ks, False, high // 2)
            (second_own,) = part(second[0], None, ks[:1], True, 1)
            got_away, got_second, home, second_own = lax.optimization_barrier(
                (got_away, got_second, home, second_own)
            )
            piece = jax.ShapeDtypeStruct((layout.single + code.pad, rank), code.dtype)
            first = small_call(
                functools.partial(add_pieces_kernel, code, high), [piece] * high, home, got_away
            )
            got_first = [swap(first[k], mask=k * LOW) for k in ks[1:]]

            half = jax.ShapeDtypeStruct((layout.pair // 2 + code.pad, rank), code.dtype)
            keep, send = pl.pallas_call(
                functools.partial(add_halves_kernel, code),
                out_shape=[half, half],
                in_specs=[pl.BlockSpec(memory_space=pltpu.SMEM)] + [WHOLE] * high,
                out_specs=[WHOLE, WHOLE],
                compiler_params=params(),
            )(pos, second_own, *got_second)
            got_send = swap(send, mask=1)
            return (
                add_all(code, [first[0], *got_first]),
                add_all(code, [keep, got_send]),
            )

        def gather(first, second, gram):
            far_in = [swap(first, mask=k * LOW) for k in far]
            near_in = [first] + [swap(first, mask=k * LOW) for k in near[1:]]
            got = swap(second, mask=1)
            lower = pos[0] == 0
            pair = jnp.stack([jnp.where(lower, second, got), jnp.where(lower, got, second)])
            mask = 1
            while mask < blocks:
                gram = gram + swap_vox(gram, mask=mask)
                mask *= 2
            near_in, gram = lax.optimization_barrier((near_in, gram))
            gram = gram + swap(gram, mask=1)
            grams = [gram] + [swap(gram, mask=k * LOW) for k in ks[1:]]
            far_in, near_in, pair, grams = lax.optimization_barrier(
                (far_in, near_in, pair, grams)
            )
            low_near = swap(jnp.stack(near_in), mask=1)
            low_far = swap(jnp.stack(far_in), mask=1)
            seconds = [pair] + [swap(pair, mask=k * LOW) for k in ks[1:]]
            early = [(0, [k], array) for k, array in zip(near + far, near_in + far_in)]
            late = [(1, near, low_near), (1, far, low_far)]
            pairs = [(None, [k], array) for k, array in zip(ks, seconds)]
            return early, late, pairs, grams

        def sum_scores(mine, send, *factor):
            mine = mine + swap_vox(send, mask=1)
            mask = 2
            while mask < blocks:
                mine = mine + swap_vox(mine, mask=mask)
                mask *= 2
            other = swap_vox(mine, mask=1)
            return pl.pallas_call(
                functools.partial(scores_kernel, bool(factor)),
                out_shape=jax.ShapeDtypeStruct((time_rows, rank), BF16),
                in_specs=[pl.BlockSpec(memory_space=pltpu.SMEM)] * 3
                + [WHOLE] * (2 + len(factor)),
                out_specs=WHOLE,
                compiler_params=params(),
                cost_estimate=LIGHT,
            )(lengths, block_subject, pos, mine, other, *factor)

        def pass_over(scores, code):
            (first, gram_first), (second, gram_second) = sketch_sum(scores, code)
            early, late, pairs, grams = gather(first, second, gram_first + gram_second)
            inverse = small_call(
                functools.partial(invert_kernel, all_voxels),
                jax.ShapeDtypeStruct((rank, rank), F32), *grams,
            )
            return early, late, pairs, inverse

        scores = sum_scores(*first_project(scans, pos, test_matrix))
        early, late, pairs, inverse = pass_over(scores, Plain)
        pairs = [(j, k, array.reshape(layout.pair, rank)) for j, k, array in pairs]
        total = project(scans, layout, pos, early)
        total = project(scans, layout, pos, late, total)
        total = project(scans, layout, pos, pairs[: high // 2], total)
        total, inverse = lax.optimization_barrier((total, inverse))
        halves = project(scans, layout, pos, pairs[high // 2 :], total, True)
        scores = sum_scores(*halves, inverse)
        early, late, pairs, inverse = pass_over(scores, Fixed)
        out = finish(layout, pos, early + late, inverse, voxels)
        return finish(layout, pos, pairs, inverse, voxels, out)

    return on_device


def solution(mesh):
    placed = (P("subj", "vox"), P("vox", None), P(), P())
    return jax.shard_map(
        make(mesh), mesh=mesh, in_specs=placed, out_specs=P("vox", None), check_vma=False
    )
```

```python
import functools

import jax
import jax.numpy as jnp
from jax import lax
from jax.experimental import pallas as pl
from jax.experimental.pallas import tpu as pltpu
from jax.sharding import PartitionSpec as P

F32 = jnp.float32
BF16 = jnp.bfloat16
I16 = jnp.int16
HIGHEST = lax.Precision.HIGHEST
STEPS = 64.0
LOW = 2
GROUP = 8
LANES = 128
VMEM_BYTES = 20 << 20
VMEM_FIRST = 48 << 20
LIGHT = pl.CostEstimate(flops=1, bytes_accessed=1, transcendentals=0)
WHOLE = pl.BlockSpec(memory_space=pltpu.VMEM)


def exchange(value, axis, size, mask):
    return lax.ppermute(value, axis, [(i, i ^ mask) for i in range(size)])


class Plain:
    pad = 0
    dtype = BF16
    limit = VMEM_FIRST

    @staticmethod
    def encode(value):
        return value.astype(BF16)

    @staticmethod
    def decode(sent):
        return sent.astype(F32)


class Fixed:
    pad = 16
    dtype = I16
    limit = VMEM_BYTES

    @staticmethod
    def encode(value):
        top = jnp.maximum(jnp.max(jnp.abs(value), axis=0, keepdims=True), 1e-30)
        power = jnp.ceil(jnp.log2(top * (1.0 / 32000.0)) * STEPS)
        codes = jnp.round(value * jnp.exp2(power * (-1.0 / STEPS)))
        codes = jnp.clip(codes, -32767.0, 32767.0)
        rows = jnp.broadcast_to(power, (Fixed.pad, value.shape[1]))
        return jnp.concatenate([codes, rows]).astype(jnp.int32).astype(I16)

    @staticmethod
    def decode(sent):
        wide = sent.astype(jnp.int32).astype(F32)
        rows = wide.shape[0] - Fixed.pad
        return wide[:rows] * jnp.exp2(wide[rows : rows + 1] * (1.0 / STEPS))


def params(limit=VMEM_BYTES):
    return pltpu.CompilerParams(vmem_limit_bytes=limit)


class Layout:
    def __init__(self, voxels, subjects):
        self.high = subjects // LOW
        unit = subjects * LANES
        for top, bottom in ((3, 4), (2, 3), (1, 2)):
            self.cut = voxels * top // bottom
            self.pair = (voxels - self.cut) // self.high
            if self.cut % unit == 0 and voxels % unit == 0 and self.cut % self.pair == 0:
                break
        self.single = self.cut // subjects

    def columns(self, j):
        return self.pair if j is None else self.single

    def block(self, j, k, pos):
        if j is None:
            return self.cut // self.pair + (pos[1] ^ k)
        return (pos[0] ^ j) * self.high + (pos[1] ^ k)


def sketch_kernel(code, apart, count, pos_ref, scores_ref, *refs):
    for u in range(count):
        product = lax.dot_general(
            scores_ref[...], refs[u][...], (((0,), (0,)), ((), ())), preferred_element_type=F32
        )
        out = refs[count + u] if apart else refs[count].at[u]
        out[...] = code.encode(product.T)


def sketch_part(scans, layout, pos, scores, j, ks, code, apart, per_step):
    time_rows = scans.shape[0]
    rank = scores.shape[1]
    n = layout.columns(j)
    rows = n + code.pad
    steps = len(ks) // per_step

    def column(u):
        return lambda g, pos: (0, layout.block(j, ks[0] + g * per_step + u, pos))

    if apart:
        out_shape = [jax.ShapeDtypeStruct((rows, rank), code.dtype)] * len(ks)
        out_specs = [pl.BlockSpec((rows, rank), lambda g, pos: (0, 0))] * len(ks)
    else:
        out_shape = jax.ShapeDtypeStruct((len(ks), rows, rank), code.dtype)
        out_specs = pl.BlockSpec((per_step, rows, rank), lambda g, pos: (g, 0, 0))
    return pl.pallas_call(
        functools.partial(sketch_kernel, code, apart, per_step),
        out_shape=out_shape,
        grid_spec=pltpu.PrefetchScalarGridSpec(
            num_scalar_prefetch=1,
            grid=(steps,),
            in_specs=[pl.BlockSpec((time_rows, rank), lambda g, pos: (0, 0))]
            + [pl.BlockSpec((time_rows, n), column(u)) for u in range(per_step)],
            out_specs=out_specs,
        ),
        compiler_params=params(code.limit),
        cost_estimate=LIGHT,
    )(pos, scores, *([scans] * per_step))


def small_call(kernel, out_shape, *args):
    return pl.pallas_call(
        kernel,
        out_shape=out_shape,
        in_specs=[WHOLE] * len(args),
        out_specs=jax.tree.map(lambda _: WHOLE, out_shape),
        compiler_params=params(),
        cost_estimate=LIGHT,
    )(*args)


def add_pieces_kernel(code, count, own_ref, got_ref, *outs):
    for k in range(count):
        outs[k][...] = code.encode(code.decode(own_ref[k]) + code.decode(got_ref[k]))


def add_all_kernel(code, *refs):
    parts, outs = refs[:-2], refs[-2:]
    total = code.decode(parts[0][...])
    for part in parts[1:]:
        total = total + code.decode(part[...])
    outs[0][...] = code.encode(total)
    outs[1][...] = lax.dot_general(
        total, total, (((0,), (0,)), ((), ())), precision=HIGHEST, preferred_element_type=F32
    )


def add_halves_kernel(code, pos_ref, *refs):
    parts, (keep_ref, send_ref) = refs[:-2], refs[-2:]
    total = code.decode(parts[0][...])
    for part in parts[1:]:
        total = total + code.decode(part[...])
    half = total.shape[0] // 2
    lower = pos_ref[0] == 0
    keep_ref[...] = code.encode(jnp.where(lower, total[:half], total[half:]))
    send_ref[...] = code.encode(jnp.where(lower, total[half:], total[:half]))


def add_all(code, parts):
    rank = parts[0].shape[1]
    out = [jax.ShapeDtypeStruct(parts[0].shape, code.dtype)]
    out.append(jax.ShapeDtypeStruct((rank, rank), F32))
    return small_call(functools.partial(add_all_kernel, code), out, *parts)


def write_halves(pos_ref, value, outs):
    half = value.shape[0] // 2
    lower = pos_ref[2] == 0
    outs[0][...] = jnp.where(lower, value[:half], value[half:])
    outs[1][...] = jnp.where(lower, value[half:], value[:half])


def first_kernel(count, pos_ref, panel_ref, *refs):
    scans, outs, total = refs[:count], refs[count:-1], refs[-1]
    n = scans[0].shape[1]
    g = pl.program_id(0)

    @pl.when(g == 0)
    def _():
        total[...] = jnp.zeros_like(total)

    for u in range(count):
        panel = panel_ref[u * n : (u + 1) * n]
        total[...] += jnp.dot(scans[u][...], panel, preferred_element_type=F32)

    @pl.when(g == pl.num_programs(0) - 1)
    def _():
        write_halves(pos_ref, total[...], outs)


def first_project(scans, pos, panel, steps=3, count=4):
    time_rows, voxels = scans.shape
    rank = panel.shape[1]
    n = voxels // (steps * count)
    half = jax.ShapeDtypeStruct((time_rows // 2, rank), F32)

    def column(u):
        return lambda g, pos: (0, g * count + u)

    return pl.pallas_call(
        functools.partial(first_kernel, count),
        out_shape=[half, half],
        grid_spec=pltpu.PrefetchScalarGridSpec(
            num_scalar_prefetch=1,
            grid=(steps,),
            in_specs=[pl.BlockSpec((count * n, rank), lambda g, pos: (g, 0))]
            + [pl.BlockSpec((time_rows, n), column(u)) for u in range(count)],
            out_specs=[pl.BlockSpec(half.shape, lambda g, pos: (0, 0))] * 2,
            scratch_shapes=[pltpu.VMEM((time_rows, rank), F32)],
        ),
        compiler_params=params(VMEM_FIRST),
        cost_estimate=LIGHT,
    )(pos, panel, *([scans] * count))


def project_kernel(has_base, split, items, pos_ref, *refs):
    refs = list(refs)
    base = refs.pop(0) if has_base else None
    outs = [refs.pop() for _ in range(2 if split else 1)][::-1]
    scans, pieces = refs[: len(items)], refs[len(items) :]
    time_rows = scans[0].shape[0]
    rank = outs[0].shape[1]
    total = jnp.zeros((time_rows, rank), F32)
    for scan, (source, index) in zip(scans, items):
        piece = pieces[source][...] if index is None else pieces[source][index]
        total += jnp.dot(scan[...], piece, preferred_element_type=F32)
    if has_base:
        total += base[...]
    if split:
        write_halves(pos_ref, total, outs)
    else:
        outs[0][...] = total


def project(scans, layout, pos, groups, base=None, split=False):
    time_rows = scans.shape[0]
    rank = groups[0][2].shape[-1]
    items, names = [], []
    for source, (j, ks, array) in enumerate(groups):
        for i, k in enumerate(ks):
            items.append((source, None if array.ndim == 2 else i))
            names.append((j, k))

    def column(j, k):
        return lambda g, pos: (0, layout.block(j, k, pos))

    full = lambda shape: pl.BlockSpec(shape, lambda g, pos: (0,) * len(shape))
    bases = [] if base is None else [base]
    arrays = [array for _, _, array in groups]
    shape = (time_rows // 2, rank) if split else (time_rows, rank)
    out_shape = [jax.ShapeDtypeStruct(shape, F32)] * (2 if split else 1)
    out = pl.pallas_call(
        functools.partial(project_kernel, base is not None, split, items),
        out_shape=out_shape,
        grid_spec=pltpu.PrefetchScalarGridSpec(
            num_scalar_prefetch=1,
            grid=(1,),
            in_specs=[full(b.shape) for b in bases]
            + [pl.BlockSpec((time_rows, layout.columns(j)), column(j, k)) for j, k in names]
            + [full(p.shape) for p in arrays],
            out_specs=[full(shape)] * len(out_shape),
        ),
        compiler_params=params(),
        cost_estimate=LIGHT,
    )(pos, *bases, *([scans] * len(items)), *arrays)
    return out if split else out[0]


def finish_kernel(layout, items, has_base, pos_ref, inverse_ref, *refs):
    refs, (out, held, sems) = refs[:-3], refs[-3:]
    if has_base:
        refs = refs[1:]
    copies = []
    used = 0
    pos = (pos_ref[0], pos_ref[1])
    for number, (source, index, j, k) in enumerate(items):
        n = layout.columns(j)
        codes = refs[source][...] if index is None else refs[source][index]
        if j is None:
            value = jnp.concatenate([Fixed.decode(codes[side]) for side in range(LOW)])
        else:
            value = Fixed.decode(codes)
        rows = pl.ds(used, n)
        held[rows] = times_transpose(value, inverse_ref[...])
        used += n
        start = pl.multiple_of(layout.block(j, k, pos) * n, n)
        copy = pltpu.make_async_copy(held.at[rows], out.at[pl.ds(start, n)], sems.at[number])
        copy.start()
        copies.append(copy)
    for copy in copies:
        copy.wait()


def finish(layout, pos, groups, inverse, voxels, base=None):
    rank = inverse.shape[0]
    items = []
    for source, (j, ks, array) in enumerate(groups):
        alone = array.ndim == (2 if j is not None else 3)
        for i, k in enumerate(ks):
            items.append((source, None if alone else i, j, k))
    columns = sum(layout.columns(j) for _, _, j, _ in items)
    bases = [] if base is None else [base]
    arrays = [array for _, _, array in groups]
    return pl.pallas_call(
        functools.partial(finish_kernel, layout, items, base is not None),
        out_shape=jax.ShapeDtypeStruct((voxels, rank), F32),
        in_specs=[pl.BlockSpec(memory_space=pltpu.SMEM), WHOLE]
        + [pl.BlockSpec(memory_space=pl.ANY)] * len(bases)
        + [WHOLE] * len(arrays),
        out_specs=pl.BlockSpec(memory_space=pl.ANY),
        scratch_shapes=[
            pltpu.VMEM((columns, rank), F32),
            pltpu.SemaphoreType.DMA((len(items),)),
        ],
        input_output_aliases={2: 0} if bases else {},
        compiler_params=params(),
    )(pos, inverse, *bases, *arrays)


def inverse_factor(gram):
    size = gram.shape[0]
    groups = size // GROUP
    shape = (GROUP, size)
    sub = lax.broadcasted_iota(jnp.int32, shape, 0)
    lane = lax.broadcasted_iota(jnp.int32, shape, 1)
    left = [gram[GROUP * i : GROUP * (i + 1)] for i in range(groups)]
    right = [jnp.where(sub + GROUP * i == lane, 1.0, 0.0).astype(F32) for i in range(groups)]
    for g in range(groups):
        first = g * GROUP
        wide = lambda value: jnp.broadcast_to(value, shape)
        rows = [wide(left[g][t : t + 1]) for t in range(GROUP)]
        inverse_rows = [wide(right[g][t : t + 1]) for t in range(GROUP)]
        block = [
            [wide(left[g][t : t + 1, first + u : first + u + 1]) for u in range(GROUP)]
            for t in range(GROUP)
        ]
        below = range(g + 1, groups)
        columns = {
            i: [wide(left[i][:, first + u : first + u + 1]) for u in range(GROUP)] for i in below
        }
        scaled = []
        for t in range(GROUP):
            pivot = 1.0 / block[t][t]
            scaled.append((rows[t] * pivot, inverse_rows[t] * pivot))
            for u in range(t + 1, GROUP):
                factor = block[t][u] * pivot
                for w in range(u, GROUP):
                    block[u][w] = block[u][w] - factor * block[t][w]
                rows[u] = rows[u] - factor * rows[t]
                inverse_rows[u] = inverse_rows[u] - factor * inverse_rows[t]
                for i in below:
                    columns[i][u] = columns[i][u] - factor * columns[i][t]
        for i in below:
            for t in range(GROUP):
                left[i] = left[i] - columns[i][t] * scaled[t][0]
                right[i] = right[i] - columns[i][t] * scaled[t][1]
        for t in range(GROUP):
            left[g] = jnp.where(sub == t, rows[t], left[g])
            right[g] = jnp.where(sub == t, inverse_rows[t], right[g])
    out = []
    for g in range(groups):
        pivots = jnp.sum(
            jnp.where(sub + GROUP * g == lane, left[g], 0.0), axis=1, keepdims=True
        )
        out.append(right[g] * lax.rsqrt(pivots))
    return jnp.concatenate(out)


def times_transpose(value, inverse):
    return lax.dot_general(
        value, inverse, (((1,), (1,)), ((), ())), precision=HIGHEST, preferred_element_type=F32
    )


def scores_kernel(with_factor, lengths_ref, subjects_ref, pos_ref, mine_ref, other_ref, *refs):
    out_ref = refs[-1]
    length = lengths_ref[subjects_ref[pos_ref[1] * LOW + pos_ref[0]]]
    mine, other = mine_ref[...], other_ref[...]
    lower = pos_ref[2] == 0
    scores = jnp.concatenate([jnp.where(lower, mine, other), jnp.where(lower, other, mine)])
    if with_factor:
        scores = times_transpose(scores, refs[0][...])
    live = lax.broadcasted_iota(jnp.int32, scores.shape, 0) < length
    out_ref[...] = jnp.where(live, scores, 0.0).astype(BF16)


def invert_kernel(all_voxels, *refs):
    terms = [ref[...] for ref in refs[:-1]]
    while len(terms) > 1:
        terms = [terms[i] + terms[i + 1] for i in range(0, len(terms), 2)]
    refs[-1][...] = inverse_factor(terms[0] * (1.0 / all_voxels))


def make(mesh):
    subjects, blocks = mesh.shape["subj"], mesh.shape["vox"]
    swap = functools.partial(exchange, axis="subj", size=subjects)
    swap_vox = functools.partial(exchange, axis="vox", size=blocks)

    def on_device(scans, test_matrix, lengths, block_subject):
        time_rows, voxels = scans.shape
        rank = test_matrix.shape[1]
        all_voxels = voxels * blocks
        layout = Layout(voxels, subjects)
        high = layout.high
        ks = list(range(high))
        near, far = ks[: high // 2], ks[high // 2 :]
        me = lax.axis_index("subj")
        core = lax.axis_index("vox") % 2
        pos = jnp.stack([me % LOW, me // LOW, core]).astype(jnp.int32)

        def sketch_sum(scores, code):
            def part(after, j, ks, apart, per_step):
                ordered = scores if after is None else lax.optimization_barrier((scores, after))[0]
                return sketch_part(
                    scans, layout, pos, ordered, j, ks, code, apart, per_step
                )

            away = part(None, 1, ks, False, high // 2)
            got_away = swap(away, mask=1)
            second = part(away, None, ks[1:], True, high - 1)
            got_second = [swap(second[k - 1], mask=k * LOW) for k in ks[1:]]
            home = part(second[0], 0, ks, False, high // 2)
            (second_own,) = part(second[0], None, ks[:1], True, 1)
            got_away, got_second, home, second_own = lax.optimization_barrier(
                (got_away, got_second, home, second_own)
            )
            piece = jax.ShapeDtypeStruct((layout.single + code.pad, rank), code.dtype)
            first = small_call(
                functools.partial(add_pieces_kernel, code, high), [piece] * high, home, got_away
            )
            got_first = [swap(first[k], mask=k * LOW) for k in ks[1:]]

            half = jax.ShapeDtypeStruct((layout.pair // 2 + code.pad, rank), code.dtype)
            keep, send = pl.pallas_call(
                functools.partial(add_halves_kernel, code),
                out_shape=[half, half],
                in_specs=[pl.BlockSpec(memory_space=pltpu.SMEM)] + [WHOLE] * high,
                out_specs=[WHOLE, WHOLE],
                compiler_params=params(),
            )(pos, second_own, *got_second)
            got_send = swap(send, mask=1)
            return (
                add_all(code, [first[0], *got_first]),
                add_all(code, [keep, got_send]),
            )

        def gather(first, second, gram):
            far_in = [swap(first, mask=k * LOW) for k in far]
            near_in = [first] + [swap(first, mask=k * LOW) for k in near[1:]]
            got = swap(second, mask=1)
            lower = pos[0] == 0
            pair = jnp.stack([jnp.where(lower, second, got), jnp.where(lower, got, second)])
            mask = 1
            while mask < blocks:
                gram = gram + swap_vox(gram, mask=mask)
                mask *= 2
            near_in, gram = lax.optimization_barrier((near_in, gram))
            low_near = swap(jnp.stack(near_in), mask=1)
            gram = gram + swap(gram, mask=1)
            far_in, pair, gram = lax.optimization_barrier((far_in, pair, gram))
            low_far = swap(jnp.stack(far_in), mask=1)
            seconds = [pair] + [swap(pair, mask=k * LOW) for k in ks[1:]]
            gram = [gram] + [swap(gram, mask=k * LOW) for k in ks[1:]]
            early = [(0, [k], array) for k, array in zip(near + far, near_in + far_in)]
            late = [(1, near, low_near), (1, far, low_far)]
            pairs = [(None, [k], array) for k, array in zip(ks, seconds)]
            return early, late, pairs, gram

        def sum_scores(mine, send, *factor):
            mine = mine + swap_vox(send, mask=1)
            mask = 2
            while mask < blocks:
                mine = mine + swap_vox(mine, mask=mask)
                mask *= 2
            other = swap_vox(mine, mask=1)
            return pl.pallas_call(
                functools.partial(scores_kernel, bool(factor)),
                out_shape=jax.ShapeDtypeStruct((time_rows, rank), BF16),
                in_specs=[pl.BlockSpec(memory_space=pltpu.SMEM)] * 3
                + [WHOLE] * (2 + len(factor)),
                out_specs=WHOLE,
                compiler_params=params(),
                cost_estimate=LIGHT,
            )(lengths, block_subject, pos, mine, other, *factor)

        def pass_over(scores, code):
            (first, gram_first), (second, gram_second) = sketch_sum(scores, code)
            early, late, pairs, grams = gather(first, second, gram_first + gram_second)
            inverse = small_call(
                functools.partial(invert_kernel, all_voxels),
                jax.ShapeDtypeStruct((rank, rank), F32), *grams,
            )
            return early, late, pairs, inverse

        scores = sum_scores(*first_project(scans, pos, test_matrix))
        early, late, pairs, inverse = pass_over(scores, Plain)
        pairs = [(j, k, array.reshape(layout.pair, rank)) for j, k, array in pairs]
        total = project(scans, layout, pos, early)
        total = project(scans, layout, pos, late, total)
        total = project(scans, layout, pos, pairs[: high // 2], total)
        total, inverse = lax.optimization_barrier((total, inverse))
        halves = project(scans, layout, pos, pairs[high // 2 :], total, True)
        scores = sum_scores(*halves, inverse)
        early, late, pairs, inverse = pass_over(scores, Fixed)
        out = finish(layout, pos, early + late, inverse, voxels)
        return finish(layout, pos, pairs, inverse, voxels, out)

    return on_device


def solution(mesh):
    placed = (P("subj", "vox"), P("vox", None), P(), P())
    return jax.shard_map(
        make(mesh), mesh=mesh, in_specs=placed, out_specs=P("vox", None), check_vma=False
    )
```

```python
import functools

import jax
import jax.numpy as jnp
from jax import lax
from jax.experimental import pallas as pl
from jax.experimental.pallas import tpu as pltpu
from jax.sharding import PartitionSpec as P

F32 = jnp.float32
BF16 = jnp.bfloat16
I16 = jnp.int16
HIGHEST = lax.Precision.HIGHEST
STEPS = 64.0
LOW = 2
GROUP = 8
LANES = 128
VMEM_BYTES = 20 << 20
VMEM_FIRST = 48 << 20
LIGHT = pl.CostEstimate(flops=1, bytes_accessed=1, transcendentals=0)
LONG = pl.CostEstimate(flops=4 * 10**9, bytes_accessed=1, transcendentals=0)
WHOLE = pl.BlockSpec(memory_space=pltpu.VMEM)


def exchange(value, axis, size, mask):
    return lax.ppermute(value, axis, [(i, i ^ mask) for i in range(size)])


class Plain:
    pad = 0
    dtype = BF16
    limit = VMEM_FIRST

    @staticmethod
    def encode(value):
        return value.astype(BF16)

    @staticmethod
    def decode(sent):
        return sent.astype(F32)


class Fixed:
    pad = 16
    dtype = I16
    limit = VMEM_BYTES

    @staticmethod
    def encode(value):
        top = jnp.maximum(jnp.max(jnp.abs(value), axis=0, keepdims=True), 1e-30)
        power = jnp.ceil(jnp.log2(top * (1.0 / 32000.0)) * STEPS)
        codes = jnp.round(value * jnp.exp2(power * (-1.0 / STEPS)))
        codes = jnp.clip(codes, -32767.0, 32767.0)
        rows = jnp.broadcast_to(power, (Fixed.pad, value.shape[1]))
        return jnp.concatenate([codes, rows]).astype(jnp.int32).astype(I16)

    @staticmethod
    def decode(sent):
        wide = sent.astype(jnp.int32).astype(F32)
        rows = wide.shape[0] - Fixed.pad
        return wide[:rows] * jnp.exp2(wide[rows : rows + 1] * (1.0 / STEPS))


def params(limit=VMEM_BYTES):
    return pltpu.CompilerParams(vmem_limit_bytes=limit)


class Layout:
    def __init__(self, voxels, subjects):
        self.high = subjects // LOW
        unit = subjects * LANES
        for top, bottom in ((2, 3), (1, 2)):
            self.cut = voxels * top // bottom
            self.pair = (voxels - self.cut) // self.high
            if self.cut % unit == 0 and voxels % unit == 0 and self.cut % self.pair == 0:
                break
        self.single = self.cut // subjects

    def columns(self, j):
        return self.pair if j is None else self.single

    def block(self, j, k, pos):
        if j is None:
            return self.cut // self.pair + (pos[1] ^ k)
        return (pos[0] ^ j) * self.high + (pos[1] ^ k)


def sketch_kernel(code, apart, count, pos_ref, scores_ref, *refs):
    for u in range(count):
        product = lax.dot_general(
            scores_ref[...], refs[u][...], (((0,), (0,)), ((), ())), preferred_element_type=F32
        )
        out = refs[count + u] if apart else refs[count].at[u]
        out[...] = code.encode(product.T)


def sketch_part(scans, layout, pos, scores, j, ks, code, apart, per_step):
    time_rows = scans.shape[0]
    rank = scores.shape[1]
    n = layout.columns(j)
    rows = n + code.pad
    steps = len(ks) // per_step

    def column(u):
        return lambda g, pos: (0, layout.block(j, ks[0] + g * per_step + u, pos))

    if apart:
        out_shape = [jax.ShapeDtypeStruct((rows, rank), code.dtype)] * len(ks)
        out_specs = [pl.BlockSpec((rows, rank), lambda g, pos: (0, 0))] * len(ks)
    else:
        out_shape = jax.ShapeDtypeStruct((len(ks), rows, rank), code.dtype)
        out_specs = pl.BlockSpec((per_step, rows, rank), lambda g, pos: (g, 0, 0))
    return pl.pallas_call(
        functools.partial(sketch_kernel, code, apart, per_step),
        out_shape=out_shape,
        grid_spec=pltpu.PrefetchScalarGridSpec(
            num_scalar_prefetch=1,
            grid=(steps,),
            in_specs=[pl.BlockSpec((time_rows, rank), lambda g, pos: (0, 0))]
            + [pl.BlockSpec((time_rows, n), column(u)) for u in range(per_step)],
            out_specs=out_specs,
        ),
        compiler_params=params(code.limit),
        cost_estimate=LIGHT,
    )(pos, scores, *([scans] * per_step))


def small_call(kernel, out_shape, *args, cost=LIGHT):
    return pl.pallas_call(
        kernel,
        out_shape=out_shape,
        in_specs=[WHOLE] * len(args),
        out_specs=jax.tree.map(lambda _: WHOLE, out_shape),
        compiler_params=params(),
        cost_estimate=cost,
    )(*args)


def add_pieces_kernel(code, count, own_ref, got_ref, *outs):
    for k in range(count):
        outs[k][...] = code.encode(code.decode(own_ref[k]) + code.decode(got_ref[k]))


def add_all_kernel(code, *refs):
    parts, outs = refs[:-2], refs[-2:]
    total = code.decode(parts[0][...])
    for part in parts[1:]:
        total = total + code.decode(part[...])
    outs[0][...] = code.encode(total)
    outs[1][...] = lax.dot_general(
        total, total, (((0,), (0,)), ((), ())), precision=HIGHEST, preferred_element_type=F32
    )


def add_halves_kernel(code, pos_ref, *refs):
    parts, (keep_ref, send_ref) = refs[:-2], refs[-2:]
    total = code.decode(parts[0][...])
    for part in parts[1:]:
        total = total + code.decode(part[...])
    half = total.shape[0] // 2
    lower = pos_ref[0] == 0
    keep_ref[...] = code.encode(jnp.where(lower, total[:half], total[half:]))
    send_ref[...] = code.encode(jnp.where(lower, total[half:], total[:half]))


def add_all(code, parts):
    rank = parts[0].shape[1]
    out = [jax.ShapeDtypeStruct(parts[0].shape, code.dtype)]
    out.append(jax.ShapeDtypeStruct((rank, rank), F32))
    return small_call(functools.partial(add_all_kernel, code), out, *parts)


def write_halves(pos_ref, value, outs):
    half = value.shape[0] // 2
    lower = pos_ref[2] == 0
    outs[0][...] = jnp.where(lower, value[:half], value[half:])
    outs[1][...] = jnp.where(lower, value[half:], value[:half])


def first_kernel(count, pos_ref, panel_ref, *refs):
    scans, outs, total = refs[:count], refs[count:-1], refs[-1]
    n = scans[0].shape[1]
    g = pl.program_id(0)

    @pl.when(g == 0)
    def _():
        total[...] = jnp.zeros_like(total)

    for u in range(count):
        panel = panel_ref[u * n : (u + 1) * n]
        total[...] += jnp.dot(scans[u][...], panel, preferred_element_type=F32)

    @pl.when(g == pl.num_programs(0) - 1)
    def _():
        write_halves(pos_ref, total[...], outs)


def first_project(scans, pos, panel, steps=3, count=4):
    time_rows, voxels = scans.shape
    rank = panel.shape[1]
    n = voxels // (steps * count)
    half = jax.ShapeDtypeStruct((time_rows // 2, rank), F32)

    def column(u):
        return lambda g, pos: (0, g * count + u)

    return pl.pallas_call(
        functools.partial(first_kernel, count),
        out_shape=[half, half],
        grid_spec=pltpu.PrefetchScalarGridSpec(
            num_scalar_prefetch=1,
            grid=(steps,),
            in_specs=[pl.BlockSpec((count * n, rank), lambda g, pos: (g, 0))]
            + [pl.BlockSpec((time_rows, n), column(u)) for u in range(count)],
            out_specs=[pl.BlockSpec(half.shape, lambda g, pos: (0, 0))] * 2,
            scratch_shapes=[pltpu.VMEM((time_rows, rank), F32)],
        ),
        compiler_params=params(VMEM_FIRST),
        cost_estimate=LIGHT,
    )(pos, panel, *([scans] * count))


def project_kernel(has_base, split, items, pos_ref, *refs):
    refs = list(refs)
    base = refs.pop(0) if has_base else None
    outs = [refs.pop() for _ in range(2 if split else 1)][::-1]
    scans, pieces = refs[: len(items)], refs[len(items) :]
    time_rows = scans[0].shape[0]
    rank = outs[0].shape[1]
    total = jnp.zeros((time_rows, rank), F32)
    for scan, (source, index) in zip(scans, items):
        piece = pieces[source][...] if index is None else pieces[source][index]
        total += jnp.dot(scan[...], piece, preferred_element_type=F32)
    if has_base:
        total += base[...]
    if split:
        write_halves(pos_ref, total, outs)
    else:
        outs[0][...] = total


def project(scans, layout, pos, groups, base=None, split=False):
    time_rows = scans.shape[0]
    rank = groups[0][2].shape[-1]
    items, names = [], []
    for source, (j, ks, array) in enumerate(groups):
        for i, k in enumerate(ks):
            items.append((source, None if array.ndim == 2 else i))
            names.append((j, k))

    def column(j, k):
        return lambda g, pos: (0, layout.block(j, k, pos))

    full = lambda shape: pl.BlockSpec(shape, lambda g, pos: (0,) * len(shape))
    bases = [] if base is None else [base]
    arrays = [array for _, _, array in groups]
    shape = (time_rows // 2, rank) if split else (time_rows, rank)
    out_shape = [jax.ShapeDtypeStruct(shape, F32)] * (2 if split else 1)
    out = pl.pallas_call(
        functools.partial(project_kernel, base is not None, split, items),
        out_shape=out_shape,
        grid_spec=pltpu.PrefetchScalarGridSpec(
            num_scalar_prefetch=1,
            grid=(1,),
            in_specs=[full(b.shape) for b in bases]
            + [pl.BlockSpec((time_rows, layout.columns(j)), column(j, k)) for j, k in names]
            + [full(p.shape) for p in arrays],
            out_specs=[full(shape)] * len(out_shape),
        ),
        compiler_params=params(),
        cost_estimate=LIGHT,
    )(pos, *bases, *([scans] * len(items)), *arrays)
    return out if split else out[0]


def finish_kernel(layout, items, has_base, pos_ref, inverse_ref, *refs):
    refs, (out, held, sems) = refs[:-3], refs[-3:]
    if has_base:
        refs = refs[1:]
    copies = []
    used = 0
    pos = (pos_ref[0], pos_ref[1])
    for number, (source, index, j, k) in enumerate(items):
        n = layout.columns(j)
        codes = refs[source][...] if index is None else refs[source][index]
        if j is None:
            value = jnp.concatenate([Fixed.decode(codes[side]) for side in range(LOW)])
        else:
            value = Fixed.decode(codes)
        rows = pl.ds(used, n)
        held[rows] = times_transpose(value, inverse_ref[...])
        used += n
        start = pl.multiple_of(layout.block(j, k, pos) * n, n)
        copy = pltpu.make_async_copy(held.at[rows], out.at[pl.ds(start, n)], sems.at[number])
        copy.start()
        copies.append(copy)
    for copy in copies:
        copy.wait()


def finish(layout, pos, groups, inverse, voxels, base=None):
    rank = inverse.shape[0]
    items = []
    for source, (j, ks, array) in enumerate(groups):
        alone = array.ndim == (2 if j is not None else 3)
        for i, k in enumerate(ks):
            items.append((source, None if alone else i, j, k))
    columns = sum(layout.columns(j) for _, _, j, _ in items)
    bases = [] if base is None else [base]
    arrays = [array for _, _, array in groups]
    return pl.pallas_call(
        functools.partial(finish_kernel, layout, items, base is not None),
        out_shape=jax.ShapeDtypeStruct((voxels, rank), F32),
        in_specs=[pl.BlockSpec(memory_space=pltpu.SMEM), WHOLE]
        + [pl.BlockSpec(memory_space=pl.ANY)] * len(bases)
        + [WHOLE] * len(arrays),
        out_specs=pl.BlockSpec(memory_space=pl.ANY),
        scratch_shapes=[
            pltpu.VMEM((columns, rank), F32),
            pltpu.SemaphoreType.DMA((len(items),)),
        ],
        input_output_aliases={2: 0} if bases else {},
        compiler_params=params(),
    )(pos, inverse, *bases, *arrays)


def inverse_factor(gram):
    size = gram.shape[0]
    groups = size // GROUP
    shape = (GROUP, size)
    sub = lax.broadcasted_iota(jnp.int32, shape, 0)
    lane = lax.broadcasted_iota(jnp.int32, shape, 1)
    left = [gram[GROUP * i : GROUP * (i + 1)] for i in range(groups)]
    right = [jnp.where(sub + GROUP * i == lane, 1.0, 0.0).astype(F32) for i in range(groups)]
    for g in range(groups):
        first = g * GROUP
        wide = lambda value: jnp.broadcast_to(value, shape)
        rows = [wide(left[g][t : t + 1]) for t in range(GROUP)]
        inverse_rows = [wide(right[g][t : t + 1]) for t in range(GROUP)]
        block = [
            [wide(left[g][t : t + 1, first + u : first + u + 1]) for u in range(GROUP)]
            for t in range(GROUP)
        ]
        below = range(g + 1, groups)
        columns = {
            i: [wide(left[i][:, first + u : first + u + 1]) for u in range(GROUP)] for i in below
        }
        scaled = []
        for t in range(GROUP):
            pivot = 1.0 / block[t][t]
            scaled.append((rows[t] * pivot, inverse_rows[t] * pivot))
            for u in range(t + 1, GROUP):
                factor = block[t][u] * pivot
                for w in range(u, GROUP):
                    block[u][w] = block[u][w] - factor * block[t][w]
                rows[u] = rows[u] - factor * rows[t]
                inverse_rows[u] = inverse_rows[u] - factor * inverse_rows[t]
                for i in below:
                    columns[i][u] = columns[i][u] - factor * columns[i][t]
        for i in below:
            for t in range(GROUP):
                left[i] = left[i] - columns[i][t] * scaled[t][0]
                right[i] = right[i] - columns[i][t] * scaled[t][1]
        for t in range(GROUP):
            left[g] = jnp.where(sub == t, rows[t], left[g])
            right[g] = jnp.where(sub == t, inverse_rows[t], right[g])
    out = []
    for g in range(groups):
        pivots = jnp.sum(
            jnp.where(sub + GROUP * g == lane, left[g], 0.0), axis=1, keepdims=True
        )
        out.append(right[g] * lax.rsqrt(pivots))
    return jnp.concatenate(out)


def times_transpose(value, inverse):
    return lax.dot_general(
        value, inverse, (((1,), (1,)), ((), ())), precision=HIGHEST, preferred_element_type=F32
    )


def scores_kernel(with_factor, lengths_ref, subjects_ref, pos_ref, mine_ref, other_ref, *refs):
    out_ref = refs[-1]
    length = lengths_ref[subjects_ref[pos_ref[1] * LOW + pos_ref[0]]]
    mine, other = mine_ref[...], other_ref[...]
    lower = pos_ref[2] == 0
    scores = jnp.concatenate([jnp.where(lower, mine, other), jnp.where(lower, other, mine)])
    if with_factor:
        scores = times_transpose(scores, refs[0][...])
    live = lax.broadcasted_iota(jnp.int32, scores.shape, 0) < length
    out_ref[...] = jnp.where(live, scores, 0.0).astype(BF16)


def invert_kernel(all_voxels, *refs):
    terms = [ref[...] for ref in refs[:-1]]
    while len(terms) > 1:
        terms = [terms[i] + terms[i + 1] for i in range(0, len(terms), 2)]
    refs[-1][...] = inverse_factor(terms[0] * (1.0 / all_voxels))


def make(mesh):
    subjects, blocks = mesh.shape["subj"], mesh.shape["vox"]
    swap = functools.partial(exchange, axis="subj", size=subjects)
    swap_vox = functools.partial(exchange, axis="vox", size=blocks)

    def on_device(scans, test_matrix, lengths, block_subject):
        time_rows, voxels = scans.shape
        rank = test_matrix.shape[1]
        all_voxels = voxels * blocks
        layout = Layout(voxels, subjects)
        high = layout.high
        ks = list(range(high))
        near, far = ks[: high // 2], ks[high // 2 :]
        me = lax.axis_index("subj")
        core = lax.axis_index("vox") % 2
        pos = jnp.stack([me % LOW, me // LOW, core]).astype(jnp.int32)

        def sketch_sum(scores, code):
            def part(after, j, ks, apart, per_step):
                ordered = scores if after is None else lax.optimization_barrier((scores, after))[0]
                return sketch_part(
                    scans, layout, pos, ordered, j, ks, code, apart, per_step
                )

            away = part(None, 1, ks, False, high // 2)
            got_away = swap(away, mask=1)
            second = part(away, None, ks[1:], True, high - 1)
            got_second = [swap(second[k - 1], mask=k * LOW) for k in ks[1:]]
            home = part(second[0], 0, ks, False, high // 2)
            (second_own,) = part(second[0], None, ks[:1], True, 1)
            got_away, got_second, home, second_own = lax.optimization_barrier(
                (got_away, got_second, home, second_own)
            )
            piece = jax.ShapeDtypeStruct((layout.single + code.pad, rank), code.dtype)
            first = small_call(
                functools.partial(add_pieces_kernel, code, high), [piece] * high, home, got_away
            )
            got_first = [swap(first[k], mask=k * LOW) for k in ks[1:]]

            half = jax.ShapeDtypeStruct((layout.pair // 2 + code.pad, rank), code.dtype)
            keep, send = pl.pallas_call(
                functools.partial(add_halves_kernel, code),
                out_shape=[half, half],
                in_specs=[pl.BlockSpec(memory_space=pltpu.SMEM)] + [WHOLE] * high,
                out_specs=[WHOLE, WHOLE],
                compiler_params=params(),
            )(pos, second_own, *got_second)
            got_send = swap(send, mask=1)
            return (
                add_all(code, [first[0], *got_first]),
                add_all(code, [keep, got_send]),
            )

        def gather(first, second, gram):
            far_in = [swap(first, mask=k * LOW) for k in far]
            near_in = [first] + [swap(first, mask=k * LOW) for k in near[1:]]
            got = swap(second, mask=1)
            lower = pos[0] == 0
            pair = jnp.stack([jnp.where(lower, second, got), jnp.where(lower, got, second)])
            mask = 1
            while mask < blocks:
                gram = gram + swap_vox(gram, mask=mask)
                mask *= 2
            near_in, gram = lax.optimization_barrier((near_in, gram))
            low_near = swap(jnp.stack(near_in), mask=1)
            gram = gram + swap(gram, mask=1)
            far_in, pair, gram = lax.optimization_barrier((far_in, pair, gram))
            low_far = swap(jnp.stack(far_in), mask=1)
            seconds = [pair] + [swap(pair, mask=k * LOW) for k in ks[1:]]
            gram = [gram] + [swap(gram, mask=k * LOW) for k in ks[1:]]
            early = [(0, [k], array) for k, array in zip(near + far, near_in + far_in)]
            late = [(1, near, low_near), (1, far, low_far)]
            pairs = [(None, [k], array) for k, array in zip(ks, seconds)]
            return early, late, pairs, gram

        def sum_scores(mine, send, *factor):
            mine = mine + swap_vox(send, mask=1)
            mask = 2
            while mask < blocks:
                mine = mine + swap_vox(mine, mask=mask)
                mask *= 2
            other = swap_vox(mine, mask=1)
            return pl.pallas_call(
                functools.partial(scores_kernel, bool(factor)),
                out_shape=jax.ShapeDtypeStruct((time_rows, rank), BF16),
                in_specs=[pl.BlockSpec(memory_space=pltpu.SMEM)] * 3
                + [WHOLE] * (2 + len(factor)),
                out_specs=WHOLE,
                compiler_params=params(),
                cost_estimate=LIGHT,
            )(lengths, block_subject, pos, mine, other, *factor)

        def invert(grams, cost):
            return small_call(
                functools.partial(invert_kernel, all_voxels),
                jax.ShapeDtypeStruct((rank, rank), F32), *grams, cost=cost,
            )

        def pass_over(scores, code):
            (first, gram_first), (second, gram_second) = sketch_sum(scores, code)
            early, late, pairs, grams = gather(first, second, gram_first + gram_second)
            return early, late, pairs, grams

        scores = sum_scores(*first_project(scans, pos, test_matrix))
        early, late, pairs, grams = pass_over(scores, Plain)
        pairs = [(j, k, array.reshape(layout.pair, rank)) for j, k, array in pairs]
        total = project(scans, layout, pos, early)
        total = project(scans, layout, pos, late, total)
        total = project(scans, layout, pos, pairs[: high // 2], total)
        total, grams = lax.optimization_barrier((total, grams))
        halves = project(scans, layout, pos, pairs[high // 2 :], total, True)
        scores = sum_scores(*halves, invert(grams, LONG))
        early, late, pairs, grams = pass_over(scores, Fixed)
        inverse = invert(grams, LIGHT)
        out = finish(layout, pos, early + late, inverse, voxels)
        return finish(layout, pos, pairs, inverse, voxels, out)

    return on_device


def solution(mesh):
    placed = (P("subj", "vox"), P("vox", None), P(), P())
    return jax.shard_map(
        make(mesh), mesh=mesh, in_specs=placed, out_specs=P("vox", None), check_vma=False
    )
```

```python
import functools

import jax
import jax.numpy as jnp
from jax import lax
from jax.experimental import pallas as pl
from jax.experimental.pallas import tpu as pltpu
from jax.sharding import PartitionSpec as P

F32 = jnp.float32
BF16 = jnp.bfloat16
I16 = jnp.int16
HIGHEST = lax.Precision.HIGHEST
STEPS = 64.0
LOW = 2
GROUP = 8
LANES = 128
VMEM_BYTES = 20 << 20
VMEM_FIRST = 48 << 20
LIGHT = pl.CostEstimate(flops=1, bytes_accessed=1, transcendentals=0)
WHOLE = pl.BlockSpec(memory_space=pltpu.VMEM)


def exchange(value, axis, size, mask):
    return lax.ppermute(value, axis, [(i, i ^ mask) for i in range(size)])


class Plain:
    pad = 0
    dtype = BF16
    limit = VMEM_FIRST

    @staticmethod
    def encode(value):
        return value.astype(BF16)

    @staticmethod
    def decode(sent):
        return sent.astype(F32)


class Fixed:
    pad = 16
    dtype = I16
    limit = VMEM_BYTES

    @staticmethod
    def encode(value):
        top = jnp.maximum(jnp.max(jnp.abs(value), axis=0, keepdims=True), 1e-30)
        power = jnp.ceil(jnp.log2(top * (1.0 / 32000.0)) * STEPS)
        codes = jnp.round(value * jnp.exp2(power * (-1.0 / STEPS)))
        codes = jnp.clip(codes, -32767.0, 32767.0)
        rows = jnp.broadcast_to(power, (Fixed.pad, value.shape[1]))
        return jnp.concatenate([codes, rows]).astype(jnp.int32).astype(I16)

    @staticmethod
    def decode(sent):
        wide = sent.astype(jnp.int32).astype(F32)
        rows = wide.shape[0] - Fixed.pad
        return wide[:rows] * jnp.exp2(wide[rows : rows + 1] * (1.0 / STEPS))


def params(limit=VMEM_BYTES):
    return pltpu.CompilerParams(vmem_limit_bytes=limit)


class Layout:
    def __init__(self, voxels, subjects):
        self.high = subjects // LOW
        unit = subjects * LANES
        for top, bottom in ((2, 3), (1, 2)):
            self.cut = voxels * top // bottom
            self.pair = (voxels - self.cut) // self.high
            if self.cut % unit == 0 and voxels % unit == 0 and self.cut % self.pair == 0:
                break
        self.single = self.cut // subjects

    def columns(self, j):
        return self.pair if j is None else self.single

    def block(self, j, k, pos):
        if j is None:
            return self.cut // self.pair + (pos[1] ^ k)
        return (pos[0] ^ j) * self.high + (pos[1] ^ k)


def sketch_kernel(code, apart, count, pos_ref, scores_ref, *refs):
    for u in range(count):
        product = lax.dot_general(
            scores_ref[...], refs[u][...], (((0,), (0,)), ((), ())), preferred_element_type=F32
        )
        out = refs[count + u] if apart else refs[count].at[u]
        out[...] = code.encode(product.T)


def sketch_part(scans, layout, pos, scores, j, ks, code, apart, per_step):
    time_rows = scans.shape[0]
    rank = scores.shape[1]
    n = layout.columns(j)
    rows = n + code.pad
    steps = len(ks) // per_step

    def column(u):
        return lambda g, pos: (0, layout.block(j, ks[0] + g * per_step + u, pos))

    if apart:
        out_shape = [jax.ShapeDtypeStruct((rows, rank), code.dtype)] * len(ks)
        out_specs = [pl.BlockSpec((rows, rank), lambda g, pos: (0, 0))] * len(ks)
    else:
        out_shape = jax.ShapeDtypeStruct((len(ks), rows, rank), code.dtype)
        out_specs = pl.BlockSpec((per_step, rows, rank), lambda g, pos: (g, 0, 0))
    return pl.pallas_call(
        functools.partial(sketch_kernel, code, apart, per_step),
        out_shape=out_shape,
        grid_spec=pltpu.PrefetchScalarGridSpec(
            num_scalar_prefetch=1,
            grid=(steps,),
            in_specs=[pl.BlockSpec((time_rows, rank), lambda g, pos: (0, 0))]
            + [pl.BlockSpec((time_rows, n), column(u)) for u in range(per_step)],
            out_specs=out_specs,
        ),
        compiler_params=params(code.limit),
        cost_estimate=LIGHT,
    )(pos, scores, *([scans] * per_step))


def small_call(kernel, out_shape, *args):
    return pl.pallas_call(
        kernel,
        out_shape=out_shape,
        in_specs=[WHOLE] * len(args),
        out_specs=jax.tree.map(lambda _: WHOLE, out_shape),
        compiler_params=params(),
        cost_estimate=LIGHT,
    )(*args)


def add_pieces_kernel(code, count, own_ref, got_ref, *outs):
    for k in range(count):
        outs[k][...] = code.encode(code.decode(own_ref[k]) + code.decode(got_ref[k]))


def add_all_kernel(code, *refs):
    parts, outs = refs[:-2], refs[-2:]
    total = code.decode(parts[0][...])
    for part in parts[1:]:
        total = total + code.decode(part[...])
    outs[0][...] = code.encode(total)
    outs[1][...] = lax.dot_general(
        total, total, (((0,), (0,)), ((), ())), precision=HIGHEST, preferred_element_type=F32
    )


def add_halves_kernel(code, pos_ref, *refs):
    parts, (keep_ref, send_ref) = refs[:-2], refs[-2:]
    total = code.decode(parts[0][...])
    for part in parts[1:]:
        total = total + code.decode(part[...])
    half = total.shape[0] // 2
    lower = pos_ref[0] == 0
    keep_ref[...] = code.encode(jnp.where(lower, total[:half], total[half:]))
    send_ref[...] = code.encode(jnp.where(lower, total[half:], total[:half]))


def add_all(code, parts):
    rank = parts[0].shape[1]
    out = [jax.ShapeDtypeStruct(parts[0].shape, code.dtype)]
    out.append(jax.ShapeDtypeStruct((rank, rank), F32))
    return small_call(functools.partial(add_all_kernel, code), out, *parts)


def write_halves(pos_ref, value, outs):
    half = value.shape[0] // 2
    lower = pos_ref[2] == 0
    outs[0][...] = jnp.where(lower, value[:half], value[half:])
    outs[1][...] = jnp.where(lower, value[half:], value[:half])


def first_kernel(count, pos_ref, panel_ref, *refs):
    scans, outs, total = refs[:count], refs[count:-1], refs[-1]
    n = scans[0].shape[1]
    g = pl.program_id(0)

    @pl.when(g == 0)
    def _():
        total[...] = jnp.zeros_like(total)

    for u in range(count):
        panel = panel_ref[u * n : (u + 1) * n]
        total[...] += jnp.dot(scans[u][...], panel, preferred_element_type=F32)

    @pl.when(g == pl.num_programs(0) - 1)
    def _():
        write_halves(pos_ref, total[...], outs)


def first_project(scans, pos, panel, steps=3, count=4):
    time_rows, voxels = scans.shape
    rank = panel.shape[1]
    n = voxels // (steps * count)
    half = jax.ShapeDtypeStruct((time_rows // 2, rank), F32)

    def column(u):
        return lambda g, pos: (0, g * count + u)

    return pl.pallas_call(
        functools.partial(first_kernel, count),
        out_shape=[half, half],
        grid_spec=pltpu.PrefetchScalarGridSpec(
            num_scalar_prefetch=1,
            grid=(steps,),
            in_specs=[pl.BlockSpec((count * n, rank), lambda g, pos: (g, 0))]
            + [pl.BlockSpec((time_rows, n), column(u)) for u in range(count)],
            out_specs=[pl.BlockSpec(half.shape, lambda g, pos: (0, 0))] * 2,
            scratch_shapes=[pltpu.VMEM((time_rows, rank), F32)],
        ),
        compiler_params=params(VMEM_FIRST),
        cost_estimate=LIGHT,
    )(pos, panel, *([scans] * count))


def project_kernel(has_base, split, items, pos_ref, *refs):
    refs = list(refs)
    base = refs.pop(0) if has_base else None
    outs = [refs.pop() for _ in range(2 if split else 1)][::-1]
    scans, pieces = refs[: len(items)], refs[len(items) :]
    time_rows = scans[0].shape[0]
    rank = outs[0].shape[1]
    total = jnp.zeros((time_rows, rank), F32)
    for scan, (source, index) in zip(scans, items):
        piece = pieces[source][...] if index is None else pieces[source][index]
        total += jnp.dot(scan[...], piece, preferred_element_type=F32)
    if has_base:
        total += base[...]
    if split:
        write_halves(pos_ref, total, outs)
    else:
        outs[0][...] = total


def project(scans, layout, pos, groups, base=None, split=False):
    time_rows = scans.shape[0]
    rank = groups[0][2].shape[-1]
    items, names = [], []
    for source, (j, ks, array) in enumerate(groups):
        for i, k in enumerate(ks):
            items.append((source, None if array.ndim == 2 else i))
            names.append((j, k))

    def column(j, k):
        return lambda g, pos: (0, layout.block(j, k, pos))

    full = lambda shape: pl.BlockSpec(shape, lambda g, pos: (0,) * len(shape))
    bases = [] if base is None else [base]
    arrays = [array for _, _, array in groups]
    shape = (time_rows // 2, rank) if split else (time_rows, rank)
    out_shape = [jax.ShapeDtypeStruct(shape, F32)] * (2 if split else 1)
    out = pl.pallas_call(
        functools.partial(project_kernel, base is not None, split, items),
        out_shape=out_shape,
        grid_spec=pltpu.PrefetchScalarGridSpec(
            num_scalar_prefetch=1,
            grid=(1,),
            in_specs=[full(b.shape) for b in bases]
            + [pl.BlockSpec((time_rows, layout.columns(j)), column(j, k)) for j, k in names]
            + [full(p.shape) for p in arrays],
            out_specs=[full(shape)] * len(out_shape),
        ),
        compiler_params=params(),
        cost_estimate=LIGHT,
    )(pos, *bases, *([scans] * len(items)), *arrays)
    return out if split else out[0]


def finish_kernel(layout, items, has_base, pos_ref, inverse_ref, *refs):
    refs, (out, held, sems) = refs[:-3], refs[-3:]
    if has_base:
        refs = refs[1:]
    copies = []
    used = 0
    pos = (pos_ref[0], pos_ref[1])
    for number, (source, index, j, k) in enumerate(items):
        n = layout.columns(j)
        codes = refs[source][...] if index is None else refs[source][index]
        if j is None:
            value = jnp.concatenate([Fixed.decode(codes[side]) for side in range(LOW)])
        else:
            value = Fixed.decode(codes)
        rows = pl.ds(used, n)
        held[rows] = times_transpose(value, inverse_ref[...])
        used += n
        start = pl.multiple_of(layout.block(j, k, pos) * n, n)
        copy = pltpu.make_async_copy(held.at[rows], out.at[pl.ds(start, n)], sems.at[number])
        copy.start()
        copies.append(copy)
    for copy in copies:
        copy.wait()


def finish(layout, pos, groups, inverse, voxels, base=None):
    rank = inverse.shape[0]
    items = []
    for source, (j, ks, array) in enumerate(groups):
        alone = array.ndim == (2 if j is not None else 3)
        for i, k in enumerate(ks):
            items.append((source, None if alone else i, j, k))
    columns = sum(layout.columns(j) for _, _, j, _ in items)
    bases = [] if base is None else [base]
    arrays = [array for _, _, array in groups]
    return pl.pallas_call(
        functools.partial(finish_kernel, layout, items, base is not None),
        out_shape=jax.ShapeDtypeStruct((voxels, rank), F32),
        in_specs=[pl.BlockSpec(memory_space=pltpu.SMEM), WHOLE]
        + [pl.BlockSpec(memory_space=pl.ANY)] * len(bases)
        + [WHOLE] * len(arrays),
        out_specs=pl.BlockSpec(memory_space=pl.ANY),
        scratch_shapes=[
            pltpu.VMEM((columns, rank), F32),
            pltpu.SemaphoreType.DMA((len(items),)),
        ],
        input_output_aliases={2: 0} if bases else {},
        compiler_params=params(),
    )(pos, inverse, *bases, *arrays)


def inverse_factor(gram):
    size = gram.shape[0]
    groups = size // GROUP
    shape = (GROUP, size)
    sub = lax.broadcasted_iota(jnp.int32, shape, 0)
    lane = lax.broadcasted_iota(jnp.int32, shape, 1)
    left = [gram[GROUP * i : GROUP * (i + 1)] for i in range(groups)]
    right = [jnp.where(sub + GROUP * i == lane, 1.0, 0.0).astype(F32) for i in range(groups)]
    for g in range(groups):
        first = g * GROUP
        wide = lambda value: jnp.broadcast_to(value, shape)
        rows = [wide(left[g][t : t + 1]) for t in range(GROUP)]
        inverse_rows = [wide(right[g][t : t + 1]) for t in range(GROUP)]
        block = [
            [wide(left[g][t : t + 1, first + u : first + u + 1]) for u in range(GROUP)]
            for t in range(GROUP)
        ]
        below = range(g + 1, groups)
        columns = {
            i: [wide(left[i][:, first + u : first + u + 1]) for u in range(GROUP)] for i in below
        }
        scaled = []
        for t in range(GROUP):
            pivot = 1.0 / block[t][t]
            scaled.append((rows[t] * pivot, inverse_rows[t] * pivot))
            for u in range(t + 1, GROUP):
                factor = block[t][u] * pivot
                for w in range(u, GROUP):
                    block[u][w] = block[u][w] - factor * block[t][w]
                rows[u] = rows[u] - factor * rows[t]
                inverse_rows[u] = inverse_rows[u] - factor * inverse_rows[t]
                for i in below:
                    columns[i][u] = columns[i][u] - factor * columns[i][t]
        for i in below:
            for t in range(GROUP):
                left[i] = left[i] - columns[i][t] * scaled[t][0]
                right[i] = right[i] - columns[i][t] * scaled[t][1]
        for t in range(GROUP):
            left[g] = jnp.where(sub == t, rows[t], left[g])
            right[g] = jnp.where(sub == t, inverse_rows[t], right[g])
    out = []
    for g in range(groups):
        pivots = jnp.sum(
            jnp.where(sub + GROUP * g == lane, left[g], 0.0), axis=1, keepdims=True
        )
        out.append(right[g] * lax.rsqrt(pivots))
    return jnp.concatenate(out)


def times_transpose(value, inverse):
    return lax.dot_general(
        value, inverse, (((1,), (1,)), ((), ())), precision=HIGHEST, preferred_element_type=F32
    )


def scores_kernel(with_factor, lengths_ref, subjects_ref, pos_ref, mine_ref, other_ref, *refs):
    out_ref = refs[-1]
    length = lengths_ref[subjects_ref[pos_ref[1] * LOW + pos_ref[0]]]
    mine, other = mine_ref[...], other_ref[...]
    lower = pos_ref[2] == 0
    scores = jnp.concatenate([jnp.where(lower, mine, other), jnp.where(lower, other, mine)])
    if with_factor:
        scores = times_transpose(scores, refs[0][...])
    live = lax.broadcasted_iota(jnp.int32, scores.shape, 0) < length
    out_ref[...] = jnp.where(live, scores, 0.0).astype(BF16)


def invert_kernel(all_voxels, *refs):
    terms = [ref[...] for ref in refs[:-1]]
    while len(terms) > 1:
        terms = [terms[i] + terms[i + 1] for i in range(0, len(terms), 2)]
    refs[-1][...] = inverse_factor(terms[0] * (1.0 / all_voxels))


def make(mesh):
    subjects, blocks = mesh.shape["subj"], mesh.shape["vox"]
    swap = functools.partial(exchange, axis="subj", size=subjects)
    swap_vox = functools.partial(exchange, axis="vox", size=blocks)

    def on_device(scans, test_matrix, lengths, block_subject):
        time_rows, voxels = scans.shape
        rank = test_matrix.shape[1]
        all_voxels = voxels * blocks
        layout = Layout(voxels, subjects)
        high = layout.high
        ks = list(range(high))
        near, far = ks[: high // 2], ks[high // 2 :]
        me = lax.axis_index("subj")
        core = lax.axis_index("vox") % 2
        pos = jnp.stack([me % LOW, me // LOW, core]).astype(jnp.int32)

        def sketch_sum(scores, code):
            def part(after, j, ks, apart, per_step):
                ordered = scores if after is None else lax.optimization_barrier((scores, after))[0]
                return sketch_part(
                    scans, layout, pos, ordered, j, ks, code, apart, per_step
                )

            away = part(None, 1, ks, False, high // 2)
            got_away = swap(away, mask=1)
            second = part(away, None, ks[1:], True, high - 1)
            got_second = [swap(second[k - 1], mask=k * LOW) for k in ks[1:]]
            home = part(second[0], 0, ks, False, high // 2)
            (second_own,) = part(second[0], None, ks[:1], True, 1)
            got_away, got_second, home, second_own = lax.optimization_barrier(
                (got_away, got_second, home, second_own)
            )
            piece = jax.ShapeDtypeStruct((layout.single + code.pad, rank), code.dtype)
            first = small_call(
                functools.partial(add_pieces_kernel, code, high), [piece] * high, home, got_away
            )
            got_first = [swap(first[k], mask=k * LOW) for k in ks[1:]]

            half = jax.ShapeDtypeStruct((layout.pair // 2 + code.pad, rank), code.dtype)
            keep, send = pl.pallas_call(
                functools.partial(add_halves_kernel, code),
                out_shape=[half, half],
                in_specs=[pl.BlockSpec(memory_space=pltpu.SMEM)] + [WHOLE] * high,
                out_specs=[WHOLE, WHOLE],
                compiler_params=params(),
            )(pos, second_own, *got_second)
            got_send = swap(send, mask=1)
            return (
                add_all(code, [first[0], *got_first]),
                add_all(code, [keep, got_send]),
            )

        def gather(first, second, gram, near_first):
            far_in = [swap(first, mask=k * LOW) for k in far]
            near_in = [first] + [swap(first, mask=k * LOW) for k in near[1:]]
            got = swap(second, mask=1)
            lower = pos[0] == 0
            pair = jnp.stack([jnp.where(lower, second, got), jnp.where(lower, got, second)])
            mask = 1
            while mask < blocks:
                gram = gram + swap_vox(gram, mask=mask)
                mask *= 2
            near_in, gram = lax.optimization_barrier((near_in, gram))
            low_near = swap(jnp.stack(near_in), mask=1)
            gram = gram + swap(gram, mask=1)
            far_in, pair, gram = lax.optimization_barrier((far_in, pair, gram))
            if near_first:
                low_near, far_in, pair, gram = lax.optimization_barrier(
                    (low_near, far_in, pair, gram)
                )
            low_far = swap(jnp.stack(far_in), mask=1)
            seconds = [pair] + [swap(pair, mask=k * LOW) for k in ks[1:]]
            gram = [gram] + [swap(gram, mask=k * LOW) for k in ks[1:]]
            early = [(0, [k], array) for k, array in zip(near + far, near_in + far_in)]
            late = [(1, near, low_near), (1, far, low_far)]
            pairs = [(None, [k], array) for k, array in zip(ks, seconds)]
            return early, late, pairs, gram

        def sum_scores(mine, send, *factor):
            mine = mine + swap_vox(send, mask=1)
            mask = 2
            while mask < blocks:
                mine = mine + swap_vox(mine, mask=mask)
                mask *= 2
            other = swap_vox(mine, mask=1)
            return pl.pallas_call(
                functools.partial(scores_kernel, bool(factor)),
                out_shape=jax.ShapeDtypeStruct((time_rows, rank), BF16),
                in_specs=[pl.BlockSpec(memory_space=pltpu.SMEM)] * 3
                + [WHOLE] * (2 + len(factor)),
                out_specs=WHOLE,
                compiler_params=params(),
                cost_estimate=LIGHT,
            )(lengths, block_subject, pos, mine, other, *factor)

        def pass_over(scores, code, near_first):
            (first, gram_first), (second, gram_second) = sketch_sum(scores, code)
            early, late, pairs, grams = gather(
                first, second, gram_first + gram_second, near_first
            )
            inverse = small_call(
                functools.partial(invert_kernel, all_voxels),
                jax.ShapeDtypeStruct((rank, rank), F32), *grams,
            )
            return early, late, pairs, inverse

        scores = sum_scores(*first_project(scans, pos, test_matrix))
        early, late, pairs, inverse = pass_over(scores, Plain, False)
        pairs = [(j, k, array.reshape(layout.pair, rank)) for j, k, array in pairs]
        total = project(scans, layout, pos, early)
        total = project(scans, layout, pos, late, total)
        total = project(scans, layout, pos, pairs[: high // 2], total)
        total, inverse = lax.optimization_barrier((total, inverse))
        halves = project(scans, layout, pos, pairs[high // 2 :], total, True)
        scores = sum_scores(*halves, inverse)
        early, late, pairs, inverse = pass_over(scores, Fixed, True)
        out = finish(layout, pos, early + late, inverse, voxels)
        return finish(layout, pos, pairs, inverse, voxels, out)

    return on_device


def solution(mesh):
    placed = (P("subj", "vox"), P("vox", None), P(), P())
    return jax.shard_map(
        make(mesh), mesh=mesh, in_specs=placed, out_specs=P("vox", None), check_vma=False
    )
```

```python
import functools

import jax
import jax.numpy as jnp
from jax import lax
from jax.experimental import pallas as pl
from jax.experimental.pallas import tpu as pltpu
from jax.sharding import PartitionSpec as P

F32 = jnp.float32
BF16 = jnp.bfloat16
I16 = jnp.int16
HIGHEST = lax.Precision.HIGHEST
STEPS = 64.0
LOW = 2
GROUP = 8
LANES = 128
VMEM_BYTES = 20 << 20
VMEM_FIRST = 48 << 20
LIGHT = pl.CostEstimate(flops=1, bytes_accessed=1, transcendentals=0)
WHOLE = pl.BlockSpec(memory_space=pltpu.VMEM)


def exchange(value, axis, size, mask):
    return lax.ppermute(value, axis, [(i, i ^ mask) for i in range(size)])


class Plain:
    pad = 0
    dtype = BF16
    limit = VMEM_FIRST

    @staticmethod
    def encode(value):
        return value.astype(BF16)

    @staticmethod
    def decode(sent):
        return sent.astype(F32)


class Fixed:
    pad = 16
    dtype = I16
    limit = VMEM_BYTES

    @staticmethod
    def encode(value):
        top = jnp.maximum(jnp.max(jnp.abs(value), axis=0, keepdims=True), 1e-30)
        power = jnp.ceil(jnp.log2(top * (1.0 / 32000.0)) * STEPS)
        codes = jnp.round(value * jnp.exp2(power * (-1.0 / STEPS)))
        codes = jnp.clip(codes, -32767.0, 32767.0)
        rows = jnp.broadcast_to(power, (Fixed.pad, value.shape[1]))
        return jnp.concatenate([codes, rows]).astype(jnp.int32).astype(I16)

    @staticmethod
    def decode(sent):
        wide = sent.astype(jnp.int32).astype(F32)
        rows = wide.shape[0] - Fixed.pad
        return wide[:rows] * jnp.exp2(wide[rows : rows + 1] * (1.0 / STEPS))


def params(limit=VMEM_BYTES):
    return pltpu.CompilerParams(vmem_limit_bytes=limit)


class Layout:
    def __init__(self, voxels, subjects):
        self.high = subjects // LOW
        unit = subjects * LANES
        for top, bottom in ((2, 3), (1, 2)):
            self.cut = voxels * top // bottom
            self.pair = (voxels - self.cut) // self.high
            if self.cut % unit == 0 and voxels % unit == 0 and self.cut % self.pair == 0:
                break
        self.single = self.cut // subjects

    def columns(self, j):
        return self.pair if j is None else self.single

    def block(self, j, k, pos):
        if j is None:
            return self.cut // self.pair + (pos[1] ^ k)
        return (pos[0] ^ j) * self.high + (pos[1] ^ k)


def sketch_kernel(code, apart, count, pos_ref, scores_ref, *refs):
    for u in range(count):
        product = lax.dot_general(
            scores_ref[...], refs[u][...], (((0,), (0,)), ((), ())), preferred_element_type=F32
        )
        out = refs[count + u] if apart else refs[count].at[u]
        out[...] = code.encode(product.T)


def sketch_part(scans, layout, pos, scores, j, ks, code, apart, per_step):
    time_rows = scans.shape[0]
    rank = scores.shape[1]
    n = layout.columns(j)
    rows = n + code.pad
    steps = len(ks) // per_step

    def column(u):
        return lambda g, pos: (0, layout.block(j, ks[0] + g * per_step + u, pos))

    if apart:
        out_shape = [jax.ShapeDtypeStruct((rows, rank), code.dtype)] * len(ks)
        out_specs = [pl.BlockSpec((rows, rank), lambda g, pos: (0, 0))] * len(ks)
    else:
        out_shape = jax.ShapeDtypeStruct((len(ks), rows, rank), code.dtype)
        out_specs = pl.BlockSpec((per_step, rows, rank), lambda g, pos: (g, 0, 0))
    return pl.pallas_call(
        functools.partial(sketch_kernel, code, apart, per_step),
        out_shape=out_shape,
        grid_spec=pltpu.PrefetchScalarGridSpec(
            num_scalar_prefetch=1,
            grid=(steps,),
            in_specs=[pl.BlockSpec((time_rows, rank), lambda g, pos: (0, 0))]
            + [pl.BlockSpec((time_rows, n), column(u)) for u in range(per_step)],
            out_specs=out_specs,
        ),
        compiler_params=params(code.limit),
        cost_estimate=LIGHT,
    )(pos, scores, *([scans] * per_step))


def small_call(kernel, out_shape, *args):
    return pl.pallas_call(
        kernel,
        out_shape=out_shape,
        in_specs=[WHOLE] * len(args),
        out_specs=jax.tree.map(lambda _: WHOLE, out_shape),
        compiler_params=params(),
        cost_estimate=LIGHT,
    )(*args)


def add_pieces_kernel(code, count, own_ref, got_ref, *outs):
    for k in range(count):
        outs[k][...] = code.encode(code.decode(own_ref[k]) + code.decode(got_ref[k]))


def add_all_kernel(code, *refs):
    parts, outs = refs[:-2], refs[-2:]
    total = code.decode(parts[0][...])
    for part in parts[1:]:
        total = total + code.decode(part[...])
    outs[0][...] = code.encode(total)
    outs[1][...] = lax.dot_general(
        total, total, (((0,), (0,)), ((), ())), precision=HIGHEST, preferred_element_type=F32
    )


def add_halves_kernel(code, pos_ref, *refs):
    parts, (keep_ref, send_ref) = refs[:-2], refs[-2:]
    total = code.decode(parts[0][...])
    for part in parts[1:]:
        total = total + code.decode(part[...])
    half = total.shape[0] // 2
    lower = pos_ref[0] == 0
    keep_ref[...] = code.encode(jnp.where(lower, total[:half], total[half:]))
    send_ref[...] = code.encode(jnp.where(lower, total[half:], total[:half]))


def add_all(code, parts):
    rank = parts[0].shape[1]
    out = [jax.ShapeDtypeStruct(parts[0].shape, code.dtype)]
    out.append(jax.ShapeDtypeStruct((rank, rank), F32))
    return small_call(functools.partial(add_all_kernel, code), out, *parts)


def write_halves(pos_ref, value, outs):
    half = value.shape[0] // 2
    lower = pos_ref[2] == 0
    outs[0][...] = jnp.where(lower, value[:half], value[half:])
    outs[1][...] = jnp.where(lower, value[half:], value[:half])


def first_kernel(count, pos_ref, panel_ref, *refs):
    scans, outs, total = refs[:count], refs[count:-1], refs[-1]
    n = scans[0].shape[1]
    g = pl.program_id(0)

    @pl.when(g == 0)
    def _():
        total[...] = jnp.zeros_like(total)

    for u in range(count):
        panel = panel_ref[u * n : (u + 1) * n]
        total[...] += jnp.dot(scans[u][...], panel, preferred_element_type=F32)

    @pl.when(g == pl.num_programs(0) - 1)
    def _():
        write_halves(pos_ref, total[...], outs)


def first_project(scans, pos, panel, steps=3, count=4):
    time_rows, voxels = scans.shape
    rank = panel.shape[1]
    n = voxels // (steps * count)
    half = jax.ShapeDtypeStruct((time_rows // 2, rank), F32)

    def column(u):
        return lambda g, pos: (0, g * count + u)

    return pl.pallas_call(
        functools.partial(first_kernel, count),
        out_shape=[half, half],
        grid_spec=pltpu.PrefetchScalarGridSpec(
            num_scalar_prefetch=1,
            grid=(steps,),
            in_specs=[pl.BlockSpec((count * n, rank), lambda g, pos: (g, 0))]
            + [pl.BlockSpec((time_rows, n), column(u)) for u in range(count)],
            out_specs=[pl.BlockSpec(half.shape, lambda g, pos: (0, 0))] * 2,
            scratch_shapes=[pltpu.VMEM((time_rows, rank), F32)],
        ),
        compiler_params=params(VMEM_FIRST),
        cost_estimate=LIGHT,
    )(pos, panel, *([scans] * count))


def project_kernel(has_base, split, items, pos_ref, *refs):
    refs = list(refs)
    base = refs.pop(0) if has_base else None
    outs = [refs.pop() for _ in range(2 if split else 1)][::-1]
    scans, pieces = refs[: len(items)], refs[len(items) :]
    time_rows = scans[0].shape[0]
    rank = outs[0].shape[1]
    total = jnp.zeros((time_rows, rank), F32)
    for scan, (source, index) in zip(scans, items):
        piece = pieces[source][...] if index is None else pieces[source][index]
        total += jnp.dot(scan[...], piece, preferred_element_type=F32)
    if has_base:
        total += base[...]
    if split:
        write_halves(pos_ref, total, outs)
    else:
        outs[0][...] = total


def project(scans, layout, pos, groups, base=None, split=False):
    time_rows = scans.shape[0]
    rank = groups[0][2].shape[-1]
    items, names = [], []
    for source, (j, ks, array) in enumerate(groups):
        for i, k in enumerate(ks):
            items.append((source, None if array.ndim == 2 else i))
            names.append((j, k))

    def column(j, k):
        return lambda g, pos: (0, layout.block(j, k, pos))

    full = lambda shape: pl.BlockSpec(shape, lambda g, pos: (0,) * len(shape))
    bases = [] if base is None else [base]
    arrays = [array for _, _, array in groups]
    shape = (time_rows // 2, rank) if split else (time_rows, rank)
    out_shape = [jax.ShapeDtypeStruct(shape, F32)] * (2 if split else 1)
    out = pl.pallas_call(
        functools.partial(project_kernel, base is not None, split, items),
        out_shape=out_shape,
        grid_spec=pltpu.PrefetchScalarGridSpec(
            num_scalar_prefetch=1,
            grid=(1,),
            in_specs=[full(b.shape) for b in bases]
            + [pl.BlockSpec((time_rows, layout.columns(j)), column(j, k)) for j, k in names]
            + [full(p.shape) for p in arrays],
            out_specs=[full(shape)] * len(out_shape),
        ),
        compiler_params=params(),
        cost_estimate=LIGHT,
    )(pos, *bases, *([scans] * len(items)), *arrays)
    return out if split else out[0]


def finish_kernel(layout, items, has_base, pos_ref, inverse_ref, *refs):
    refs, (out, held, sems) = refs[:-3], refs[-3:]
    if has_base:
        refs = refs[1:]
    copies = []
    used = 0
    pos = (pos_ref[0], pos_ref[1])
    for number, (source, index, j, k) in enumerate(items):
        n = layout.columns(j)
        codes = refs[source][...] if index is None else refs[source][index]
        if j is None:
            value = jnp.concatenate([Fixed.decode(codes[side]) for side in range(LOW)])
        else:
            value = Fixed.decode(codes)
        rows = pl.ds(used, n)
        held[rows] = times_transpose(value, inverse_ref[...])
        used += n
        start = pl.multiple_of(layout.block(j, k, pos) * n, n)
        copy = pltpu.make_async_copy(held.at[rows], out.at[pl.ds(start, n)], sems.at[number])
        copy.start()
        copies.append(copy)
    for copy in copies:
        copy.wait()


def finish(layout, pos, groups, inverse, voxels, base=None):
    rank = inverse.shape[0]
    items = []
    for source, (j, ks, array) in enumerate(groups):
        alone = array.ndim == (2 if j is not None else 3)
        for i, k in enumerate(ks):
            items.append((source, None if alone else i, j, k))
    columns = sum(layout.columns(j) for _, _, j, _ in items)
    bases = [] if base is None else [base]
    arrays = [array for _, _, array in groups]
    return pl.pallas_call(
        functools.partial(finish_kernel, layout, items, base is not None),
        out_shape=jax.ShapeDtypeStruct((voxels, rank), F32),
        in_specs=[pl.BlockSpec(memory_space=pltpu.SMEM), WHOLE]
        + [pl.BlockSpec(memory_space=pl.ANY)] * len(bases)
        + [WHOLE] * len(arrays),
        out_specs=pl.BlockSpec(memory_space=pl.ANY),
        scratch_shapes=[
            pltpu.VMEM((columns, rank), F32),
            pltpu.SemaphoreType.DMA((len(items),)),
        ],
        input_output_aliases={2: 0} if bases else {},
        compiler_params=params(),
    )(pos, inverse, *bases, *arrays)


def inverse_factor(gram):
    size = gram.shape[0]
    groups = size // GROUP
    shape = (GROUP, size)
    sub = lax.broadcasted_iota(jnp.int32, shape, 0)
    lane = lax.broadcasted_iota(jnp.int32, shape, 1)
    left = [gram[GROUP * i : GROUP * (i + 1)] for i in range(groups)]
    right = [jnp.where(sub + GROUP * i == lane, 1.0, 0.0).astype(F32) for i in range(groups)]
    for g in range(groups):
        first = g * GROUP
        wide = lambda value: jnp.broadcast_to(value, shape)
        rows = [wide(left[g][t : t + 1]) for t in range(GROUP)]
        inverse_rows = [wide(right[g][t : t + 1]) for t in range(GROUP)]
        block = [
            [wide(left[g][t : t + 1, first + u : first + u + 1]) for u in range(GROUP)]
            for t in range(GROUP)
        ]
        below = range(g + 1, groups)
        columns = {
            i: [wide(left[i][:, first + u : first + u + 1]) for u in range(GROUP)] for i in below
        }
        scaled = []
        for t in range(GROUP):
            pivot = 1.0 / block[t][t]
            scaled.append((rows[t] * pivot, inverse_rows[t] * pivot))
            for u in range(t + 1, GROUP):
                factor = block[t][u] * pivot
                for w in range(u, GROUP):
                    block[u][w] = block[u][w] - factor * block[t][w]
                rows[u] = rows[u] - factor * rows[t]
                inverse_rows[u] = inverse_rows[u] - factor * inverse_rows[t]
                for i in below:
                    columns[i][u] = columns[i][u] - factor * columns[i][t]
        for i in below:
            for t in range(GROUP):
                left[i] = left[i] - columns[i][t] * scaled[t][0]
                right[i] = right[i] - columns[i][t] * scaled[t][1]
        for t in range(GROUP):
            left[g] = jnp.where(sub == t, rows[t], left[g])
            right[g] = jnp.where(sub == t, inverse_rows[t], right[g])
    out = []
    for g in range(groups):
        pivots = jnp.sum(
            jnp.where(sub + GROUP * g == lane, left[g], 0.0), axis=1, keepdims=True
        )
        out.append(right[g] * lax.rsqrt(pivots))
    return jnp.concatenate(out)


def times_transpose(value, inverse):
    return lax.dot_general(
        value, inverse, (((1,), (1,)), ((), ())), precision=HIGHEST, preferred_element_type=F32
    )


def scores_kernel(with_factor, lengths_ref, subjects_ref, pos_ref, mine_ref, other_ref, *refs):
    out_ref = refs[-1]
    length = lengths_ref[subjects_ref[pos_ref[1] * LOW + pos_ref[0]]]
    mine, other = mine_ref[...], other_ref[...]
    lower = pos_ref[2] == 0
    scores = jnp.concatenate([jnp.where(lower, mine, other), jnp.where(lower, other, mine)])
    if with_factor:
        scores = times_transpose(scores, refs[0][...])
    live = lax.broadcasted_iota(jnp.int32, scores.shape, 0) < length
    out_ref[...] = jnp.where(live, scores, 0.0).astype(BF16)


def invert_kernel(all_voxels, *refs):
    terms = [ref[...] for ref in refs[:-1]]
    while len(terms) > 1:
        terms = [terms[i] + terms[i + 1] for i in range(0, len(terms), 2)]
    refs[-1][...] = inverse_factor(terms[0] * (1.0 / all_voxels))


def make(mesh):
    subjects, blocks = mesh.shape["subj"], mesh.shape["vox"]
    swap = functools.partial(exchange, axis="subj", size=subjects)
    swap_vox = functools.partial(exchange, axis="vox", size=blocks)

    def on_device(scans, test_matrix, lengths, block_subject):
        time_rows, voxels = scans.shape
        rank = test_matrix.shape[1]
        all_voxels = voxels * blocks
        layout = Layout(voxels, subjects)
        high = layout.high
        ks = list(range(high))
        near, far = ks[: high // 2], ks[high // 2 :]
        me = lax.axis_index("subj")
        core = lax.axis_index("vox") % 2
        pos = jnp.stack([me % LOW, me // LOW, core]).astype(jnp.int32)

        def sketch_sum(scores, code):
            def part(after, j, ks, apart, per_step):
                ordered = scores if after is None else lax.optimization_barrier((scores, after))[0]
                return sketch_part(
                    scans, layout, pos, ordered, j, ks, code, apart, per_step
                )

            away = part(None, 1, ks, False, high // 2)
            got_away = swap(away, mask=1)
            second = part(away, None, ks[1:], True, high - 1)
            got_second = [swap(second[k - 1], mask=k * LOW) for k in ks[1:]]
            home = part(second[0], 0, ks, False, high // 2)
            (second_own,) = part(second[0], None, ks[:1], True, 1)
            got_away, got_second, home, second_own = lax.optimization_barrier(
                (got_away, got_second, home, second_own)
            )
            piece = jax.ShapeDtypeStruct((layout.single + code.pad, rank), code.dtype)
            first = small_call(
                functools.partial(add_pieces_kernel, code, high), [piece] * high, home, got_away
            )
            got_first = [swap(first[k], mask=k * LOW) for k in ks[1:]]

            half = jax.ShapeDtypeStruct((layout.pair // 2 + code.pad, rank), code.dtype)
            keep, send = pl.pallas_call(
                functools.partial(add_halves_kernel, code),
                out_shape=[half, half],
                in_specs=[pl.BlockSpec(memory_space=pltpu.SMEM)] + [WHOLE] * high,
                out_specs=[WHOLE, WHOLE],
                compiler_params=params(),
            )(pos, second_own, *got_second)
            got_send = swap(send, mask=1)
            return (
                add_all(code, [first[0], *got_first]),
                add_all(code, [keep, got_send]),
            )

        def gather(first, second, gram):
            far_in = [swap(first, mask=k * LOW) for k in far]
            near_in = [first] + [swap(first, mask=k * LOW) for k in near[1:]]
            got = swap(second, mask=1)
            lower = pos[0] == 0
            pair = jnp.stack([jnp.where(lower, second, got), jnp.where(lower, got, second)])
            mask = 1
            while mask < blocks:
                gram = gram + swap_vox(gram, mask=mask)
                mask *= 2
            near_in, gram = lax.optimization_barrier((near_in, gram))
            low_near = swap(jnp.stack(near_in), mask=1)
            gram = gram + swap(gram, mask=1)
            far_in, pair, gram = lax.optimization_barrier((far_in, pair, gram))
            low_far = swap(jnp.stack(far_in), mask=1)
            seconds = [pair] + [swap(pair, mask=k * LOW) for k in ks[1:]]
            gram = [gram] + [swap(gram, mask=k * LOW) for k in ks[1:]]
            early = [(0, [k], array) for k, array in zip(near + far, near_in + far_in)]
            late = [(1, near, low_near), (1, far, low_far)]
            pairs = [(None, [k], array) for k, array in zip(ks, seconds)]
            return early, late, pairs, gram

        def sum_scores(mine, send, *factor):
            mine = mine + swap_vox(send, mask=1)
            mask = 2
            while mask < blocks:
                mine = mine + swap_vox(mine, mask=mask)
                mask *= 2
            other = swap_vox(mine, mask=1)
            return pl.pallas_call(
                functools.partial(scores_kernel, bool(factor)),
                out_shape=jax.ShapeDtypeStruct((time_rows, rank), BF16),
                in_specs=[pl.BlockSpec(memory_space=pltpu.SMEM)] * 3
                + [WHOLE] * (2 + len(factor)),
                out_specs=WHOLE,
                compiler_params=params(),
                cost_estimate=LIGHT,
            )(lengths, block_subject, pos, mine, other, *factor)

        def pass_over(scores, code):
            (first, gram_first), (second, gram_second) = sketch_sum(scores, code)
            early, late, pairs, grams = gather(first, second, gram_first + gram_second)
            inverse = small_call(
                functools.partial(invert_kernel, all_voxels),
                jax.ShapeDtypeStruct((rank, rank), F32), *grams,
            )
            return early, late, pairs, inverse

        scores = sum_scores(*first_project(scans, pos, test_matrix))
        early, late, pairs, inverse = pass_over(scores, Plain)
        pairs = [(j, k, array.reshape(layout.pair, rank)) for j, k, array in pairs]
        total = project(scans, layout, pos, early)
        total = project(scans, layout, pos, late, total)
        total = project(scans, layout, pos, pairs[: high // 2], total)
        total, inverse = lax.optimization_barrier((total, inverse))
        halves = project(scans, layout, pos, pairs[high // 2 :], total, True)
        scores = sum_scores(*halves, inverse)
        early, late, pairs, inverse = pass_over(scores, Fixed)
        out = finish(layout, pos, early + late + pairs[:1], inverse, voxels)
        return finish(layout, pos, pairs[1:], inverse, voxels, out)

    return on_device


def solution(mesh):
    placed = (P("subj", "vox"), P("vox", None), P(), P())
    return jax.shard_map(
        make(mesh), mesh=mesh, in_specs=placed, out_specs=P("vox", None), check_vma=False
    )
```

```python
import functools

import jax
import jax.numpy as jnp
from jax import lax
from jax.experimental import pallas as pl
from jax.experimental.pallas import tpu as pltpu
from jax.sharding import PartitionSpec as P

F32 = jnp.float32
BF16 = jnp.bfloat16
I16 = jnp.int16
HIGHEST = lax.Precision.HIGHEST
STEPS = 64.0
LOW = 2
GROUP = 8
LANES = 128
VMEM_BYTES = 20 << 20
VMEM_FIRST = 48 << 20
LIGHT = pl.CostEstimate(flops=1, bytes_accessed=1, transcendentals=0)
WHOLE = pl.BlockSpec(memory_space=pltpu.VMEM)


def exchange(value, axis, size, mask):
    return lax.ppermute(value, axis, [(i, i ^ mask) for i in range(size)])


class Plain:
    pad = 0
    dtype = BF16
    limit = VMEM_FIRST

    @staticmethod
    def encode(value):
        return value.astype(BF16)

    @staticmethod
    def decode(sent):
        return sent.astype(F32)


class Fixed:
    pad = 16
    dtype = I16
    limit = VMEM_BYTES

    @staticmethod
    def encode(value):
        top = jnp.maximum(jnp.max(jnp.abs(value), axis=0, keepdims=True), 1e-30)
        power = jnp.ceil(jnp.log2(top * (1.0 / 32000.0)) * STEPS)
        codes = jnp.round(value * jnp.exp2(power * (-1.0 / STEPS)))
        codes = jnp.clip(codes, -32767.0, 32767.0)
        rows = jnp.broadcast_to(power, (Fixed.pad, value.shape[1]))
        return jnp.concatenate([codes, rows]).astype(jnp.int32).astype(I16)

    @staticmethod
    def decode(sent):
        wide = sent.astype(jnp.int32).astype(F32)
        rows = wide.shape[0] - Fixed.pad
        return wide[:rows] * jnp.exp2(wide[rows : rows + 1] * (1.0 / STEPS))


def params(limit=VMEM_BYTES):
    return pltpu.CompilerParams(vmem_limit_bytes=limit)


class Layout:
    def __init__(self, voxels, subjects):
        self.high = subjects // LOW
        unit = subjects * LANES
        for top, bottom in ((2, 3), (1, 2)):
            self.cut = voxels * top // bottom
            self.pair = (voxels - self.cut) // self.high
            if self.cut % unit == 0 and voxels % unit == 0 and self.cut % self.pair == 0:
                break
        self.single = self.cut // subjects

    def columns(self, j):
        return self.pair if j is None else self.single

    def block(self, j, k, pos):
        if j is None:
            return self.cut // self.pair + (pos[1] ^ k)
        return (pos[0] ^ j) * self.high + (pos[1] ^ k)


def sketch_kernel(code, apart, count, pos_ref, scores_ref, *refs):
    for u in range(count):
        product = lax.dot_general(
            scores_ref[...], refs[u][...], (((0,), (0,)), ((), ())), preferred_element_type=F32
        )
        out = refs[count + u] if apart else refs[count].at[u]
        out[...] = code.encode(product.T)


def sketch_part(scans, layout, pos, scores, j, ks, code, apart, per_step):
    time_rows = scans.shape[0]
    rank = scores.shape[1]
    n = layout.columns(j)
    rows = n + code.pad
    steps = len(ks) // per_step

    def column(u):
        return lambda g, pos: (0, layout.block(j, ks[0] + g * per_step + u, pos))

    if apart:
        out_shape = [jax.ShapeDtypeStruct((rows, rank), code.dtype)] * len(ks)
        out_specs = [pl.BlockSpec((rows, rank), lambda g, pos: (0, 0))] * len(ks)
    else:
        out_shape = jax.ShapeDtypeStruct((len(ks), rows, rank), code.dtype)
        out_specs = pl.BlockSpec((per_step, rows, rank), lambda g, pos: (g, 0, 0))
    return pl.pallas_call(
        functools.partial(sketch_kernel, code, apart, per_step),
        out_shape=out_shape,
        grid_spec=pltpu.PrefetchScalarGridSpec(
            num_scalar_prefetch=1,
            grid=(steps,),
            in_specs=[pl.BlockSpec((time_rows, rank), lambda g, pos: (0, 0))]
            + [pl.BlockSpec((time_rows, n), column(u)) for u in range(per_step)],
            out_specs=out_specs,
        ),
        compiler_params=params(code.limit),
        cost_estimate=LIGHT,
    )(pos, scores, *([scans] * per_step))


def small_call(kernel, out_shape, *args):
    return pl.pallas_call(
        kernel,
        out_shape=out_shape,
        in_specs=[WHOLE] * len(args),
        out_specs=jax.tree.map(lambda _: WHOLE, out_shape),
        compiler_params=params(),
        cost_estimate=LIGHT,
    )(*args)


def add_pieces_kernel(code, count, own_ref, got_ref, *outs):
    for k in range(count):
        outs[k][...] = code.encode(code.decode(own_ref[k]) + code.decode(got_ref[k]))


def add_all_kernel(code, *refs):
    parts, outs = refs[:-2], refs[-2:]
    total = code.decode(parts[0][...])
    for part in parts[1:]:
        total = total + code.decode(part[...])
    outs[0][...] = code.encode(total)
    outs[1][...] = lax.dot_general(
        total, total, (((0,), (0,)), ((), ())), precision=HIGHEST, preferred_element_type=F32
    )


def add_halves_kernel(code, pos_ref, *refs):
    parts, (keep_ref, send_ref) = refs[:-2], refs[-2:]
    total = code.decode(parts[0][...])
    for part in parts[1:]:
        total = total + code.decode(part[...])
    half = total.shape[0] // 2
    lower = pos_ref[0] == 0
    keep_ref[...] = code.encode(jnp.where(lower, total[:half], total[half:]))
    send_ref[...] = code.encode(jnp.where(lower, total[half:], total[:half]))


def add_all(code, parts):
    rank = parts[0].shape[1]
    out = [jax.ShapeDtypeStruct(parts[0].shape, code.dtype)]
    out.append(jax.ShapeDtypeStruct((rank, rank), F32))
    return small_call(functools.partial(add_all_kernel, code), out, *parts)


def write_halves(pos_ref, value, outs):
    half = value.shape[0] // 2
    lower = pos_ref[2] == 0
    outs[0][...] = jnp.where(lower, value[:half], value[half:])
    outs[1][...] = jnp.where(lower, value[half:], value[:half])


def first_kernel(count, pos_ref, panel_ref, *refs):
    scans, outs, total = refs[:count], refs[count:-1], refs[-1]
    n = scans[0].shape[1]
    g = pl.program_id(0)

    @pl.when(g == 0)
    def _():
        total[...] = jnp.zeros_like(total)

    for u in range(count):
        panel = panel_ref[u * n : (u + 1) * n]
        total[...] += jnp.dot(scans[u][...], panel, preferred_element_type=F32)

    @pl.when(g == pl.num_programs(0) - 1)
    def _():
        write_halves(pos_ref, total[...], outs)


def first_project(scans, pos, panel, steps=3, count=4):
    time_rows, voxels = scans.shape
    rank = panel.shape[1]
    n = voxels // (steps * count)
    half = jax.ShapeDtypeStruct((time_rows // 2, rank), F32)

    def column(u):
        return lambda g, pos: (0, g * count + u)

    return pl.pallas_call(
        functools.partial(first_kernel, count),
        out_shape=[half, half],
        grid_spec=pltpu.PrefetchScalarGridSpec(
            num_scalar_prefetch=1,
            grid=(steps,),
            in_specs=[pl.BlockSpec((count * n, rank), lambda g, pos: (g, 0))]
            + [pl.BlockSpec((time_rows, n), column(u)) for u in range(count)],
            out_specs=[pl.BlockSpec(half.shape, lambda g, pos: (0, 0))] * 2,
            scratch_shapes=[pltpu.VMEM((time_rows, rank), F32)],
        ),
        compiler_params=params(VMEM_FIRST),
        cost_estimate=LIGHT,
    )(pos, panel, *([scans] * count))


def project_kernel(has_base, split, items, pos_ref, *refs):
    refs = list(refs)
    base = refs.pop(0) if has_base else None
    outs = [refs.pop() for _ in range(2 if split else 1)][::-1]
    scans, pieces = refs[: len(items)], refs[len(items) :]
    time_rows = scans[0].shape[0]
    rank = outs[0].shape[1]
    total = jnp.zeros((time_rows, rank), F32)
    for scan, (source, index) in zip(scans, items):
        piece = pieces[source][...] if index is None else pieces[source][index]
        total += jnp.dot(scan[...], piece, preferred_element_type=F32)
    if has_base:
        total += base[...]
    if split:
        write_halves(pos_ref, total, outs)
    else:
        outs[0][...] = total


def project(scans, layout, pos, groups, base=None, split=False):
    time_rows = scans.shape[0]
    rank = groups[0][2].shape[-1]
    items, names = [], []
    for source, (j, ks, array) in enumerate(groups):
        for i, k in enumerate(ks):
            items.append((source, None if array.ndim == 2 else i))
            names.append((j, k))

    def column(j, k):
        return lambda g, pos: (0, layout.block(j, k, pos))

    full = lambda shape: pl.BlockSpec(shape, lambda g, pos: (0,) * len(shape))
    bases = [] if base is None else [base]
    arrays = [array for _, _, array in groups]
    shape = (time_rows // 2, rank) if split else (time_rows, rank)
    out_shape = [jax.ShapeDtypeStruct(shape, F32)] * (2 if split else 1)
    out = pl.pallas_call(
        functools.partial(project_kernel, base is not None, split, items),
        out_shape=out_shape,
        grid_spec=pltpu.PrefetchScalarGridSpec(
            num_scalar_prefetch=1,
            grid=(1,),
            in_specs=[full(b.shape) for b in bases]
            + [pl.BlockSpec((time_rows, layout.columns(j)), column(j, k)) for j, k in names]
            + [full(p.shape) for p in arrays],
            out_specs=[full(shape)] * len(out_shape),
        ),
        compiler_params=params(),
        cost_estimate=LIGHT,
    )(pos, *bases, *([scans] * len(items)), *arrays)
    return out if split else out[0]


def finish_kernel(layout, items, has_base, pos_ref, inverse_ref, *refs):
    refs, (out, held, sems) = refs[:-3], refs[-3:]
    if has_base:
        refs = refs[1:]
    copies = []
    used = 0
    pos = (pos_ref[0], pos_ref[1])
    for number, (source, index, j, k) in enumerate(items):
        n = layout.columns(j)
        codes = refs[source][...] if index is None else refs[source][index]
        if j is None:
            value = jnp.concatenate([Fixed.decode(codes[side]) for side in range(LOW)])
        else:
            value = Fixed.decode(codes)
        rows = pl.ds(used, n)
        held[rows] = times_transpose(value, inverse_ref[...])
        used += n
        start = pl.multiple_of(layout.block(j, k, pos) * n, n)
        copy = pltpu.make_async_copy(held.at[rows], out.at[pl.ds(start, n)], sems.at[number])
        copy.start()
        copies.append(copy)
    for copy in copies:
        copy.wait()


def finish(layout, pos, groups, inverse, voxels, base=None):
    rank = inverse.shape[0]
    items = []
    for source, (j, ks, array) in enumerate(groups):
        alone = array.ndim == (2 if j is not None else 3)
        for i, k in enumerate(ks):
            items.append((source, None if alone else i, j, k))
    columns = sum(layout.columns(j) for _, _, j, _ in items)
    bases = [] if base is None else [base]
    arrays = [array for _, _, array in groups]
    return pl.pallas_call(
        functools.partial(finish_kernel, layout, items, base is not None),
        out_shape=jax.ShapeDtypeStruct((voxels, rank), F32),
        in_specs=[pl.BlockSpec(memory_space=pltpu.SMEM), WHOLE]
        + [pl.BlockSpec(memory_space=pl.ANY)] * len(bases)
        + [WHOLE] * len(arrays),
        out_specs=pl.BlockSpec(memory_space=pl.ANY),
        scratch_shapes=[
            pltpu.VMEM((columns, rank), F32),
            pltpu.SemaphoreType.DMA((len(items),)),
        ],
        input_output_aliases={2: 0} if bases else {},
        compiler_params=params(),
    )(pos, inverse, *bases, *arrays)


def inverse_factor(gram):
    size = gram.shape[0]
    groups = size // GROUP
    shape = (GROUP, size)
    sub = lax.broadcasted_iota(jnp.int32, shape, 0)
    lane = lax.broadcasted_iota(jnp.int32, shape, 1)
    left = [gram[GROUP * i : GROUP * (i + 1)] for i in range(groups)]
    right = [jnp.where(sub + GROUP * i == lane, 1.0, 0.0).astype(F32) for i in range(groups)]
    for g in range(groups):
        first = g * GROUP
        wide = lambda value: jnp.broadcast_to(value, shape)
        rows = [wide(left[g][t : t + 1]) for t in range(GROUP)]
        inverse_rows = [wide(right[g][t : t + 1]) for t in range(GROUP)]
        block = [
            [wide(left[g][t : t + 1, first + u : first + u + 1]) for u in range(GROUP)]
            for t in range(GROUP)
        ]
        below = range(g + 1, groups)
        columns = {
            i: [wide(left[i][:, first + u : first + u + 1]) for u in range(GROUP)] for i in below
        }
        scaled = []
        for t in range(GROUP):
            pivot = 1.0 / block[t][t]
            scaled.append((rows[t] * pivot, inverse_rows[t] * pivot))
            for u in range(t + 1, GROUP):
                factor = block[t][u] * pivot
                for w in range(u, GROUP):
                    block[u][w] = block[u][w] - factor * block[t][w]
                rows[u] = rows[u] - factor * rows[t]
                inverse_rows[u] = inverse_rows[u] - factor * inverse_rows[t]
                for i in below:
                    columns[i][u] = columns[i][u] - factor * columns[i][t]
        for i in below:
            for t in range(GROUP):
                left[i] = left[i] - columns[i][t] * scaled[t][0]
                right[i] = right[i] - columns[i][t] * scaled[t][1]
        for t in range(GROUP):
            left[g] = jnp.where(sub == t, rows[t], left[g])
            right[g] = jnp.where(sub == t, inverse_rows[t], right[g])
    out = []
    for g in range(groups):
        pivots = jnp.sum(
            jnp.where(sub + GROUP * g == lane, left[g], 0.0), axis=1, keepdims=True
        )
        out.append(right[g] * lax.rsqrt(pivots))
    return jnp.concatenate(out)


def times_transpose(value, inverse):
    return lax.dot_general(
        value, inverse, (((1,), (1,)), ((), ())), precision=HIGHEST, preferred_element_type=F32
    )


def scores_kernel(with_factor, lengths_ref, subjects_ref, pos_ref, mine_ref, other_ref, *refs):
    out_ref = refs[-1]
    length = lengths_ref[subjects_ref[pos_ref[1] * LOW + pos_ref[0]]]
    mine, other = mine_ref[...], other_ref[...]
    lower = pos_ref[2] == 0
    scores = jnp.concatenate([jnp.where(lower, mine, other), jnp.where(lower, other, mine)])
    if with_factor:
        scores = times_transpose(scores, refs[0][...])
    live = lax.broadcasted_iota(jnp.int32, scores.shape, 0) < length
    out_ref[...] = jnp.where(live, scores, 0.0).astype(BF16)


def invert_kernel(all_voxels, *refs):
    terms = [ref[...] for ref in refs[:-1]]
    while len(terms) > 1:
        terms = [terms[i] + terms[i + 1] for i in range(0, len(terms), 2)]
    refs[-1][...] = inverse_factor(terms[0] * (1.0 / all_voxels))


def make(mesh):
    subjects, blocks = mesh.shape["subj"], mesh.shape["vox"]
    swap = functools.partial(exchange, axis="subj", size=subjects)
    swap_vox = functools.partial(exchange, axis="vox", size=blocks)

    def on_device(scans, test_matrix, lengths, block_subject):
        time_rows, voxels = scans.shape
        rank = test_matrix.shape[1]
        all_voxels = voxels * blocks
        layout = Layout(voxels, subjects)
        high = layout.high
        ks = list(range(high))
        near, far = ks[: high // 2], ks[high // 2 :]
        me = lax.axis_index("subj")
        core = lax.axis_index("vox") % 2
        pos = jnp.stack([me % LOW, me // LOW, core]).astype(jnp.int32)

        def sketch_sum(scores, code):
            def part(after, j, ks, apart, per_step):
                ordered = scores if after is None else lax.optimization_barrier((scores, after))[0]
                return sketch_part(
                    scans, layout, pos, ordered, j, ks, code, apart, per_step
                )

            away = part(None, 1, ks, False, high // 2)
            got_away = swap(away, mask=1)
            second = part(away, None, ks[1:], True, high - 1)
            got_second = [swap(second[k - 1], mask=k * LOW) for k in ks[1:]]
            home = part(second[0], 0, ks, False, high // 2)
            (second_own,) = part(second[0], None, ks[:1], True, 1)
            got_away, got_second, home, second_own = lax.optimization_barrier(
                (got_away, got_second, home, second_own)
            )
            piece = jax.ShapeDtypeStruct((layout.single + code.pad, rank), code.dtype)
            first = small_call(
                functools.partial(add_pieces_kernel, code, high), [piece] * high, home, got_away
            )
            got_first = [swap(first[k], mask=k * LOW) for k in ks[1:]]

            half = jax.ShapeDtypeStruct((layout.pair // 2 + code.pad, rank), code.dtype)
            keep, send = pl.pallas_call(
                functools.partial(add_halves_kernel, code),
                out_shape=[half, half],
                in_specs=[pl.BlockSpec(memory_space=pltpu.SMEM)] + [WHOLE] * high,
                out_specs=[WHOLE, WHOLE],
                compiler_params=params(),
            )(pos, second_own, *got_second)
            got_send = swap(send, mask=1)
            return (
                add_all(code, [first[0], *got_first]),
                add_all(code, [keep, got_send]),
            )

        def gather(first, second, gram):
            far_in = [swap(first, mask=k * LOW) for k in far]
            near_in = [first] + [swap(first, mask=k * LOW) for k in near[1:]]
            got = swap(second, mask=1)
            lower = pos[0] == 0
            pair = jnp.stack([jnp.where(lower, second, got), jnp.where(lower, got, second)])
            mask = 1
            while mask < blocks:
                gram = gram + swap_vox(gram, mask=mask)
                mask *= 2
            near_in, gram = lax.optimization_barrier((near_in, gram))
            low_near = swap(jnp.stack(near_in), mask=1)
            gram = gram + swap(gram, mask=1)
            far_in, pair, gram = lax.optimization_barrier((far_in, pair, gram))
            low_far = swap(jnp.stack(far_in), mask=1)
            seconds = [pair] + [swap(pair, mask=k * LOW) for k in ks[1:]]
            gram = [gram] + [swap(gram, mask=k * LOW) for k in ks[1:]]
            early = [(0, [k], array) for k, array in zip(near + far, near_in + far_in)]
            late = [(1, near, low_near), (1, far, low_far)]
            pairs = [(None, [k], array) for k, array in zip(ks, seconds)]
            return early, late, pairs, gram

        def sum_scores(mine, send, *factor):
            mine = mine + swap_vox(send, mask=1)
            mask = 2
            while mask < blocks:
                mine = mine + swap_vox(mine, mask=mask)
                mask *= 2
            other = swap_vox(mine, mask=1)
            return pl.pallas_call(
                functools.partial(scores_kernel, bool(factor)),
                out_shape=jax.ShapeDtypeStruct((time_rows, rank), BF16),
                in_specs=[pl.BlockSpec(memory_space=pltpu.SMEM)] * 3
                + [WHOLE] * (2 + len(factor)),
                out_specs=WHOLE,
                compiler_params=params(),
                cost_estimate=LIGHT,
            )(lengths, block_subject, pos, mine, other, *factor)

        def pass_over(scores, code):
            (first, gram_first), (second, gram_second) = sketch_sum(scores, code)
            early, late, pairs, grams = gather(first, second, gram_first + gram_second)
            inverse = small_call(
                functools.partial(invert_kernel, all_voxels),
                jax.ShapeDtypeStruct((rank, rank), F32), *grams,
            )
            return early, late, pairs, inverse

        scores = sum_scores(*first_project(scans, pos, test_matrix))
        early, late, pairs, inverse = pass_over(scores, Plain)
        pairs = [(j, k, array.reshape(layout.pair, rank)) for j, k, array in pairs]
        total = project(scans, layout, pos, early)
        total = project(scans, layout, pos, late, total)
        total, inverse = lax.optimization_barrier((total, inverse))
        halves = project(scans, layout, pos, pairs, total, True)
        scores = sum_scores(*halves, inverse)
        early, late, pairs, inverse = pass_over(scores, Fixed)
        out = finish(layout, pos, early + late, inverse, voxels)
        return finish(layout, pos, pairs, inverse, voxels, out)

    return on_device


def solution(mesh):
    placed = (P("subj", "vox"), P("vox", None), P(), P())
    return jax.shard_map(
        make(mesh), mesh=mesh, in_specs=placed, out_specs=P("vox", None), check_vma=False
    )
```
